256 devices in a mesh: region: 8 (over z), cell: 32 (over x, y, core).
Axes of the slice: x: 4, y: 4, z: 8, core: 2. Of those that a mesh axis runs over, the one named last changes fastest.
Arguments:
- positions: float32 [3, 1024, 512], P(None, ('region', 'cell')), may hold values from 0 to 1
- velocities: float32 [3, 1024, 512], P(None, ('region', 'cell')), may hold values from -6 to 6
- mass: float32 [1024, 512], P(('region', 'cell')), may hold values from 0.0002 to 0.001
- smoothing: float32 [1024, 512], P(('region', 'cell')), may hold values from 0.25 to 0.5
- energy: float32 [1024, 512], P(('region', 'cell')), may hold values from 0.5 to 2
- counts: int32 [1024], P(('region', 'cell')), may hold values from 128 to 512
- send_cells: int32 [8, 32, 32, 1], P('region', 'cell'), may hold values from -1 to 3, as said below
- local_pairs: int32 [8, 32, 4, 2], P('region', 'cell'), may hold values from 0 to 3, as said below
- edge_cells: int32 [8, 32, 2], P('region', 'cell'), may hold values from 0 to 3
Outputs:
- density: float32 [1024, 512], P(('region', 'cell'))
- accel: float32 [3, 1024, 512], P(None, ('region', 'cell'))
- energy_rate: float32 [1024, 512], P(('region', 'cell'))
The draws below stay inside these ranges and needn't reach their ends.
Inputs may be any that keep to these rules, and one draw needn't show every extreme that they name: send_cells[r, c, c2, s] is a local cell index of device (r, c), or -1 for an empty slot; slot s is empty from c to c2 exactly when it is empty from c2 to c, and always empty for c2 = c. `local_pairs`: each row holds two different local cell indices of the device.
All inputs are finite; a program needn't handle non-finite values.
Results may differ from the reference program's by a relative error of at most 0.0003.
Values sent between devices are 32-bit elements; how exact they have to be, the bound alone decides.
A program may use at most 64 MiB of HBM per device.

```python
import math
import jax
import jax.numpy as jnp
from jax import lax

P_SIZE = 512
C_DEV = 4
SLOT = 1
EB = 1
CELLS = 1024
N_REGION = 8
N_CELL = 32
DEVICES = 256


def draw_send_cells(key, part):
    key = jax.random.fold_in(key, 11)
    key_live, key_pick = jax.random.split(key)
    shape = (N_REGION, N_CELL, N_CELL, SLOT)
    chance = jax.random.randint(key_live, shape, 0, 10)
    row_ids = jnp.arange(N_CELL)[:, None, None]
    col_ids = jnp.arange(N_CELL)[None, :, None]
    mirrored = jnp.where(row_ids < col_ids, chance, jnp.swapaxes(chance, 1, 2))
    alive = (mirrored < 6) & (row_ids != col_ids)
    picked = jax.random.randint(key_pick, shape, 0, C_DEV)
    return jnp.where(alive, picked, -1).astype(jnp.int32)


def draw_local_pairs(key, part):
    key = jax.random.fold_in(key, 12)
    key_first, key_step = jax.random.split(key)
    shape = (N_REGION, N_CELL, C_DEV)
    first = jax.random.randint(key_first, shape, 0, C_DEV)
    second = (first + jax.random.randint(key_step, shape, 1, C_DEV)) % C_DEV
    return jnp.stack([first, second], axis=-1).astype(jnp.int32)


def with_ends(entries, key, smallest, top_value):
    place = [jax.random.randint(jax.random.fold_in(key, axis), (), 0, length) for axis, length in enumerate(entries.shape)]
    longest = entries.shape.index(max(entries.shape))
    next_to = place[:longest] + [(place[longest] + 1) % entries.shape[longest]] + place[longest + 1:]
    return entries.at[tuple(place)].set(smallest).at[tuple(next_to)].set(top_value)


def shard_levels(stream_key, extent, cuts, smallest, largest):
    factor_of = 1.0
    for axis_at, parts in cuts:
        heights = jax.random.uniform(jax.random.fold_in(jax.random.fold_in(stream_key, 6), axis_at), (parts,), jnp.float32, smallest / len(cuts), largest / len(cuts))
        factor_of = factor_of * jnp.repeat(jnp.exp(heights), extent[axis_at] // parts).reshape((-1,) + (1,) * (len(extent) - 1 - axis_at))
    return factor_of


def gaussian(stream_key, dims, spread, bound, cuts=(), kind=jnp.bfloat16):
    gain = shard_levels(stream_key, dims, cuts, -0.22, 0.18) if cuts else 1.0
    array = jax.random.normal(stream_key, dims, jnp.float32) * spread * gain
    return jnp.minimum(jnp.maximum(array, -bound), bound).astype(kind)


def setup_inputs(seed: int = 0) -> dict:
    splits = jax.random.split(jax.random.key(seed), 10)
    return {
        "positions": jnp.clip(1.0 * jax.random.uniform(splits[0], (3, CELLS, P_SIZE), jnp.float32) ** shard_levels(splits[0], (3, CELLS, P_SIZE), ((1, 256),), -0.2, 0.2), 0.0, 1.0),
        "velocities": gaussian(splits[1], (3, CELLS, P_SIZE), 1.0, 6.0, ((1, 256),), jnp.float32),
        "mass": jnp.clip(jnp.exp(math.log(0.001) - 1.609438 * jax.random.uniform(splits[2], (CELLS, P_SIZE), jnp.float32) ** shard_levels(splits[2], (CELLS, P_SIZE), ((0, 256),), -0.2, 0.2)), 0.0002, 0.001),
        "smoothing": jnp.clip(jnp.exp(math.log(0.5) - 0.6931472 * jax.random.uniform(splits[3], (CELLS, P_SIZE), jnp.float32) ** shard_levels(splits[3], (CELLS, P_SIZE), ((0, 256),), -0.2, 0.2)), 0.25, 0.5),
        "energy": jnp.clip(jnp.exp(math.log(2.0) - 1.3862944 * jax.random.uniform(splits[4], (CELLS, P_SIZE), jnp.float32) ** shard_levels(splits[4], (CELLS, P_SIZE), ((0, 256),), -0.2, 0.2)), 0.5, 2.0),
        "counts": with_ends(jax.random.randint(splits[5], (CELLS,), P_SIZE // 4, P_SIZE + 1), jax.random.fold_in(splits[5], 1), P_SIZE // 4, P_SIZE).astype(jnp.int32),
        "send_cells": draw_send_cells(jax.random.fold_in(splits[9], 71), 0),
        "local_pairs": draw_local_pairs(jax.random.fold_in(splits[9], 71), 0),
        "edge_cells": with_ends(jax.random.randint(splits[8], (N_REGION, N_CELL, 2 * EB), 0, C_DEV), jax.random.fold_in(splits[8], 1), 0, C_DEV - 1).astype(jnp.int32),
    }


GAMMA = 5.0 / 3.0

def spline(distance, support_raw):
    support = jnp.where(support_raw > 0.0, support_raw, 1.0)
    scaled = distance / support
    norm_factor = 8.0 / (math.pi * support * support * support)
    inside = scaled < 0.5
    within = scaled < 1.0
    profile = jnp.where(inside, 1.0 - 6.0 * scaled * scaled + 6.0 * scaled * scaled * scaled, jnp.where(within, 2.0 * (1.0 - scaled) ** 3, 0.0))
    slope_term = jnp.where(inside, -12.0 + 18.0 * scaled, jnp.where(within, -6.0 * (1.0 - scaled) ** 2 / jnp.maximum(scaled, 0.5), 0.0))
    return (norm_factor * profile, norm_factor * slope_term / (support * support))

def separation(target, source):
    apart_x = target[0][:, None] - source[0][None, :]
    apart_y = target[1][:, None] - source[1][None, :]
    apart_z = target[2][:, None] - source[2][None, :]
    distance = jnp.sqrt(apart_x * apart_x + apart_y * apart_y + apart_z * apart_z)
    return (apart_x, apart_y, apart_z, distance)

def density_tile(target, source):
    apart_x, apart_y, apart_z, distance = separation(target, source)
    kernel_value, _ = spline(distance, target[7][:, None])
    return lax.optimization_barrier(jnp.sum(kernel_value * source[6][None, :], axis=1))

def force_tile(target, source):
    apart_x, apart_y, apart_z, distance = separation(target, source)
    _, own_slope = spline(distance, target[7][:, None])
    _, other_slope = spline(distance, source[7][None, :])
    weighted = source[6][None, :] * 0.5 * (own_slope + other_slope)
    coupled = weighted * (target[8][:, None] + source[8][None, :])
    accel_x = -lax.optimization_barrier(jnp.sum(coupled * apart_x, axis=1))
    accel_y = -lax.optimization_barrier(jnp.sum(coupled * apart_y, axis=1))
    accel_z = -lax.optimization_barrier(jnp.sum(coupled * apart_z, axis=1))
    closing = (target[3][:, None] - source[3][None, :]) * apart_x + (target[4][:, None] - source[4][None, :]) * apart_y + (target[5][:, None] - source[5][None, :]) * apart_z
    heating = target[8] * lax.optimization_barrier(jnp.sum(weighted * closing, axis=1))
    return jnp.stack([accel_x, accel_y, accel_z, heating])

def run_tiles(worker, targets, sources):
    total = targets.shape[0]
    block_count = total // 4
    target_blocks = targets.reshape((block_count, 4) + targets.shape[1:])
    source_blocks = sources.reshape((block_count, 4) + sources.shape[1:])
    results = lax.map(lambda block_pair: jax.vmap(worker)(block_pair[0], block_pair[1]), (target_blocks, source_blocks))
    return results.reshape((total,) + results.shape[2:])

def tile_index(cell_pairs, send_list, edge_list, cell_count, peer_count):
    own_cells = jnp.arange(cell_count, dtype=jnp.int32)
    picked = jnp.clip(send_list, 0, cell_count - 1).reshape(-1).astype(jnp.int32)
    edge_base = cell_count + peer_count * SLOT
    edge_slots = jnp.arange(EB, dtype=jnp.int32)
    target_ids = jnp.concatenate([own_cells, cell_pairs[:, 0], cell_pairs[:, 1], picked, jnp.repeat(edge_list[:EB], EB), jnp.repeat(edge_list[EB:], EB)])
    source_ids = jnp.concatenate([own_cells, cell_pairs[:, 1], cell_pairs[:, 0], cell_count + jnp.arange(peer_count * SLOT, dtype=jnp.int32), edge_base + jnp.tile(edge_slots, EB), edge_base + EB + jnp.tile(edge_slots, EB)])
    used = 3 * cell_count + peer_count * SLOT + 2 * EB * EB
    padding = -used % 4
    weights = jnp.concatenate([jnp.ones((used,), jnp.float32), jnp.zeros((padding,), jnp.float32)])
    target_ids = jnp.concatenate([target_ids, jnp.zeros((padding,), jnp.int32)]).astype(jnp.int32)
    source_ids = jnp.concatenate([source_ids, jnp.zeros((padding,), jnp.int32)]).astype(jnp.int32)
    return (target_ids, source_ids, weights)

def reference(positions, velocities, mass, smoothing, energy, counts, send_cells, local_pairs, edge_cells):
    slot_ids = lax.broadcasted_iota(jnp.int32, (CELLS, P_SIZE), 1)
    occupied = (slot_ids < counts[:, None]).astype(jnp.float32)
    state_rows = jnp.concatenate([jnp.transpose(positions, (1, 0, 2)), jnp.transpose(velocities, (1, 0, 2)), (mass * occupied)[:, None], smoothing[:, None]], axis=1)
    device_ids = jnp.arange(DEVICES, dtype=jnp.int32)

    def device_table(rows_all, device):
        region_id = device // N_CELL
        cell_id = device % N_CELL
        own_rows = lax.dynamic_slice_in_dim(rows_all, (device * C_DEV).astype(jnp.int32), C_DEV, 0)
        mine = send_cells[region_id, cell_id]
        theirs = send_cells[region_id, :, cell_id, :]
        alive = (mine >= 0).astype(jnp.float32).reshape(-1)
        peer_cells = ((region_id * N_CELL + jnp.arange(N_CELL, dtype=jnp.int32))[:, None] * C_DEV + jnp.clip(theirs, 0, C_DEV - 1)).reshape(-1).astype(jnp.int32)
        received = rows_all[peer_cells] * alive[:, None, None]
        lower = jnp.maximum(region_id - 1, 0)
        upper = jnp.minimum(region_id + 1, N_REGION - 1)
        lower_ids = ((lower * N_CELL + cell_id) * C_DEV + edge_cells[lower, cell_id, EB:]).astype(jnp.int32)
        upper_ids = ((upper * N_CELL + cell_id) * C_DEV + edge_cells[upper, cell_id, :EB]).astype(jnp.int32)
        lower_ok = (region_id > 0).astype(jnp.float32)
        upper_ok = (region_id < N_REGION - 1).astype(jnp.float32)
        outside = jnp.concatenate([rows_all[lower_ids] * lower_ok, rows_all[upper_ids] * upper_ok])
        table = jnp.concatenate([own_rows, received, outside])
        target_ids, source_ids, weights = tile_index(local_pairs[region_id, cell_id], mine, edge_cells[region_id, cell_id], C_DEV, N_CELL)
        assign = (target_ids[:, None] == jnp.arange(C_DEV, dtype=jnp.int32)[None, :]).astype(jnp.float32) * weights[:, None]
        return (own_rows[target_ids], table[source_ids], assign)

    def density_device(device):
        targets, sources, assign = device_table(state_rows, device)
        terms = run_tiles(density_tile, targets, sources)
        return jnp.dot(assign.T, terms, precision=lax.Precision.HIGHEST)
    rho = lax.map(density_device, device_ids).reshape(CELLS, P_SIZE)
    pressure_term = occupied * (GAMMA - 1.0) * energy / (rho + 1.0 - occupied)
    force_rows = jnp.concatenate([state_rows, pressure_term[:, None]], axis=1)

    def force_device(device):
        targets, sources, assign = device_table(force_rows, device)
        terms = run_tiles(force_tile, targets, sources)
        return jnp.einsum('tc,tkp->kcp', assign, terms, precision=lax.Precision.HIGHEST)
    forces = lax.map(force_device, device_ids)
    forces = jnp.transpose(forces, (1, 0, 2, 3)).reshape(4, CELLS, P_SIZE)
    return (rho * occupied, forces[:3] * occupied[None], forces[3] * occupied)
```

```python
import math
import jax
import jax.numpy as jnp
from jax import lax
from jax.experimental import pallas as pl
from jax.experimental.pallas import tpu as pltpu
from jax.sharding import PartitionSpec as P

GAMMA = 5.0 / 3.0
F32, BF16 = jnp.float32, jnp.bfloat16
U = 3
NSLOT = 38
OWN = 34
MAXT = 46
GBLK = MAXT * 16 + 20 + 6 * U
ROOT = math.sqrt(24.0 / math.pi)


def halves(v):
    hi = v.astype(BF16).astype(F32)
    return hi, v - hi


def thirds(v):
    first, rest = halves(v)
    second, third = halves(rest)
    return first, second, third


def nt(a, b):
    return lax.dot_general(a, b, (((1,), (1,)), ((), ())), preferred_element_type=F32)


def nn(a, b):
    return lax.dot_general(a, b, (((1,), (0,)), ((), ())), preferred_element_type=F32)


def compute_kernel(n_ref, send_ref, pair_ref, edge_ref, table, energy, rho_out, acc_out, er_out, t_out,
                   ta, ts, feat_s, rows_s, lane_s, feat_o, s_o, near_a, near_b, gst, acc_g, acc_w, q_rows):
    row = lax.broadcasted_iota(jnp.int32, (8, 512), 0)

    def blocks(s):
        return (n_ref[s] + 127) >> 7

    def add(count, a, s):
        ta[count] = a
        ts[count] = s
        return count + (n_ref[s] > 0).astype(jnp.int32)
    for k in range(4):
        ta[k] = k
        ts[k] = OWN + k
    for k in range(4):
        a, b = pair_ref[2 * k], pair_ref[2 * k + 1]
        ta[4 + 2 * k] = a
        ts[4 + 2 * k] = OWN + b
        ta[5 + 2 * k] = b
        ts[5 + 2 * k] = OWN + a
    count = lax.fori_loop(0, 32, lambda s, cnt: add(cnt, jnp.maximum(send_ref[s], 0), s), jnp.int32(12))
    count = add(count, edge_ref[0], jnp.int32(32))
    count = add(count, edge_ref[1], jnp.int32(33))
    ta[count] = 0
    ts[count] = OWN
    total = lax.fori_loop(0, count, lambda k, v: v + blocks(OWN + ta[k]) * blocks(ts[k]), jnp.int32(0))

    def source(s):
        st = table[s]
        x = st[1:2]
        y = st[2:3]
        z = st[3:4]
        sq = x * x + y * y + z * z
        hinv = 1.0 / st[7:8]
        sj = ROOT * hinv * hinv
        tj = sj * hinv
        f = jnp.where(row == 0, sq, jnp.where(row <= 3, st, jnp.where(row == 4, 1.0, jnp.where(row == 5, tj, 0.0))))
        f1, f2, f3 = thirds(f)
        feats = jnp.concatenate([f1, f1, f2, f2, f1, f3], axis=0)
        five = lax.broadcasted_iota(jnp.int32, (48, 512), 0) % 8 == 5
        near = jnp.where(five, 0.0, feats).astype(BF16)
        ratio = jnp.where(five, feats, 0.0).astype(BF16)
        vx = x * st[4:5] + y * st[5:6] + z * st[6:7]
        r = jnp.where(row == 0, 1.0, jnp.where(row == 7, vx, st)) * st[0:1]
        r1, r2 = halves(r)
        rows = jnp.concatenate([r1, r2], axis=0).astype(BF16)
        lane = jnp.where(row == 0, sj, st[0:1])
        for jb in range(4):
            cut = slice(jb * 128, (jb + 1) * 128)
            feat_s[s * 4 + jb, :, 0:128] = near[:, cut]
            feat_s[s * 4 + jb, :, 128:256] = ratio[:, cut]
            rows_s[s * 4 + jb, :, 0:128] = rows[:, cut]
            rows_s[s * 4 + jb, :, 128:256] = rows[:, cut]
            lane_s[s * 4 + jb] = lane[:, cut]

    def source_loop(g, _):
        source(2 * g)
        source(2 * g + 1)
        return 0
    lax.fori_loop(0, NSLOT // 2, source_loop, 0)

    eye = (lax.broadcasted_iota(jnp.int32, (128, 128), 0) == lax.broadcasted_iota(jnp.int32, (128, 128), 1))
    eye = eye.astype(F32).astype(BF16)
    pick = (lax.broadcasted_iota(jnp.int32, (64, 128), 0) >= 48).astype(F32).astype(BF16)
    for a in range(4):
        st = table[OWN + a]
        x = st[1:2]
        y = st[2:3]
        z = st[3:4]
        sq = x * x + y * y + z * z
        h = st[7:8]
        hinv = 1.0 / h
        si = ROOT * hinv * hinv
        tt = si * si * hinv * hinv
        f = jnp.where(row == 0, 1.0, jnp.where(row <= 3, -2.0 * st, jnp.where(row == 4, sq, 0.0)))
        f = jnp.where(row == 5, h * h * h * (1.0 / ROOT), f * tt)
        f1, f2, f3 = thirds(f)
        s1, s2, s3 = thirds(si)
        s_rows = jnp.where(row == 0, s1, jnp.where(row == 1, s2, jnp.where(row == 2, s3, 0.0)))
        whole = jnp.concatenate([f1, f2, f1, f2, f3, f1, s_rows, jnp.zeros((8, 512), F32)], axis=0).astype(BF16)
        for ib in range(4):
            part = nt(eye, whole[:, ib * 128:(ib + 1) * 128]).astype(BF16)
            feat_o[a * 4 + ib] = part[:, :48]
            s_o[a * 4 + ib] = nn(part, pick)

    acc_g[...] = jnp.zeros_like(acc_g)
    acc_w[...] = jnp.zeros_like(acc_w)
    for u in range(U):
        gst[u] = jnp.zeros((128, 256), BF16)

    def at(tile):
        a, s = ta[tile], ts[tile]
        return a, s, blocks(OWN + a), blocks(s)

    def advance(state):
        tile, ib, jb, a, s, ni, nj = state
        ib = ib + 1
        wrap_i = ib >= ni
        ib = jnp.where(wrap_i, 0, ib)
        jb = jnp.where(wrap_i, jb + 1, jb)
        wrap_j = jb >= nj
        jb = jnp.where(wrap_j, 0, jb)
        tile = jnp.where(wrap_j, jnp.minimum(tile + 1, count), tile)
        return (tile, ib, jb) + at(tile)

    def group(state):
        out = []
        for _ in range(U):
            out.append((state[3] * 4 + state[1], state[4] * 4 + state[2]))
            state = advance(state)
        return state, tuple(out)

    def distances(buf, where):
        for u in range(U):
            buf[u] = nn(feat_o[where[u][0]], feat_s[where[u][1]])

    def elements(buf, where, base):
        for u in range(U):
            oi, sj_ = where[u]
            live = (base + u < total).astype(F32)
            sj = lane_s[sj_][0:1]
            mass = lane_s[sj_][1:2] * live
            d2 = jnp.maximum(buf[u, :, 0:128], 1e-6)
            inv = lax.rsqrt(d2)
            pi = d2 * inv
            pj = pi * buf[u, :, 128:256]
            ai = jnp.maximum(s_o[oi] - pi, 0.0)
            ci = jnp.maximum(ai - pi, 0.0)
            qa = ai * ai
            qc = ci * ci
            acc_w[oi] += ((ai + ai) * qa - qc * ci) * mass
            aj = jnp.maximum(sj - pj, 0.0)
            mj = jnp.minimum(pj, aj)
            g = (qa - qc + mj * (aj + aj - mj)) * inv
            hi = g.astype(BF16)
            gst[base + U + u, :, 0:128] = hi
            gst[base + U + u, :, 128:256] = (g - hi.astype(F32)).astype(BF16)

    def products(where, base):
        return [nt(rows_s[where[u][1]], gst[base + U + u]) for u in range(U)]

    def collect(sums, where, base):
        for u in range(U):
            acc_g[where[u][0]] += jnp.where(base + u < total, sums[u], 0.0)

    zero = jnp.int32(0)
    walk, first = group((zero, zero, zero) + at(zero))
    walk, second = group(walk)
    distances(near_a, first)

    def body(n, carry):
        walk, prev, now, later = carry
        base = n * (2 * U)
        sums = products(prev, base - U)
        elements(near_a, now, base)
        distances(near_b, later)
        collect(sums, prev, base - U)
        walk, after = group(walk)
        sums = products(now, base)
        elements(near_b, later, base + U)
        distances(near_a, after)
        collect(sums, now, base)
        walk, last = group(walk)
        return walk, later, after, last

    steps = (total + 2 * U - 1) // (2 * U)
    lax.fori_loop(0, steps + 1, body, (walk, first, first, second))

    def clear(k, _):
        gst[(2 * steps + 3) * U + k] = jnp.zeros((128, 256), BF16)
        return 0
    lax.fori_loop(0, 17, clear, 0)

    lane_id = lax.broadcasted_iota(jnp.int32, (1, 512), 1)
    for a in range(4):
        st = table[OWN + a]
        h = st[7:8]
        h3 = h * h * h
        ti = ROOT / h3
        sums = jnp.concatenate([acc_g[a * 4 + ib] for ib in range(4)], axis=1)
        sums = (sums[:8] + sums[8:]) * ti
        wsum = jnp.concatenate([jnp.sum(acc_w[a * 4 + ib].T, axis=0, keepdims=True) for ib in range(4)], axis=1)
        rho = wsum * (h3 * (8.0 / math.pi / ROOT ** 3))
        live = lane_id < n_ref[OWN + a]
        press = jnp.where(live, (GAMMA - 1.0) * energy[a:a + 1] / jnp.where(live, rho, 1.0), 0.0)
        rho_out[a:a + 1] = jnp.where(live, rho, 0.0)
        dx = [st[1 + k:2 + k] * sums[0:1] - sums[1 + k:2 + k] for k in range(3)]
        heat = sums[7:8]
        for k in range(3):
            heat = heat + st[4 + k:5 + k] * dx[k] - st[1 + k:2 + k] * sums[4 + k:5 + k]
            acc_out[k, a:a + 1] = jnp.where(live, press * dx[k], 0.0)
        er_out[a:a + 1] = jnp.where(live, -press * heat, 0.0)
        q = jnp.where(row == 0, 1.0, jnp.where(row <= 3, st, 0.0)) * (st[0:1] * press * ti)
        q1, q2 = halves(q)
        q_rows[a] = jnp.concatenate([q1, q2], axis=0).astype(BF16)

    t_out[...] = jnp.zeros_like(t_out)

    def mirror(tile, base):
        a, s, ni, nj = at(tile)
        q = q_rows[a]
        st = table[s]
        for jb in range(4):
            first = base + jb * ni
            g = gst[pl.ds(first, 4)].reshape(512, 256)
            o = nn(q, g)
            o = o[:8] + o[8:]
            o = o[:, :128] + o[:, 128:]
            cut = slice(jb * 128, (jb + 1) * 128)
            add_ = st[:, cut] * o[0:1] - o
            t_out[s, :, cut] += add_[0:4]
        return base + ni * nj
    lax.fori_loop(0, count, mirror, jnp.int32(U))

    for a in range(4):
        live = lane_id < n_ref[OWN + a]
        for k in range(3):
            acc_out[k, a:a + 1] += jnp.where(live, t_out[OWN + a, 1 + k:2 + k], 0.0)


def compute(counts, send, pairs, edge, table, energy):
    smem = pl.BlockSpec(memory_space=pltpu.SMEM)
    vmem = pl.BlockSpec(memory_space=pltpu.VMEM)
    return pl.pallas_call(
        compute_kernel,
        out_shape=(
            jax.ShapeDtypeStruct((4, 512), F32),
            jax.ShapeDtypeStruct((3, 4, 512), F32),
            jax.ShapeDtypeStruct((4, 512), F32),
            jax.ShapeDtypeStruct((NSLOT, 4, 512), F32),
        ),
        in_specs=[smem] * 4 + [vmem] * 2,
        out_specs=(vmem,) * 4,
        scratch_shapes=[
            pltpu.SMEM((MAXT + 2,), jnp.int32),
            pltpu.SMEM((MAXT + 2,), jnp.int32),
            pltpu.VMEM((NSLOT * 4, 48, 256), BF16),
            pltpu.VMEM((NSLOT * 4, 16, 256), BF16),
            pltpu.VMEM((NSLOT * 4, 8, 128), F32),
            pltpu.VMEM((16, 128, 48), BF16),
            pltpu.VMEM((16, 128, 128), F32),
            pltpu.VMEM((U, 128, 256), F32),
            pltpu.VMEM((U, 128, 256), F32),
            pltpu.VMEM((GBLK, 128, 256), BF16),
            pltpu.VMEM((16, 16, 128), F32),
            pltpu.VMEM((16, 128, 128), F32),
            pltpu.VMEM((4, 16, 512), BF16),
        ],
        compiler_params=pltpu.CompilerParams(vmem_limit_bytes=63 * 1024 * 1024),
        name="tiles",
    )(counts, send, pairs, edge, table, energy)


def shifted(down, up):
    count = lax.axis_size("region")
    from_lower = lax.ppermute(up, "region", [(i, i + 1) for i in range(count - 1)])
    from_upper = lax.ppermute(down, "region", [(i + 1, i) for i in range(count - 1)])
    return from_lower, from_upper


def on_device(
    positions, velocities, mass, smoothing, energy, counts, send_cells, local_pairs, edge_cells
):
    slot_ids = lax.broadcasted_iota(jnp.int32, (4, 512), 1)
    occupied = slot_ids < counts[:, None]
    rows = jnp.concatenate(
        [
            jnp.where(occupied, mass, 0.0)[:, None],
            jnp.transpose(positions, (1, 0, 2)) - 0.5,
            jnp.transpose(velocities, (1, 0, 2)),
            smoothing[:, None],
        ],
        axis=1,
    )
    send = send_cells[0, 0, :, 0]
    edge = edge_cells[0, 0]
    payload = jnp.where((send >= 0)[:, None, None], rows[jnp.maximum(send, 0)], 0.0)
    received = lax.all_to_all(payload, "cell", split_axis=0, concat_axis=0, tiled=True)
    lower, upper = shifted(rows[edge[0]], rows[edge[1]])
    table = jnp.concatenate([received, lower[None], upper[None], rows], axis=0)
    n = jnp.sum((table[:, 0] > 0.0).astype(jnp.int32), axis=1)
    density, accel, heat, back = compute(n, send, local_pairs[0, 0].reshape(8), edge, table, energy)
    returned = lax.all_to_all(back[:32], "cell", split_axis=0, concat_axis=0, tiled=True)
    lower, upper = shifted(back[32], back[33])
    whole = jnp.concatenate([returned, lower[None], upper[None]], axis=0)
    target = jnp.concatenate([send, edge])
    own = jnp.arange(4, dtype=jnp.int32)
    hit = (target[None, :] == own[:, None]).astype(jnp.float32)
    extra = jnp.sum(hit[:, :, None, None] * whole[None, :, 1:4], axis=1)
    extra = jnp.where(occupied[None], jnp.transpose(extra, (1, 0, 2)), 0.0)
    return density, accel + extra, heat


def solution(mesh):
    placed = (
        P(None, ("region", "cell"), None),
        P(None, ("region", "cell"), None),
        P(("region", "cell"), None),
        P(("region", "cell"), None),
        P(("region", "cell"), None),
        P(("region", "cell")),
        P("region", "cell", None, None),
        P("region", "cell", None, None),
        P("region", "cell", None),
    )
    return jax.shard_map(
        on_device,
        mesh=mesh,
        in_specs=placed,
        out_specs=(
            P(("region", "cell"), None),
            P(None, ("region", "cell"), None),
            P(("region", "cell"), None),
        ),
        check_vma=False,
    )
```

```python
import math
import jax
import jax.numpy as jnp
from jax import lax
from jax.experimental import pallas as pl
from jax.experimental.pallas import tpu as pltpu
from jax.sharding import PartitionSpec as P

GAMMA = 5.0 / 3.0
F32, BF16 = jnp.float32, jnp.bfloat16
U = 3
NSLOT = 38
OWN = 34
MAXT = 46
GBLK = MAXT * 16 + 20 + 6 * U
ROOT = math.sqrt(24.0 / math.pi)


def halves(v):
    hi = v.astype(BF16).astype(F32)
    return hi, v - hi


def thirds(v):
    first, rest = halves(v)
    second, third = halves(rest)
    return first, second, third


def nt(a, b):
    return lax.dot_general(a, b, (((1,), (1,)), ((), ())), preferred_element_type=F32)


def nn(a, b):
    return lax.dot_general(a, b, (((1,), (0,)), ((), ())), preferred_element_type=F32)


def compute_kernel(send_ref, pair_ref, edge_ref, table, energy, rho_out, acc_out, er_out, t_out,
                   ta, ts, feat_s, rows_s, lane_s, feat_o, s_o, near_a, near_b, gst, acc_g, acc_w, q_rows,
                   cnt_v, n_ref, cnt_sem):
    found = jnp.sum((table[:, 0, :] > 0.0).astype(F32), axis=1, keepdims=True)
    cnt_v[...] = jnp.broadcast_to(found, (NSLOT, 128)).astype(jnp.int32)
    fetch = pltpu.make_async_copy(cnt_v, n_ref, cnt_sem)
    fetch.start()
    row = lax.broadcasted_iota(jnp.int32, (8, 512), 0)

    def blocks(s):
        return (n_ref[s, 0] + 127) >> 7

    def source(s):
        st = table[s]
        x = st[1:2]
        y = st[2:3]
        z = st[3:4]
        sq = x * x + y * y + z * z
        hinv = 1.0 / st[7:8]
        sj = ROOT * hinv * hinv
        tj = sj * hinv
        f = jnp.where(row == 0, sq, jnp.where(row <= 3, st, jnp.where(row == 4, 1.0, jnp.where(row == 5, tj, 0.0))))
        f1, f2, f3 = thirds(f)
        feats = jnp.concatenate([f1, f1, f2, f2, f1, f3], axis=0)
        five = lax.broadcasted_iota(jnp.int32, (48, 512), 0) % 8 == 5
        near = jnp.where(five, 0.0, feats).astype(BF16)
        ratio = jnp.where(five, feats, 0.0).astype(BF16)
        vx = x * st[4:5] + y * st[5:6] + z * st[6:7]
        r = jnp.where(row == 0, 1.0, jnp.where(row == 7, vx, st)) * st[0:1]
        r1, r2 = halves(r)
        rows = jnp.concatenate([r1, r2], axis=0).astype(BF16)
        lane = jnp.where(row == 0, sj, st[0:1])
        for jb in range(4):
            cut = slice(jb * 128, (jb + 1) * 128)
            feat_s[s * 4 + jb, :, 0:128] = near[:, cut]
            feat_s[s * 4 + jb, :, 128:256] = ratio[:, cut]
            rows_s[s * 4 + jb, :, 0:128] = rows[:, cut]
            rows_s[s * 4 + jb, :, 128:256] = rows[:, cut]
            lane_s[s * 4 + jb] = lane[:, cut]

    def source_loop(g, _):
        source(2 * g)
        source(2 * g + 1)
        return 0
    lax.fori_loop(0, NSLOT // 2, source_loop, 0)
    fetch.wait()

    def add(count, a, s):
        ta[count] = a
        ts[count] = s
        return count + (n_ref[s, 0] > 0).astype(jnp.int32)
    for k in range(4):
        ta[k] = k
        ts[k] = OWN + k
    for k in range(4):
        a, b = pair_ref[2 * k], pair_ref[2 * k + 1]
        ta[4 + 2 * k] = a
        ts[4 + 2 * k] = OWN + b
        ta[5 + 2 * k] = b
        ts[5 + 2 * k] = OWN + a
    count = lax.fori_loop(0, 32, lambda s, cnt: add(cnt, jnp.maximum(send_ref[s], 0), s), jnp.int32(12))
    count = add(count, edge_ref[0], jnp.int32(32))
    count = add(count, edge_ref[1], jnp.int32(33))
    ta[count] = 0
    ts[count] = OWN
    total = lax.fori_loop(0, count, lambda k, v: v + blocks(OWN + ta[k]) * blocks(ts[k]), jnp.int32(0))


    eye = (lax.broadcasted_iota(jnp.int32, (128, 128), 0) == lax.broadcasted_iota(jnp.int32, (128, 128), 1))
    eye = eye.astype(F32).astype(BF16)
    pick = (lax.broadcasted_iota(jnp.int32, (64, 128), 0) >= 48).astype(F32).astype(BF16)
    for a in range(4):
        st = table[OWN + a]
        x = st[1:2]
        y = st[2:3]
        z = st[3:4]
        sq = x * x + y * y + z * z
        h = st[7:8]
        hinv = 1.0 / h
        si = ROOT * hinv * hinv
        tt = si * si * hinv * hinv
        f = jnp.where(row == 0, 1.0, jnp.where(row <= 3, -2.0 * st, jnp.where(row == 4, sq, 0.0)))
        f = jnp.where(row == 5, h * h * h * (1.0 / ROOT), f * tt)
        f1, f2, f3 = thirds(f)
        s1, s2, s3 = thirds(si)
        s_rows = jnp.where(row == 0, s1, jnp.where(row == 1, s2, jnp.where(row == 2, s3, 0.0)))
        whole = jnp.concatenate([f1, f2, f1, f2, f3, f1, s_rows, jnp.zeros((8, 512), F32)], axis=0).astype(BF16)
        for ib in range(4):
            part = nt(eye, whole[:, ib * 128:(ib + 1) * 128]).astype(BF16)
            feat_o[a * 4 + ib] = part[:, :48]
            s_o[a * 4 + ib] = nn(part, pick)

    acc_g[...] = jnp.zeros_like(acc_g)
    acc_w[...] = jnp.zeros_like(acc_w)
    for u in range(U):
        gst[u] = jnp.zeros((128, 256), BF16)

    def at(tile):
        a, s = ta[tile], ts[tile]
        return a, s, blocks(OWN + a), blocks(s)

    def advance(state):
        tile, ib, jb, a, s, ni, nj = state
        ib = ib + 1
        wrap_i = ib >= ni
        ib = jnp.where(wrap_i, 0, ib)
        jb = jnp.where(wrap_i, jb + 1, jb)
        wrap_j = jb >= nj
        jb = jnp.where(wrap_j, 0, jb)
        tile = jnp.where(wrap_j, jnp.minimum(tile + 1, count), tile)
        return (tile, ib, jb) + at(tile)

    def group(state):
        out = []
        for _ in range(U):
            out.append((state[3] * 4 + state[1], state[4] * 4 + state[2]))
            state = advance(state)
        return state, tuple(out)

    def distances(buf, where):
        for u in range(U):
            buf[u] = nn(feat_o[where[u][0]], feat_s[where[u][1]])

    def elements(buf, where, base):
        for u in range(U):
            oi, sj_ = where[u]
            live = (base + u < total).astype(F32)
            sj = lane_s[sj_][0:1]
            mass = lane_s[sj_][1:2] * live
            d2 = jnp.maximum(buf[u, :, 0:128], 1e-6)
            inv = lax.rsqrt(d2)
            pi = d2 * inv
            pj = pi * buf[u, :, 128:256]
            ai = jnp.maximum(s_o[oi] - pi, 0.0)
            ci = jnp.maximum(ai - pi, 0.0)
            qa = ai * ai
            qc = ci * ci
            acc_w[oi] += ((ai + ai) * qa - qc * ci) * mass
            aj = jnp.maximum(sj - pj, 0.0)
            mj = jnp.minimum(pj, aj)
            g = (qa - qc + mj * (aj + aj - mj)) * inv
            hi = g.astype(BF16)
            gst[base + U + u, :, 0:128] = hi
            gst[base + U + u, :, 128:256] = (g - hi.astype(F32)).astype(BF16)

    def products(where, base):
        return [nt(rows_s[where[u][1]], gst[base + U + u]) for u in range(U)]

    def collect(sums, where, base):
        for u in range(U):
            acc_g[where[u][0]] += jnp.where(base + u < total, sums[u], 0.0)

    zero = jnp.int32(0)
    walk, first = group((zero, zero, zero) + at(zero))
    walk, second = group(walk)
    distances(near_a, first)

    def body(n, carry):
        walk, prev, now, later = carry
        base = n * (2 * U)
        sums = products(prev, base - U)
        elements(near_a, now, base)
        distances(near_b, later)
        collect(sums, prev, base - U)
        walk, after = group(walk)
        sums = products(now, base)
        elements(near_b, later, base + U)
        distances(near_a, after)
        collect(sums, now, base)
        walk, last = group(walk)
        return walk, later, after, last

    steps = (total + 2 * U - 1) // (2 * U)
    lax.fori_loop(0, steps + 1, body, (walk, first, first, second))

    def clear(k, _):
        gst[(2 * steps + 3) * U + k] = jnp.zeros((128, 256), BF16)
        return 0
    lax.fori_loop(0, 17, clear, 0)

    lane_id = lax.broadcasted_iota(jnp.int32, (1, 512), 1)
    for a in range(4):
        st = table[OWN + a]
        h = st[7:8]
        h3 = h * h * h
        ti = ROOT / h3
        sums = jnp.concatenate([acc_g[a * 4 + ib] for ib in range(4)], axis=1)
        sums = (sums[:8] + sums[8:]) * ti
        wsum = jnp.concatenate([jnp.sum(acc_w[a * 4 + ib].T, axis=0, keepdims=True) for ib in range(4)], axis=1)
        rho = wsum * (h3 * (8.0 / math.pi / ROOT ** 3))
        live = lane_id < n_ref[OWN + a, 0]
        press = jnp.where(live, (GAMMA - 1.0) * energy[a:a + 1] / jnp.where(live, rho, 1.0), 0.0)
        rho_out[a:a + 1] = jnp.where(live, rho, 0.0)
        dx = [st[1 + k:2 + k] * sums[0:1] - sums[1 + k:2 + k] for k in range(3)]
        heat = sums[7:8]
        for k in range(3):
            heat = heat + st[4 + k:5 + k] * dx[k] - st[1 + k:2 + k] * sums[4 + k:5 + k]
            acc_out[k, a:a + 1] = jnp.where(live, press * dx[k], 0.0)
        er_out[a:a + 1] = jnp.where(live, -press * heat, 0.0)
        q = jnp.where(row == 0, 1.0, jnp.where(row <= 3, st, 0.0)) * (st[0:1] * press * ti)
        q1, q2 = halves(q)
        q_rows[a] = jnp.concatenate([q1, q2], axis=0).astype(BF16)

    t_out[...] = jnp.zeros_like(t_out)

    def mirror(tile, base):
        a, s, ni, nj = at(tile)
        q = q_rows[a]
        st = table[s]
        for jb in range(4):
            first = base + jb * ni
            g = gst[pl.ds(first, 4)].reshape(512, 256)
            o = nn(q, g)
            o = o[:8] + o[8:]
            o = o[:, :128] + o[:, 128:]
            cut = slice(jb * 128, (jb + 1) * 128)
            add_ = st[:, cut] * o[0:1] - o
            t_out[s, :, cut] += add_[0:4]
        return base + ni * nj
    lax.fori_loop(0, count, mirror, jnp.int32(U))

    for a in range(4):
        live = lane_id < n_ref[OWN + a, 0]
        for k in range(3):
            acc_out[k, a:a + 1] += jnp.where(live, t_out[OWN + a, 1 + k:2 + k], 0.0)


def compute(send, pairs, edge, table, energy):
    smem = pl.BlockSpec(memory_space=pltpu.SMEM)
    vmem = pl.BlockSpec(memory_space=pltpu.VMEM)
    return pl.pallas_call(
        compute_kernel,
        out_shape=(
            jax.ShapeDtypeStruct((4, 512), F32),
            jax.ShapeDtypeStruct((3, 4, 512), F32),
            jax.ShapeDtypeStruct((4, 512), F32),
            jax.ShapeDtypeStruct((NSLOT, 4, 512), F32),
        ),
        in_specs=[smem] * 3 + [vmem] * 2,
        out_specs=(vmem,) * 4,
        scratch_shapes=[
            pltpu.SMEM((MAXT + 2,), jnp.int32),
            pltpu.SMEM((MAXT + 2,), jnp.int32),
            pltpu.VMEM((NSLOT * 4, 48, 256), BF16),
            pltpu.VMEM((NSLOT * 4, 16, 256), BF16),
            pltpu.VMEM((NSLOT * 4, 8, 128), F32),
            pltpu.VMEM((16, 128, 48), BF16),
            pltpu.VMEM((16, 128, 128), F32),
            pltpu.VMEM((U, 128, 256), F32),
            pltpu.VMEM((U, 128, 256), F32),
            pltpu.VMEM((GBLK, 128, 256), BF16),
            pltpu.VMEM((16, 16, 128), F32),
            pltpu.VMEM((16, 128, 128), F32),
            pltpu.VMEM((4, 16, 512), BF16),
            pltpu.VMEM((NSLOT, 128), jnp.int32),
            pltpu.SMEM((NSLOT, 128), jnp.int32),
            pltpu.SemaphoreType.DMA,
        ],
        compiler_params=pltpu.CompilerParams(vmem_limit_bytes=63 * 1024 * 1024),
        name="tiles",
    )(send, pairs, edge, table, energy)


MESH = pl.DeviceIdType.MESH
PEERS = 32
LOWER, UPPER = 32, 33


def place():
    region, cell = lax.axis_index("region"), lax.axis_index("cell")
    count = lax.axis_size("region")
    return region, cell, lax.rem(region + count - 1, count), lax.rem(region + 1, count)


def greet():
    region, cell, below, above = place()
    barrier = pltpu.get_barrier_semaphore()

    def one(k, _):
        peer = lax.rem(cell + k, PEERS)
        pl.semaphore_signal(barrier, inc=1, device_id=(region, peer), device_id_type=MESH)
        return 0
    lax.fori_loop(1, PEERS, one, 0)
    pl.semaphore_signal(barrier, inc=1, device_id=(below, cell), device_id_type=MESH)
    pl.semaphore_signal(barrier, inc=1, device_id=(above, cell), device_id_type=MESH)
    return barrier


def remote(src, dst, send_sem, recv_sem, slot, mine, device):
    return pltpu.make_async_remote_copy(
        src_ref=src.at[slot],
        dst_ref=dst.at[mine],
        send_sem=send_sem.at[slot],
        recv_sem=recv_sem.at[mine],
        device_id=device,
        device_id_type=MESH,
    )


def exchange_kernel(counts, send_ref, edge_ref, positions, velocities, mass, smoothing, table,
                    own, payload, send_sem, recv_sem, local_sem):
    region, cell, below, above = place()
    barrier = greet()
    lane_id = lax.broadcasted_iota(jnp.int32, (1, 512), 1)
    for k in range(4):
        live = lane_id < counts[k]
        own[k] = jnp.concatenate(
            [jnp.where(live, mass[k:k + 1], 0.0)]
            + [positions[i, k:k + 1] - 0.5 for i in range(3)]
            + [velocities[i, k:k + 1] for i in range(3)]
            + [smoothing[k:k + 1]],
            axis=0,
        )
        pltpu.make_async_copy(own.at[k], table.at[OWN + k], local_sem.at[k]).start()
    low = (region > 0).astype(F32)
    high = (region < lax.axis_size("region") - 1).astype(F32)
    payload[LOWER] = own[edge_ref[0]] * low
    payload[UPPER] = own[edge_ref[1]] * high
    payload[cell] = jnp.zeros((8, 512), F32)
    pltpu.make_async_copy(payload.at[cell], table.at[cell], local_sem.at[4]).start()
    pl.semaphore_wait(barrier, PEERS + 1)
    remote(payload, table, send_sem, recv_sem, LOWER, UPPER, (below, cell)).start()
    remote(payload, table, send_sem, recv_sem, UPPER, LOWER, (above, cell)).start()

    def push(k, _):
        peer = lax.rem(cell + k, PEERS)
        pick = send_ref[peer]
        payload[peer] = jnp.where(pick >= 0, own[jnp.maximum(pick, 0)], 0.0)
        remote(payload, table, send_sem, recv_sem, peer, cell, (region, peer)).start()
        return 0
    lax.fori_loop(1, PEERS, push, 0)
    for k in range(4):
        pltpu.make_async_copy(own.at[k], table.at[OWN + k], local_sem.at[k]).wait()
    pltpu.make_async_copy(payload.at[cell], table.at[cell], local_sem.at[4]).wait()

    def finish(k, _):
        peer = lax.rem(cell + k, PEERS)
        copy = remote(payload, table, send_sem, recv_sem, peer, peer, (region, peer))
        copy.wait_recv()
        copy.wait_send()
        return 0
    lax.fori_loop(1, PEERS, finish, 0)
    for slot, device in ((LOWER, (below, cell)), (UPPER, (above, cell))):
        copy = remote(payload, table, send_sem, recv_sem, slot, slot, device)
        copy.wait_recv()
        copy.wait_send()


def exchange(counts, send, edge, positions, velocities, mass, smoothing):
    smem = pl.BlockSpec(memory_space=pltpu.SMEM)
    vmem = pl.BlockSpec(memory_space=pltpu.VMEM)
    return pl.pallas_call(
        exchange_kernel,
        out_shape=jax.ShapeDtypeStruct((NSLOT, 8, 512), F32),
        in_specs=[smem] * 3 + [vmem] * 4,
        out_specs=pl.BlockSpec(memory_space=pl.ANY),
        scratch_shapes=[
            pltpu.VMEM((4, 8, 512), F32),
            pltpu.VMEM((34, 8, 512), F32),
            pltpu.SemaphoreType.DMA((34,)),
            pltpu.SemaphoreType.DMA((34,)),
            pltpu.SemaphoreType.DMA((5,)),
        ],
        compiler_params=pltpu.CompilerParams(
            collective_id=0, has_side_effects=True, vmem_limit_bytes=60 * 1024 * 1024
        ),
        name="exchange",
    )(counts, send, edge, positions, velocities, mass, smoothing)


def return_kernel(counts, send_ref, edge_ref, back, part, accel, inbox, total, send_sem, recv_sem):
    region, cell, below, above = place()
    barrier = greet()
    pl.semaphore_wait(barrier, PEERS + 1)

    def push(k, _):
        peer = lax.rem(cell + k, PEERS)
        remote(back, inbox, send_sem, recv_sem, peer, cell, (region, peer)).start()
        return 0
    lax.fori_loop(1, PEERS, push, 0)
    remote(back, inbox, send_sem, recv_sem, LOWER, UPPER, (below, cell)).start()
    remote(back, inbox, send_sem, recv_sem, UPPER, LOWER, (above, cell)).start()
    total[...] = jnp.zeros_like(total)

    def gather(slot, device, target):
        copy = remote(back, inbox, send_sem, recv_sem, slot, slot, device)
        copy.wait_recv()
        copy.wait_send()
        rows = inbox[slot]
        for a in range(4):
            total[a] += jnp.where(target == a, rows, 0.0)

    def finish(k, _):
        peer = lax.rem(cell + k, PEERS)
        gather(peer, (region, peer), send_ref[peer])
        return 0
    lax.fori_loop(1, PEERS, finish, 0)
    gather(LOWER, (below, cell), edge_ref[0])
    gather(UPPER, (above, cell), edge_ref[1])
    lane_id = lax.broadcasted_iota(jnp.int32, (1, 512), 1)
    for a in range(4):
        live = lane_id < counts[a]
        for k in range(3):
            accel[k, a:a + 1] = part[k, a:a + 1] + jnp.where(live, total[a, 1 + k:2 + k], 0.0)


def give_back(counts, send, edge, back, part):
    smem = pl.BlockSpec(memory_space=pltpu.SMEM)
    vmem = pl.BlockSpec(memory_space=pltpu.VMEM)
    return pl.pallas_call(
        return_kernel,
        out_shape=jax.ShapeDtypeStruct((3, 4, 512), F32),
        in_specs=[smem] * 3 + [pl.BlockSpec(memory_space=pl.ANY), vmem],
        out_specs=vmem,
        scratch_shapes=[
            pltpu.VMEM((34, 4, 512), F32),
            pltpu.VMEM((4, 4, 512), F32),
            pltpu.SemaphoreType.DMA((34,)),
            pltpu.SemaphoreType.DMA((34,)),
        ],
        compiler_params=pltpu.CompilerParams(
            collective_id=1, has_side_effects=True, vmem_limit_bytes=60 * 1024 * 1024
        ),
        name="give_back",
    )(counts, send, edge, back, part)


def on_device(
    positions, velocities, mass, smoothing, energy, counts, send_cells, local_pairs, edge_cells
):
    send = send_cells.reshape(32)
    edge = edge_cells.reshape(2)
    table = exchange(counts, send, edge, positions, velocities, mass, smoothing)
    density, part, heat, back = compute(send, local_pairs.reshape(8), edge, table, energy)
    accel = give_back(counts, send, edge, back, part)
    return density, accel, heat


def solution(mesh):
    placed = (
        P(None, ("region", "cell"), None),
        P(None, ("region", "cell"), None),
        P(("region", "cell"), None),
        P(("region", "cell"), None),
        P(("region", "cell"), None),
        P(("region", "cell")),
        P("region", "cell", None, None),
        P("region", "cell", None, None),
        P("region", "cell", None),
    )
    return jax.shard_map(
        on_device,
        mesh=mesh,
        in_specs=placed,
        out_specs=(
            P(("region", "cell"), None),
            P(None, ("region", "cell"), None),
            P(("region", "cell"), None),
        ),
        check_vma=False,
    )
```

```python
import math
import jax
import jax.numpy as jnp
from jax import lax
from jax.experimental import pallas as pl
from jax.experimental.pallas import tpu as pltpu
from jax.sharding import PartitionSpec as P

GAMMA = 5.0 / 3.0
F32, BF16, I32 = jnp.float32, jnp.bfloat16, jnp.int32
U = 3
UL = 2
PEERS = 32
LOWER, UPPER, OWN, NSLOT = 32, 33, 34, 38
MAXT = 34
LOCAL = 104
GBLK = LOCAL + MAXT * 16 + 20 + 6 * U
ROOT = math.sqrt(24.0 / math.pi)
MIB = 1024 * 1024
MESH = pl.DeviceIdType.MESH


def halves(v):
    hi = v.astype(BF16).astype(F32)
    return hi, v - hi


def thirds(v):
    first, rest = halves(v)
    second, third = halves(rest)
    return first, second, third


def nt(a, b):
    return lax.dot_general(a, b, (((1,), (1,)), ((), ())), preferred_element_type=F32)


def nn(a, b):
    return lax.dot_general(a, b, (((1,), (0,)), ((), ())), preferred_element_type=F32)


def row_ids():
    return lax.broadcasted_iota(I32, (8, 512), 0)


def square(st):
    x = st[1:2]
    y = st[2:3]
    z = st[3:4]
    return x * x + y * y + z * z


def moments(st):
    row = row_ids()
    vx = st[1:2] * st[4:5] + st[2:3] * st[5:6] + st[3:4] * st[6:7]
    return jnp.where(row == 0, 1.0, jnp.where(row == 7, vx, st)) * st[0:1]


def pair_rows(v):
    first, second = halves(v)
    return jnp.concatenate([first, second], axis=0).astype(BF16)


def store_source(st, base, feat_s, rows_s, lane_s):
    row = row_ids()
    hinv = 1.0 / st[7:8]
    sj = ROOT * hinv * hinv
    f = jnp.where(row == 0, square(st), jnp.where(row <= 3, st, jnp.where(row == 4, 1.0, 0.0)))
    f1, f2, f3 = thirds(f)
    t1, t2, t3 = thirds(sj * hinv)
    t1 = jnp.where(row == 5, t1, 0.0)
    t2 = jnp.where(row == 5, t2, 0.0)
    t3 = jnp.where(row == 5, t3, 0.0)
    near = jnp.concatenate([f1, f1, f2, f2, f1, f3], axis=0).astype(BF16)
    ratio = jnp.concatenate([t1, t1, t2, t2, t1, t3], axis=0).astype(BF16)
    rows = pair_rows(moments(st))
    lane = jnp.where(row == 0, sj, st[0:1])
    for jb in range(4):
        cut = slice(jb * 128, (jb + 1) * 128)
        feat_s[base + jb, :, 0:128] = near[:, cut]
        feat_s[base + jb, :, 128:256] = ratio[:, cut]
        rows_s[base + jb, :, 0:128] = rows[:, cut]
        rows_s[base + jb, :, 128:256] = rows[:, cut]
        lane_s[base + jb] = lane[:, cut]


def store_target(st, base, feat_o, s_o, m_o, rows_o):
    row = row_ids()
    h = st[7:8]
    hinv = 1.0 / h
    si = ROOT * hinv * hinv
    ti = si * hinv
    f = jnp.where(row == 0, 1.0, jnp.where(row <= 3, -2.0 * st, jnp.where(row == 4, square(st), 0.0)))
    f = jnp.where(row == 5, h * h * h * (1.0 / ROOT), f * (ti * ti))
    f1, f2, f3 = thirds(f)
    s1, s2, s3 = thirds(si)
    m1, m2, m3 = thirds(st[0:1])
    extra = jnp.where(row == 0, s1, jnp.where(row == 1, s2, jnp.where(row == 2, s3, 0.0)))
    extra = jnp.where(row == 3, m1, jnp.where(row == 4, m2, jnp.where(row == 5, m3, extra)))
    whole = jnp.concatenate([f1, f2, f1, f2, f3, f1, extra, jnp.zeros((8, 512), F32)], axis=0).astype(BF16)
    rows = pair_rows(moments(st) * ti)
    size = (128, 128)
    eye = (lax.broadcasted_iota(I32, size, 0) == lax.broadcasted_iota(I32, size, 1)).astype(F32).astype(BF16)
    at = lax.broadcasted_iota(I32, (64, 256), 0)
    side = lax.broadcasted_iota(I32, (64, 256), 1) >= 128
    lowest = jnp.where(side, 51, 48)
    pick = ((at >= lowest) & (at < lowest + 3)).astype(F32).astype(BF16)
    for ib in range(4):
        cut = slice(ib * 128, (ib + 1) * 128)
        part = nt(eye, whole[:, cut]).astype(BF16)
        feat_o[base + ib] = part[:, :48]
        wide = nn(part, pick)
        s_o[base + ib] = wide[:, :128]
        m_o[base + ib] = wide[:, 128:]
        rows_o[base + ib] = rows[:, cut]


def split_store(gst, at, g):
    hi = g.astype(BF16)
    gst[at, :, 0:128] = hi
    gst[at, :, 128:256] = (g - hi.astype(F32)).astype(BF16)


def fold(v):
    return v[:, :128] + v[:, 128:]


def local_tiles(pair_ref, own, feat_s, rows_s, lane_s, feat_o, s_o, m_o, rows_o, near_a, near_b,
                gst, acc_w, row_w, acc_g, row_g):
    for a in range(4):
        store_source(own[a], a * 4, feat_s, rows_s, lane_s)
        store_target(own[a], a * 4, feat_o, s_o, m_o, rows_o)
    acc_w[...] = jnp.zeros_like(acc_w)
    row_w[...] = jnp.zeros_like(row_w)
    acc_g[...] = jnp.zeros_like(acc_g)
    row_g[...] = jnp.zeros_like(row_g)
    for u in range(UL):
        gst[LOCAL + 2 * UL + u] = jnp.zeros((128, 256), BF16)

    def where(n):
        n = jnp.minimum(n, LOCAL - 1)
        t = lax.rem(n, 10)
        j1 = (t >= 1).astype(I32) + (t >= 3).astype(I32) + (t >= 6).astype(I32)
        i1 = t - (j1 * (j1 + 1)) // 2
        m = jnp.maximum(n - 40, 0)
        k = m // 16
        self_ = n < 40
        ib = jnp.where(self_, i1, lax.rem(m, 4))
        jb = jnp.where(self_, j1, lax.rem(m // 4, 4))
        a = jnp.where(self_, n // 10, pair_ref[0, k])
        b = jnp.where(self_, n // 10, pair_ref[1, k])
        group = jnp.where(self_, n // 10, 4 + k)
        both = jnp.where(self_ & (i1 == j1), 0.0, 1.0)
        return a * 4 + ib, b * 4 + jb, group * 4 + ib, group * 4 + jb, both

    def distances(buf, n):
        for u in range(UL):
            oi, sj, _, _, _ = where(n + u)
            buf[u] = nn(feat_o[oi], feat_s[sj])

    def elements(buf, n):
        for u in range(UL):
            oi, si, gi, gj, both = where(n + u)
            both = jnp.where(n + u < LOCAL, both, 0.0)
            sj = lane_s[si][0:1]
            mass = jnp.where(n + u < LOCAL, lane_s[si][1:2], 0.0)
            d2 = jnp.maximum(buf[u, :, 0:128], 1e-6)
            inv = lax.rsqrt(d2)
            pi = d2 * inv
            pj = pi * buf[u, :, 128:256]
            ai = jnp.maximum(s_o[oi] - pi, 0.0)
            ci = jnp.maximum(ai - pi, 0.0)
            aj = jnp.maximum(sj - pj, 0.0)
            cj = jnp.maximum(aj - pj, 0.0)
            qa = ai * ai
            qc = ci * ci
            ra = aj * aj
            rc = cj * cj
            acc_w[gi] += ((ai + ai) * qa - qc * ci) * mass
            back = ((aj + aj) * ra - rc * cj) * m_o[oi]
            row_w[gj] += both * jnp.sum(back.reshape(16, 8, 128), axis=0)
            split_store(gst, n + u, (qa - qc + ra - rc) * inv)

    def products(n, slot):
        out = []
        for u in range(UL):
            oi, sj, _, _, _ = where(jnp.maximum(n + u, 0))
            g = gst[slot + u]
            out.append((nt(rows_s[sj], g), fold(nn(rows_o[oi], g))))
        return out

    def collect(sums, n):
        for u in range(UL):
            _, _, gi, gj, both = where(jnp.maximum(n + u, 0))
            good = (n + u >= 0) & (n + u < LOCAL)
            acc_g[gi] += jnp.where(good, sums[u][0], 0.0)
            row_g[gj] += jnp.where(good, sums[u][1], 0.0) * both

    distances(near_a, 0)
    step = 2 * UL

    def body(n, _):
        base = n * step
        before = jnp.where(n == 0, LOCAL + 2 * UL, base - UL)
        sums = products(base - UL, before)
        elements(near_a, base)
        distances(near_b, base + UL)
        collect(sums, base - UL)
        sums = products(base, base)
        elements(near_b, base + UL)
        distances(near_a, base + step)
        collect(sums, base)
        return 0
    lax.fori_loop(0, LOCAL // step, body, 0)
    sums = products(LOCAL - UL, LOCAL - UL)
    collect(sums, LOCAL - UL)


LOCAL_SCRATCH = [
    pltpu.VMEM((16, 48, 256), BF16),
    pltpu.VMEM((16, 16, 256), BF16),
    pltpu.VMEM((16, 8, 128), F32),
    pltpu.VMEM((16, 128, 48), BF16),
    pltpu.VMEM((16, 128, 128), F32),
    pltpu.VMEM((16, 128, 128), F32),
    pltpu.VMEM((16, 16, 128), BF16),
    pltpu.VMEM((UL, 128, 256), F32),
    pltpu.VMEM((UL, 128, 256), F32),
    pltpu.VMEM((LOCAL + 3 * UL, 128, 256), BF16),
    pltpu.VMEM((32, 128, 128), F32),
    pltpu.VMEM((32, 8, 128), F32),
    pltpu.VMEM((32, 16, 128), F32),
    pltpu.VMEM((32, 16, 128), F32),
]
LOCAL_OUT = (
    jax.ShapeDtypeStruct((LOCAL, 128, 256), BF16),
    jax.ShapeDtypeStruct((32, 128, 128), F32),
    jax.ShapeDtypeStruct((32, 8, 128), F32),
    jax.ShapeDtypeStruct((32, 16, 128), F32),
    jax.ShapeDtypeStruct((32, 16, 128), F32),
    jax.ShapeDtypeStruct((16, 128, 48), BF16),
    jax.ShapeDtypeStruct((16, 128, 128), F32),
)
NLOCAL = len(LOCAL_OUT)


def local_results(scratch):
    feat_o, s_o = scratch[3], scratch[4]
    gst, acc_w, row_w, acc_g, row_g = scratch[9:14]
    return gst.at[pl.ds(0, LOCAL)], acc_w, row_w, acc_g, row_g, feat_o, s_o


def compute_kernel(send_ref, pair_ref, edge_ref, table, energy, g_in, w_in, roww_in, gg_in, rowg_in, feat_o, s_o,
                   rho_out, acc_out, er_out, t_out,
                   ta, ts, feat_s, rows_s, lane_s, near_a, near_b, gst, acc_g, acc_w, q_rows, q_wide,
                   cnt_v, n_ref, w_pair, cnt_sem, g_sem, w_sem):
    found = jnp.sum((table[:, 0, :] > 0.0).astype(F32), axis=1, keepdims=True)
    cnt_v[...] = jnp.broadcast_to(found, (NSLOT, 128)).astype(I32)
    fetch = pltpu.make_async_copy(cnt_v, n_ref, cnt_sem)
    fetch.start()
    get_g = pltpu.make_async_copy(g_in, gst.at[pl.ds(0, LOCAL)], g_sem)
    get_w = pltpu.make_async_copy(w_in.at[pl.ds(0, 16)], acc_w, w_sem.at[0])
    get_p = pltpu.make_async_copy(w_in.at[pl.ds(16, 16)], w_pair, w_sem.at[1])
    get_w.start()
    get_p.start()
    get_g.start()
    row = row_ids()
    for k in range(16):
        acc_g[k] = gg_in[k]
    for u in range(U):
        gst[LOCAL + u] = jnp.zeros((128, 256), BF16)
    t_out[...] = jnp.zeros_like(t_out)
    fetch.wait()

    def blocks(s):
        return (n_ref[s, 0] + 127) >> 7

    def add(count, a, s):
        ta[count] = a
        ts[count] = s
        return count + (n_ref[s, 0] > 0).astype(I32)
    count = lax.fori_loop(0, 32, lambda s, cnt: add(cnt, jnp.maximum(send_ref[s], 0), s), I32(0))
    count = add(count, edge_ref[0], I32(LOWER))
    count = add(count, edge_ref[1], I32(UPPER))
    ta[count] = ta[0]
    ts[count] = ts[0]
    total = lax.fori_loop(0, count, lambda k, v: v + blocks(OWN + ta[k]) * blocks(ts[k]), I32(0))

    def source_loop(k, _):
        for u in range(2):
            s = ts[2 * k + u]
            store_source(table[s], s * 4, feat_s, rows_s, lane_s)
        return 0
    lax.fori_loop(0, (count + 1) // 2, source_loop, 0)
    get_w.wait()

    def at(tile):
        a, s = ta[tile], ts[tile]
        return a, s, blocks(OWN + a), blocks(s)

    def advance(state):
        tile, ib, jb, a, s, ni, nj = state
        ib = ib + 1
        wrap_i = ib >= ni
        ib = jnp.where(wrap_i, 0, ib)
        jb = jnp.where(wrap_i, jb + 1, jb)
        wrap_j = jb >= nj
        jb = jnp.where(wrap_j, 0, jb)
        tile = jnp.where(wrap_j, jnp.minimum(tile + 1, count), tile)
        return (tile, ib, jb) + at(tile)

    def group(state):
        out = []
        for _ in range(U):
            out.append((state[3] * 4 + state[1], state[4] * 4 + state[2]))
            state = advance(state)
        return state, tuple(out)

    def distances(buf, where):
        for u in range(U):
            buf[u] = nn(feat_o[where[u][0]], feat_s[where[u][1]])

    def elements(buf, where, base):
        for u in range(U):
            oi, si = where[u]
            sj = lane_s[si][0:1]
            mass = lane_s[si][1:2] * (base + u < total).astype(F32)
            d2 = jnp.maximum(buf[u, :, 0:128], 1e-6)
            inv = lax.rsqrt(d2)
            pi = d2 * inv
            pj = pi * buf[u, :, 128:256]
            ai = jnp.maximum(s_o[oi] - pi, 0.0)
            ci = jnp.maximum(ai - pi, 0.0)
            qa = ai * ai
            qc = ci * ci
            acc_w[oi] += ((ai + ai) * qa - qc * ci) * mass
            aj = jnp.maximum(sj - pj, 0.0)
            mj = jnp.minimum(pj, aj)
            split_store(gst, LOCAL + base + U + u, (qa - qc + mj * (aj + aj - mj)) * inv)

    def products(where, base):
        return [nt(rows_s[where[u][1]], gst[LOCAL + base + U + u]) for u in range(U)]

    def collect(sums, where, base):
        for u in range(U):
            acc_g[where[u][0]] += jnp.where(base + u < total, sums[u], 0.0)

    zero = I32(0)
    walk, first = group((zero, zero, zero) + at(zero))
    walk, second = group(walk)
    distances(near_a, first)

    def body(n, carry):
        walk, prev, now, later = carry
        base = n * (2 * U)
        sums = products(prev, base - U)
        elements(near_a, now, base)
        distances(near_b, later)
        collect(sums, prev, base - U)
        walk, after = group(walk)
        sums = products(now, base)
        elements(near_b, later, base + U)
        distances(near_a, after)
        collect(sums, now, base)
        walk, last = group(walk)
        return walk, later, after, last

    steps = (total + 2 * U - 1) // (2 * U)
    lax.fori_loop(0, steps + 1, body, (walk, first, first, second))

    def clear(k, _):
        gst[LOCAL + (2 * steps + 3) * U + k] = jnp.zeros((128, 256), BF16)
        return 0
    lax.fori_loop(0, 17, clear, 0)

    get_p.wait()
    lane_id = lax.broadcasted_iota(I32, (1, 512), 1)
    row_sum = [None] * 4
    flat = [None] * 4
    for a in range(4):
        row_sum[a] = jnp.concatenate([roww_in[a * 4 + b] for b in range(4)], axis=1)
        flat[a] = jnp.concatenate([rowg_in[a * 4 + b] for b in range(4)], axis=1)
    for k in range(4):
        ka, kb = pair_ref[0, k], pair_ref[1, k]
        rw = jnp.concatenate([roww_in[16 + k * 4 + b] for b in range(4)], axis=1)
        rg = jnp.concatenate([rowg_in[16 + k * 4 + b] for b in range(4)], axis=1)
        for a in range(4):
            row_sum[a] = row_sum[a] + jnp.where(kb == a, rw, 0.0)
            flat[a] = flat[a] + jnp.where(kb == a, rg, 0.0)
        for b in range(4):
            acc_g[ka * 4 + b] += gg_in[16 + k * 4 + b]
            acc_w[ka * 4 + b] += w_pair[k * 4 + b]

    for a in range(4):
        st = table[OWN + a]
        h = st[7:8]
        h3 = h * h * h
        ti = ROOT / h3
        sums = jnp.concatenate([acc_g[a * 4 + ib] for ib in range(4)], axis=1)
        sums = (sums[:8] + sums[8:]) * ti + flat[a][:8] + flat[a][8:]
        wsum = jnp.concatenate([jnp.sum(acc_w[a * 4 + ib].T, axis=0, keepdims=True) for ib in range(4)], axis=1)
        wsum = wsum + jnp.sum(row_sum[a], axis=0, keepdims=True)
        rho = wsum * (h3 * (8.0 / math.pi / ROOT ** 3))
        live = lane_id < n_ref[OWN + a, 0]
        press = jnp.where(live, (GAMMA - 1.0) * energy[a:a + 1] / jnp.where(live, rho, 1.0), 0.0)
        rho_out[a:a + 1] = jnp.where(live, rho, 0.0)
        dx = [st[1 + k:2 + k] * sums[0:1] - sums[1 + k:2 + k] for k in range(3)]
        heat = sums[7:8]
        for k in range(3):
            heat = heat + st[4 + k:5 + k] * dx[k] - st[1 + k:2 + k] * sums[4 + k:5 + k]
            acc_out[k, a:a + 1] = jnp.where(live, press * dx[k], 0.0)
        er_out[a:a + 1] = jnp.where(live, -press * heat, 0.0)
        q = jnp.where(row == 0, 1.0, jnp.where(row <= 3, st, 0.0)) * (st[0:1] * press)
        q_rows[a] = pair_rows(q * ti)
        plain = pair_rows(q)
        for jb in range(4):
            cut = slice(jb * 128, (jb + 1) * 128)
            q_wide[a * 4 + jb, :, 0:128] = plain[:, cut]
            q_wide[a * 4 + jb, :, 128:256] = plain[:, cut]
    get_g.wait()

    def settle(s, cut, o, good):
        o = o[:8] + o[8:]
        st = table[s][:, cut]
        extra = st * o[0:1] - o
        t_out[s, :, cut] += jnp.where(good, extra[0:4], 0.0)

    def mirror(step, base):
        for u in range(2):
            tile = 2 * step + u
            a, s, ni, nj = at(tile)
            q = q_rows[a]
            for jb in range(4):
                g = gst[pl.ds(LOCAL + base + jb * ni, 4)].reshape(512, 256)
                settle(s, slice(jb * 128, (jb + 1) * 128), fold(nn(q, g)), tile < count)
            base = base + ni * nj
        return base
    lax.fori_loop(0, (count + 1) // 2, mirror, I32(U))

    for a in range(4):
        ti = ROOT / (table[OWN + a][7:8] * table[OWN + a][7:8] * table[OWN + a][7:8])
        for jb in range(4):
            first = a * 10 + (jb * (jb + 1)) // 2
            cut = slice(jb * 128, (jb + 1) * 128)
            g = gst[pl.ds(first, jb + 1)].reshape((jb + 1) * 128, 256)
            o = fold(nn(q_rows[a, :, 0:(jb + 1) * 128], g))
            for other in range(jb + 1, 4):
                at_ = a * 10 + (other * (other + 1)) // 2 + jb
                o = o + nt(q_wide[a * 4 + other], gst[at_]) * ti[:, cut]
            settle(OWN + a, cut, o, True)
    for k in range(4):
        ka, kb = pair_ref[0, k], pair_ref[1, k]
        hk = table[OWN + ka][7:8]
        ti = ROOT / (hk * hk * hk)
        for jb in range(4):
            cut = slice(jb * 128, (jb + 1) * 128)
            first = 40 + k * 16
            g = gst[pl.ds(first + jb * 4, 4)].reshape(512, 256)
            settle(OWN + kb, cut, fold(nn(q_rows[ka], g)), True)
            o = nt(q_wide[kb * 4], gst[first + jb])
            for other in range(1, 4):
                o = o + nt(q_wide[kb * 4 + other], gst[first + other * 4 + jb])
            settle(OWN + ka, cut, o * ti[:, cut], True)

    for a in range(4):
        live = lane_id < n_ref[OWN + a, 0]
        for k in range(3):
            acc_out[k, a:a + 1] += jnp.where(live, t_out[OWN + a, 1 + k:2 + k], 0.0)


def compute(send, pairs, edge, table, energy, local):
    smem = pl.BlockSpec(memory_space=pltpu.SMEM)
    vmem = pl.BlockSpec(memory_space=pltpu.VMEM)
    hbm = pl.BlockSpec(memory_space=pl.ANY)
    return pl.pallas_call(
        compute_kernel,
        out_shape=(
            jax.ShapeDtypeStruct((4, 512), F32),
            jax.ShapeDtypeStruct((3, 4, 512), F32),
            jax.ShapeDtypeStruct((4, 512), F32),
            jax.ShapeDtypeStruct((NSLOT, 4, 512), F32),
        ),
        in_specs=[smem] * 3 + [vmem] * 2 + [hbm] * 2 + [vmem] * 5,
        out_specs=(vmem,) * 4,
        scratch_shapes=[
            pltpu.SMEM((MAXT + 2,), I32),
            pltpu.SMEM((MAXT + 2,), I32),
            pltpu.VMEM((34 * 4, 48, 256), BF16),
            pltpu.VMEM((34 * 4, 16, 256), BF16),
            pltpu.VMEM((34 * 4, 8, 128), F32),
            pltpu.VMEM((U, 128, 256), F32),
            pltpu.VMEM((U, 128, 256), F32),
            pltpu.VMEM((GBLK, 128, 256), BF16),
            pltpu.VMEM((16, 16, 128), F32),
            pltpu.VMEM((16, 128, 128), F32),
            pltpu.VMEM((4, 16, 512), BF16),
            pltpu.VMEM((16, 16, 256), BF16),
            pltpu.VMEM((NSLOT, 128), I32),
            pltpu.SMEM((NSLOT, 128), I32),
            pltpu.VMEM((16, 128, 128), F32),
            pltpu.SemaphoreType.DMA,
            pltpu.SemaphoreType.DMA,
            pltpu.SemaphoreType.DMA((2,)),
        ],
        compiler_params=pltpu.CompilerParams(vmem_limit_bytes=62 * MIB),
        name="tiles",
    )(send, pairs, edge, table, energy, *local)


def place():
    region, cell = lax.axis_index("region"), lax.axis_index("cell")
    count = lax.axis_size("region")
    return region, cell, lax.rem(region + count - 1, count), lax.rem(region + 1, count)


def greet():
    region, cell, below, above = place()
    barrier = pltpu.get_barrier_semaphore()

    def one(k, _):
        peer = lax.rem(cell + k, PEERS)
        pl.semaphore_signal(barrier, inc=1, device_id=(region, peer), device_id_type=MESH)
        return 0
    lax.fori_loop(1, PEERS, one, 0)
    pl.semaphore_signal(barrier, inc=1, device_id=(below, cell), device_id_type=MESH)
    pl.semaphore_signal(barrier, inc=1, device_id=(above, cell), device_id_type=MESH)
    return barrier


def remote(src, dst, send_sem, recv_sem, slot, mine, device):
    return pltpu.make_async_remote_copy(
        src_ref=src.at[slot],
        dst_ref=dst.at[mine],
        send_sem=send_sem.at[slot],
        recv_sem=recv_sem.at[mine],
        device_id=device,
        device_id_type=MESH,
    )


def exchange_kernel(counts, send_ref, edge_ref, pair_ref, positions, velocities, mass, smoothing, table, *refs):
    outs, scratch = refs[:NLOCAL], refs[NLOCAL:-5]
    own, payload, send_sem, recv_sem, local_sem = refs[-5:]
    region, cell, below, above = place()
    barrier = greet()
    lane_id = lax.broadcasted_iota(I32, (1, 512), 1)
    for k in range(4):
        live = lane_id < counts[k]
        own[k] = jnp.concatenate(
            [jnp.where(live, mass[k:k + 1], 0.0)]
            + [positions[i, k:k + 1] - 0.5 for i in range(3)]
            + [velocities[i, k:k + 1] for i in range(3)]
            + [smoothing[k:k + 1]],
            axis=0,
        )
        pltpu.make_async_copy(own.at[k], table.at[OWN + k], local_sem.at[k]).start()
    low = (region > 0).astype(F32)
    high = (region < lax.axis_size("region") - 1).astype(F32)
    payload[LOWER] = own[edge_ref[0]] * low
    payload[UPPER] = own[edge_ref[1]] * high
    payload[cell] = jnp.zeros((8, 512), F32)
    pltpu.make_async_copy(payload.at[cell], table.at[cell], local_sem.at[4]).start()
    pl.semaphore_wait(barrier, PEERS + 1)
    remote(payload, table, send_sem, recv_sem, LOWER, UPPER, (below, cell)).start()
    remote(payload, table, send_sem, recv_sem, UPPER, LOWER, (above, cell)).start()

    def push(k, _):
        peer = lax.rem(cell + k, PEERS)
        pick = send_ref[peer]
        payload[peer] = jnp.where(pick >= 0, own[jnp.maximum(pick, 0)], 0.0)
        remote(payload, table, send_sem, recv_sem, peer, cell, (region, peer)).start()
        return 0
    lax.fori_loop(1, PEERS, push, 0)

    local_tiles(pair_ref, own, *scratch)
    copies = [
        pltpu.make_async_copy(src, dst, local_sem.at[5 + i])
        for i, (src, dst) in enumerate(zip(local_results(scratch), outs))
    ]
    for copy in copies:
        copy.start()
    for k in range(4):
        pltpu.make_async_copy(own.at[k], table.at[OWN + k], local_sem.at[k]).wait()
    pltpu.make_async_copy(payload.at[cell], table.at[cell], local_sem.at[4]).wait()

    def finish(k, _):
        peer = lax.rem(cell + k, PEERS)
        copy = remote(payload, table, send_sem, recv_sem, peer, peer, (region, peer))
        copy.wait_recv()
        copy.wait_send()
        return 0
    lax.fori_loop(1, PEERS, finish, 0)
    for slot, device in ((LOWER, (below, cell)), (UPPER, (above, cell))):
        copy = remote(payload, table, send_sem, recv_sem, slot, slot, device)
        copy.wait_recv()
        copy.wait_send()
    for copy in copies:
        copy.wait()


def exchange(counts, send, edge, pairs, positions, velocities, mass, smoothing):
    smem = pl.BlockSpec(memory_space=pltpu.SMEM)
    vmem = pl.BlockSpec(memory_space=pltpu.VMEM)
    hbm = pl.BlockSpec(memory_space=pl.ANY)
    return pl.pallas_call(
        exchange_kernel,
        out_shape=(jax.ShapeDtypeStruct((NSLOT, 8, 512), F32),) + LOCAL_OUT,
        in_specs=[smem] * 4 + [vmem] * 4,
        out_specs=(hbm,) * (1 + NLOCAL),
        scratch_shapes=LOCAL_SCRATCH + [
            pltpu.VMEM((4, 8, 512), F32),
            pltpu.VMEM((34, 8, 512), F32),
            pltpu.SemaphoreType.DMA((34,)),
            pltpu.SemaphoreType.DMA((34,)),
            pltpu.SemaphoreType.DMA((5 + NLOCAL,)),
        ],
        compiler_params=pltpu.CompilerParams(
            collective_id=0, has_side_effects=True, vmem_limit_bytes=60 * MIB
        ),
        name="exchange",
    )(counts, send, edge, pairs, positions, velocities, mass, smoothing)


def return_kernel(counts, send_ref, edge_ref, back, accel, inbox, total, send_sem, recv_sem):
    region, cell, below, above = place()
    barrier = greet()
    pl.semaphore_wait(barrier, PEERS + 1)

    def push(k, _):
        peer = lax.rem(cell + k, PEERS)
        remote(back, inbox, send_sem, recv_sem, peer, cell, (region, peer)).start()
        return 0
    lax.fori_loop(1, PEERS, push, 0)
    remote(back, inbox, send_sem, recv_sem, LOWER, UPPER, (below, cell)).start()
    remote(back, inbox, send_sem, recv_sem, UPPER, LOWER, (above, cell)).start()
    total[...] = jnp.zeros_like(total)

    def gather(slot, device, target):
        copy = remote(back, inbox, send_sem, recv_sem, slot, slot, device)
        copy.wait_recv()
        copy.wait_send()
        rows = inbox[slot]
        for a in range(4):
            total[a] += jnp.where(target == a, rows, 0.0)

    def finish(k, _):
        peer = lax.rem(cell + k, PEERS)
        gather(peer, (region, peer), send_ref[peer])
        return 0
    lax.fori_loop(1, PEERS, finish, 0)
    gather(LOWER, (below, cell), edge_ref[0])
    gather(UPPER, (above, cell), edge_ref[1])
    lane_id = lax.broadcasted_iota(jnp.int32, (1, 512), 1)
    for a in range(4):
        live = lane_id < counts[a]
        for k in range(3):
            accel[k, a:a + 1] = jnp.where(live, total[a, 1 + k:2 + k], 0.0)


def give_back(counts, send, edge, back):
    smem = pl.BlockSpec(memory_space=pltpu.SMEM)
    vmem = pl.BlockSpec(memory_space=pltpu.VMEM)
    return pl.pallas_call(
        return_kernel,
        out_shape=jax.ShapeDtypeStruct((3, 4, 512), F32),
        in_specs=[smem] * 3 + [pl.BlockSpec(memory_space=pl.ANY)],
        out_specs=vmem,
        scratch_shapes=[
            pltpu.VMEM((34, 4, 512), F32),
            pltpu.VMEM((4, 4, 512), F32),
            pltpu.SemaphoreType.DMA((34,)),
            pltpu.SemaphoreType.DMA((34,)),
        ],
        compiler_params=pltpu.CompilerParams(
            collective_id=1, has_side_effects=True, vmem_limit_bytes=60 * MIB
        ),
        name="give_back",
    )(counts, send, edge, back)


def on_device(
    positions, velocities, mass, smoothing, energy, counts, send_cells, local_pairs, edge_cells
):
    send = send_cells.reshape(32)
    edge = edge_cells.reshape(2)
    pairs = local_pairs[0, 0].T
    table, *local = exchange(counts, send, edge, pairs, positions, velocities, mass, smoothing)
    density, part, heat, back = compute(send, pairs, edge, table, energy, local)
    return density, part + give_back(counts, send, edge, back), heat


def solution(mesh):
    placed = (
        P(None, ("region", "cell"), None),
        P(None, ("region", "cell"), None),
        P(("region", "cell"), None),
        P(("region", "cell"), None),
        P(("region", "cell"), None),
        P(("region", "cell")),
        P("region", "cell", None, None),
        P("region", "cell", None, None),
        P("region", "cell", None),
    )
    return jax.shard_map(
        on_device,
        mesh=mesh,
        in_specs=placed,
        out_specs=(
            P(("region", "cell"), None),
            P(None, ("region", "cell"), None),
            P(("region", "cell"), None),
        ),
        check_vma=False,
    )
```

```python
import math
import jax
import jax.numpy as jnp
from jax import lax
from jax.experimental import pallas as pl
from jax.experimental.pallas import tpu as pltpu
from jax.sharding import PartitionSpec as P

GAMMA = 5.0 / 3.0
F32, BF16, I32 = jnp.float32, jnp.bfloat16, jnp.int32
U = 3
UL = 2
PEERS = 32
LOWER, UPPER, OWN, NSLOT = 32, 33, 34, 38
MAXT = 34
LOCAL = 104
GBLK = MAXT * 16 + 20 + 6 * U
ROOT = math.sqrt(24.0 / math.pi)
MIB = 1024 * 1024
MESH = pl.DeviceIdType.MESH


def halves(v):
    hi = v.astype(BF16).astype(F32)
    return hi, v - hi


def thirds(v):
    first, rest = halves(v)
    second, third = halves(rest)
    return first, second, third


def nt(a, b):
    return lax.dot_general(a, b, (((1,), (1,)), ((), ())), preferred_element_type=F32)


def nn(a, b):
    return lax.dot_general(a, b, (((1,), (0,)), ((), ())), preferred_element_type=F32)


def row_ids():
    return lax.broadcasted_iota(I32, (8, 512), 0)


def square(st):
    x = st[1:2]
    y = st[2:3]
    z = st[3:4]
    return x * x + y * y + z * z


def moments(st):
    row = row_ids()
    vx = st[1:2] * st[4:5] + st[2:3] * st[5:6] + st[3:4] * st[6:7]
    return jnp.where(row == 0, 1.0, jnp.where(row == 7, vx, st)) * st[0:1]


def pair_rows(v):
    first, second = halves(v)
    return jnp.concatenate([first, second], axis=0).astype(BF16)


def store_source(st, base, feat_s, rows_s, lane_s):
    row = row_ids()
    hinv = 1.0 / st[7:8]
    sj = ROOT * hinv * hinv
    f = jnp.where(row == 0, square(st), jnp.where(row <= 3, st, jnp.where(row == 4, 1.0, 0.0)))
    f1, f2, f3 = thirds(f)
    t1, t2, t3 = thirds(sj * hinv)
    t1 = jnp.where(row == 5, t1, 0.0)
    t2 = jnp.where(row == 5, t2, 0.0)
    t3 = jnp.where(row == 5, t3, 0.0)
    near = jnp.concatenate([f1, f1, f2, f2, f1, f3], axis=0).astype(BF16)
    ratio = jnp.concatenate([t1, t1, t2, t2, t1, t3], axis=0).astype(BF16)
    rows = pair_rows(moments(st))
    lane = jnp.where(row == 0, sj, st[0:1])
    for jb in range(4):
        cut = slice(jb * 128, (jb + 1) * 128)
        feat_s[base + jb, :, 0:128] = near[:, cut]
        feat_s[base + jb, :, 128:256] = ratio[:, cut]
        rows_s[base + jb, :, 0:128] = rows[:, cut]
        rows_s[base + jb, :, 128:256] = rows[:, cut]
        lane_s[base + jb] = lane[:, cut]


def store_target(st, base, feat_o, s_o, m_o, rows_o):
    row = row_ids()
    h = st[7:8]
    hinv = 1.0 / h
    si = ROOT * hinv * hinv
    ti = si * hinv
    f = jnp.where(row == 0, 1.0, jnp.where(row <= 3, -2.0 * st, jnp.where(row == 4, square(st), 0.0)))
    f = jnp.where(row == 5, h * h * h * (1.0 / ROOT), f * (ti * ti))
    f1, f2, f3 = thirds(f)
    s1, s2, s3 = thirds(si)
    m1, m2, m3 = thirds(st[0:1])
    extra = jnp.where(row == 0, s1, jnp.where(row == 1, s2, jnp.where(row == 2, s3, 0.0)))
    extra = jnp.where(row == 3, m1, jnp.where(row == 4, m2, jnp.where(row == 5, m3, extra)))
    whole = jnp.concatenate([f1, f2, f1, f2, f3, f1, extra, jnp.zeros((8, 512), F32)], axis=0).astype(BF16)
    rows = pair_rows(moments(st) * ti)
    size = (128, 128)
    eye = (lax.broadcasted_iota(I32, size, 0) == lax.broadcasted_iota(I32, size, 1)).astype(F32).astype(BF16)
    at = lax.broadcasted_iota(I32, (64, 256), 0)
    side = lax.broadcasted_iota(I32, (64, 256), 1) >= 128
    lowest = jnp.where(side, 51, 48)
    pick = ((at >= lowest) & (at < lowest + 3)).astype(F32).astype(BF16)
    for ib in range(4):
        cut = slice(ib * 128, (ib + 1) * 128)
        part = nt(eye, whole[:, cut]).astype(BF16)
        feat_o[base + ib] = part[:, :48]
        wide = nn(part, pick)
        s_o[base + ib] = wide[:, :128]
        m_o[base + ib] = wide[:, 128:]
        rows_o[base + ib] = rows[:, cut]


def split_store(gst, at, g):
    hi = g.astype(BF16)
    gst[at, :, 0:128] = hi
    gst[at, :, 128:256] = (g - hi.astype(F32)).astype(BF16)


def fold(v):
    return v[:, :128] + v[:, 128:]


def local_features(own, feat_s, rows_s, lane_s, feat_o, s_o, m_o, rows_o, *_):
    for a in range(4):
        store_source(own[a], a * 4, feat_s, rows_s, lane_s)
        store_target(own[a], a * 4, feat_o, s_o, m_o, rows_o)


def local_tiles(pair_ref, emit, feat_s, rows_s, lane_s, feat_o, s_o, m_o, rows_o, near_a, near_b,
                gst, acc_w, row_w, acc_g, row_g):
    acc_w[...] = jnp.zeros_like(acc_w)
    row_w[...] = jnp.zeros_like(row_w)
    acc_g[...] = jnp.zeros_like(acc_g)
    row_g[...] = jnp.zeros_like(row_g)
    for u in range(UL):
        gst[LOCAL + 2 * UL + u] = jnp.zeros((128, 256), BF16)

    def where(n):
        n = jnp.minimum(n, LOCAL - 1)
        t = lax.rem(n, 10)
        j1 = (t >= 1).astype(I32) + (t >= 3).astype(I32) + (t >= 6).astype(I32)
        i1 = t - (j1 * (j1 + 1)) // 2
        m = jnp.maximum(n - 40, 0)
        k = m // 16
        self_ = n < 40
        ib = jnp.where(self_, i1, lax.rem(m, 4))
        jb = jnp.where(self_, j1, lax.rem(m // 4, 4))
        a = jnp.where(self_, n // 10, pair_ref[0, k])
        b = jnp.where(self_, n // 10, pair_ref[1, k])
        group = jnp.where(self_, n // 10, 4 + k)
        both = jnp.where(self_ & (i1 == j1), 0.0, 1.0)
        return a * 4 + ib, b * 4 + jb, group * 4 + ib, group * 4 + jb, both

    def group(n):
        return tuple(where(n + u) for u in range(UL))

    def distances(buf, those):
        for u in range(UL):
            buf[u] = nn(feat_o[those[u][0]], feat_s[those[u][1]])

    def elements(buf, those, n):
        for u in range(UL):
            oi, si, gi, gj, both = those[u]
            sj = lane_s[si][0:1]
            mass = lane_s[si][1:2]
            d2 = jnp.maximum(buf[u, :, 0:128], 1e-6)
            inv = lax.rsqrt(d2)
            pi = d2 * inv
            pj = pi * buf[u, :, 128:256]
            ai = jnp.maximum(s_o[oi] - pi, 0.0)
            ci = jnp.maximum(ai - pi, 0.0)
            aj = jnp.maximum(sj - pj, 0.0)
            cj = jnp.maximum(aj - pj, 0.0)
            qa = ai * ai
            qc = ci * ci
            ra = aj * aj
            rc = cj * cj
            acc_w[gi] += ((ai + ai) * qa - qc * ci) * mass
            back = ((aj + aj) * ra - rc * cj) * m_o[oi]
            row_w[gj] += both * jnp.sum(back.reshape(16, 8, 128), axis=0)
            split_store(gst, n + u, (qa - qc + ra - rc) * inv)

    def products(those, slot):
        out = []
        for u in range(UL):
            g = gst[slot + u]
            out.append((nt(rows_s[those[u][1]], g), fold(nn(rows_o[those[u][0]], g))))
        return out

    def collect(sums, those):
        for u in range(UL):
            _, _, gi, gj, both = those[u]
            acc_g[gi] += sums[u][0]
            row_g[gj] += sums[u][1] * both

    step = 2 * UL

    def body(n, carry):
        prev, now, later = carry
        base = n * step
        before = jnp.where(n == 0, LOCAL + 2 * UL, base - UL)
        sums = products(prev, before)
        elements(near_a, now, base)
        distances(near_b, later)
        collect(sums, prev)
        after = group(base + step)
        sums = products(now, base)
        elements(near_b, later, base + UL)
        distances(near_a, after)
        collect(sums, now)
        return later, after, group(base + step + UL)

    state = group(I32(0))
    distances(near_a, state)
    state = (state, state, group(I32(UL)))
    marks = (0, 7, 14, 20, LOCAL // step)
    for part, (low, high) in enumerate(zip(marks[:-1], marks[1:])):
        state = lax.fori_loop(low, high, body, state)
        emit(part, low * step, (high - low) * step)
    collect(products(state[0], LOCAL - UL), state[0])


LOCAL_SCRATCH = [
    pltpu.VMEM((16, 48, 256), BF16),
    pltpu.VMEM((16, 16, 256), BF16),
    pltpu.VMEM((16, 8, 128), F32),
    pltpu.VMEM((16, 128, 48), BF16),
    pltpu.VMEM((16, 128, 128), F32),
    pltpu.VMEM((16, 128, 128), F32),
    pltpu.VMEM((16, 16, 128), BF16),
    pltpu.VMEM((UL, 128, 256), F32),
    pltpu.VMEM((UL, 128, 256), F32),
    pltpu.VMEM((LOCAL + 3 * UL, 128, 256), BF16),
    pltpu.VMEM((32, 128, 128), F32),
    pltpu.VMEM((32, 8, 128), F32),
    pltpu.VMEM((32, 16, 128), F32),
    pltpu.VMEM((32, 16, 128), F32),
]
LOCAL_OUT = (
    jax.ShapeDtypeStruct((32, 128, 128), F32),
    jax.ShapeDtypeStruct((32, 8, 128), F32),
    jax.ShapeDtypeStruct((32, 16, 128), F32),
    jax.ShapeDtypeStruct((32, 16, 128), F32),
    jax.ShapeDtypeStruct((16, 128, 48), BF16),
    jax.ShapeDtypeStruct((16, 128, 128), F32),
)
NLOCAL = len(LOCAL_OUT)


def local_results(scratch):
    feat_o, s_o = scratch[3], scratch[4]
    return tuple(scratch[10:14]) + (feat_o, s_o)


def compute_kernel(send_ref, pair_ref, edge_ref, table, energy, w_in, roww_in, gg_in, rowg_in, feat_o, s_o,
                   rho_out, acc_out, er_out, t_out, q_rows, q_wide,
                   ta, ts, feat_s, rows_s, lane_s, near_a, near_b, gst, acc_g, acc_w,
                   cnt_v, n_ref, w_pair, cnt_sem, w_sem):
    found = jnp.sum((table[:, 0, :] > 0.0).astype(F32), axis=1, keepdims=True)
    cnt_v[...] = jnp.broadcast_to(found, (NSLOT, 128)).astype(I32)
    fetch = pltpu.make_async_copy(cnt_v, n_ref, cnt_sem)
    fetch.start()
    get_w = pltpu.make_async_copy(w_in.at[pl.ds(0, 16)], acc_w, w_sem.at[0])
    get_p = pltpu.make_async_copy(w_in.at[pl.ds(16, 16)], w_pair, w_sem.at[1])
    get_w.start()
    get_p.start()
    row = row_ids()
    for k in range(16):
        acc_g[k] = gg_in[k]
    for u in range(U):
        gst[u] = jnp.zeros((128, 256), BF16)
    t_out[...] = jnp.zeros_like(t_out)
    fetch.wait()

    def blocks(s):
        return (n_ref[s, 0] + 127) >> 7

    def add(count, a, s):
        ta[count] = a
        ts[count] = s
        return count + (n_ref[s, 0] > 0).astype(I32)
    count = lax.fori_loop(0, 32, lambda s, cnt: add(cnt, jnp.maximum(send_ref[s], 0), s), I32(0))
    count = add(count, edge_ref[0], I32(LOWER))
    count = add(count, edge_ref[1], I32(UPPER))
    ta[count] = ta[0]
    ts[count] = ts[0]
    total = lax.fori_loop(0, count, lambda k, v: v + blocks(OWN + ta[k]) * blocks(ts[k]), I32(0))

    def source_loop(k, _):
        for u in range(2):
            s = ts[2 * k + u]
            store_source(table[s], s * 4, feat_s, rows_s, lane_s)
        return 0
    lax.fori_loop(0, (count + 1) // 2, source_loop, 0)
    get_w.wait()

    def at(tile):
        a, s = ta[tile], ts[tile]
        return a, s, blocks(OWN + a), blocks(s)

    def advance(state):
        tile, ib, jb, a, s, ni, nj = state
        ib = ib + 1
        wrap_i = ib >= ni
        ib = jnp.where(wrap_i, 0, ib)
        jb = jnp.where(wrap_i, jb + 1, jb)
        wrap_j = jb >= nj
        jb = jnp.where(wrap_j, 0, jb)
        tile = jnp.where(wrap_j, jnp.minimum(tile + 1, count), tile)
        return (tile, ib, jb) + at(tile)

    def group(state):
        out = []
        for _ in range(U):
            out.append((state[3] * 4 + state[1], state[4] * 4 + state[2]))
            state = advance(state)
        return state, tuple(out)

    def distances(buf, where):
        for u in range(U):
            buf[u] = nn(feat_o[where[u][0]], feat_s[where[u][1]])

    def elements(buf, where, base):
        for u in range(U):
            oi, si = where[u]
            sj = lane_s[si][0:1]
            mass = lane_s[si][1:2] * (base + u < total).astype(F32)
            d2 = jnp.maximum(buf[u, :, 0:128], 1e-6)
            inv = lax.rsqrt(d2)
            pi = d2 * inv
            pj = pi * buf[u, :, 128:256]
            ai = jnp.maximum(s_o[oi] - pi, 0.0)
            ci = jnp.maximum(ai - pi, 0.0)
            qa = ai * ai
            qc = ci * ci
            acc_w[oi] += ((ai + ai) * qa - qc * ci) * mass
            aj = jnp.maximum(sj - pj, 0.0)
            mj = jnp.minimum(pj, aj)
            split_store(gst, base + U + u, (qa - qc + mj * (aj + aj - mj)) * inv)

    def products(where, base):
        return [nt(rows_s[where[u][1]], gst[base + U + u]) for u in range(U)]

    def collect(sums, where, base):
        for u in range(U):
            acc_g[where[u][0]] += jnp.where(base + u < total, sums[u], 0.0)

    zero = I32(0)
    walk, first = group((zero, zero, zero) + at(zero))
    walk, second = group(walk)
    distances(near_a, first)

    def body(n, carry):
        walk, prev, now, later = carry
        base = n * (2 * U)
        sums = products(prev, base - U)
        elements(near_a, now, base)
        distances(near_b, later)
        collect(sums, prev, base - U)
        walk, after = group(walk)
        sums = products(now, base)
        elements(near_b, later, base + U)
        distances(near_a, after)
        collect(sums, now, base)
        walk, last = group(walk)
        return walk, later, after, last

    steps = (total + 2 * U - 1) // (2 * U)
    lax.fori_loop(0, steps + 1, body, (walk, first, first, second))

    def clear(k, _):
        gst[(2 * steps + 3) * U + k] = jnp.zeros((128, 256), BF16)
        return 0
    lax.fori_loop(0, 17, clear, 0)

    get_p.wait()
    lane_id = lax.broadcasted_iota(I32, (1, 512), 1)
    row_sum = [None] * 4
    flat = [None] * 4
    for a in range(4):
        row_sum[a] = jnp.concatenate([roww_in[a * 4 + b] for b in range(4)], axis=1)
        flat[a] = jnp.concatenate([rowg_in[a * 4 + b] for b in range(4)], axis=1)
    for k in range(4):
        ka, kb = pair_ref[0, k], pair_ref[1, k]
        rw = jnp.concatenate([roww_in[16 + k * 4 + b] for b in range(4)], axis=1)
        rg = jnp.concatenate([rowg_in[16 + k * 4 + b] for b in range(4)], axis=1)
        for a in range(4):
            row_sum[a] = row_sum[a] + jnp.where(kb == a, rw, 0.0)
            flat[a] = flat[a] + jnp.where(kb == a, rg, 0.0)
        for b in range(4):
            acc_g[ka * 4 + b] += gg_in[16 + k * 4 + b]
            acc_w[ka * 4 + b] += w_pair[k * 4 + b]

    for a in range(4):
        st = table[OWN + a]
        h = st[7:8]
        h3 = h * h * h
        ti = ROOT / h3
        sums = jnp.concatenate([acc_g[a * 4 + ib] for ib in range(4)], axis=1)
        sums = (sums[:8] + sums[8:]) * ti + flat[a][:8] + flat[a][8:]
        wsum = jnp.concatenate([jnp.sum(acc_w[a * 4 + ib].T, axis=0, keepdims=True) for ib in range(4)], axis=1)
        wsum = wsum + jnp.sum(row_sum[a], axis=0, keepdims=True)
        rho = wsum * (h3 * (8.0 / math.pi / ROOT ** 3))
        live = lane_id < n_ref[OWN + a, 0]
        press = jnp.where(live, (GAMMA - 1.0) * energy[a:a + 1] / jnp.where(live, rho, 1.0), 0.0)
        rho_out[a:a + 1] = jnp.where(live, rho, 0.0)
        dx = [st[1 + k:2 + k] * sums[0:1] - sums[1 + k:2 + k] for k in range(3)]
        heat = sums[7:8]
        for k in range(3):
            heat = heat + st[4 + k:5 + k] * dx[k] - st[1 + k:2 + k] * sums[4 + k:5 + k]
            acc_out[k, a:a + 1] = jnp.where(live, press * dx[k], 0.0)
        er_out[a:a + 1] = jnp.where(live, -press * heat, 0.0)
        q = jnp.where(row == 0, 1.0, jnp.where(row <= 3, st, 0.0)) * (st[0:1] * press)
        q_rows[a] = pair_rows(q * ti)
        plain = pair_rows(q)
        for jb in range(4):
            cut = slice(jb * 128, (jb + 1) * 128)
            q_wide[a * 4 + jb, :, 0:128] = plain[:, cut]
            q_wide[a * 4 + jb, :, 128:256] = plain[:, cut]

    def mirror(step, base):
        for u in range(2):
            tile = 2 * step + u
            a, s, ni, nj = at(tile)
            q = q_rows[a]
            st = table[s]
            slot = jnp.where(tile < count, s, OWN)
            for jb in range(4):
                cut = slice(jb * 128, (jb + 1) * 128)
                o = fold(nn(q, gst[pl.ds(base + jb * ni, 4)].reshape(512, 256)))
                o = o[:8] + o[8:]
                t_out[slot, :, cut] = (st[:, cut] * o[0:1] - o)[0:4]
            base = base + ni * nj
        return base
    lax.fori_loop(0, (count + 1) // 2, mirror, I32(U))


def compute(send, pairs, edge, table, energy, local):
    smem = pl.BlockSpec(memory_space=pltpu.SMEM)
    vmem = pl.BlockSpec(memory_space=pltpu.VMEM)
    hbm = pl.BlockSpec(memory_space=pl.ANY)
    return pl.pallas_call(
        compute_kernel,
        out_shape=(
            jax.ShapeDtypeStruct((4, 512), F32),
            jax.ShapeDtypeStruct((3, 4, 512), F32),
            jax.ShapeDtypeStruct((4, 512), F32),
            jax.ShapeDtypeStruct((OWN + 1, 4, 512), F32),
            jax.ShapeDtypeStruct((4, 16, 512), BF16),
            jax.ShapeDtypeStruct((16, 16, 256), BF16),
        ),
        in_specs=[smem] * 3 + [vmem] * 2 + [hbm] + [vmem] * 5,
        out_specs=(vmem,) * 6,
        scratch_shapes=[
            pltpu.SMEM((MAXT + 2,), I32),
            pltpu.SMEM((MAXT + 2,), I32),
            pltpu.VMEM((34 * 4, 48, 256), BF16),
            pltpu.VMEM((34 * 4, 16, 256), BF16),
            pltpu.VMEM((34 * 4, 8, 128), F32),
            pltpu.VMEM((U, 128, 256), F32),
            pltpu.VMEM((U, 128, 256), F32),
            pltpu.VMEM((GBLK, 128, 256), BF16),
            pltpu.VMEM((16, 16, 128), F32),
            pltpu.VMEM((16, 128, 128), F32),
            pltpu.VMEM((NSLOT, 128), I32),
            pltpu.SMEM((NSLOT, 128), I32),
            pltpu.VMEM((16, 128, 128), F32),
            pltpu.SemaphoreType.DMA,
            pltpu.SemaphoreType.DMA((2,)),
        ],
        compiler_params=pltpu.CompilerParams(vmem_limit_bytes=62 * MIB),
        name="tiles",
    )(send, pairs, edge, table, energy, *local)


def local_mirror(pair_ref, own, gst, q_rows, q_wide, self_t, pair_t):
    def scale(st):
        return ROOT / (st[7:8] * st[7:8] * st[7:8])

    def settle(st, parts):
        o = jnp.concatenate(parts, axis=1)
        o = o[:8] + o[8:]
        return st * o[0:1] - o

    def one_cell(a, _):
        st = own[a]
        ti = scale(st)
        parts = []
        for jb in range(4):
            first = a * 10 + (jb * (jb + 1)) // 2
            g = gst[pl.ds(first, jb + 1)].reshape((jb + 1) * 128, 256)
            o = fold(nn(q_rows[a, :, 0:(jb + 1) * 128], g))
            for other in range(jb + 1, 4):
                block = gst[a * 10 + (other * (other + 1)) // 2 + jb]
                o = o + nt(q_wide[a * 4 + other], block) * ti[:, jb * 128:(jb + 1) * 128]
            parts.append(o)
        self_t[a] = settle(st, parts)
        return 0
    lax.fori_loop(0, 4, one_cell, 0)

    def one_pair(k, _):
        ka, kb = pair_ref[0, k], pair_ref[1, k]
        first = 40 + k * 16
        there, here = [], []
        q = q_rows[ka]
        wide = [q_wide[kb * 4 + other] for other in range(4)]
        for jb in range(4):
            there.append(fold(nn(q, gst[pl.ds(first + jb * 4, 4)].reshape(512, 256))))
            o = nt(wide[0], gst[first + jb])
            for other in range(1, 4):
                o = o + nt(wide[other], gst[first + other * 4 + jb])
            here.append(o)
        st = own[ka]
        ti = scale(st)
        pair_t[k] = settle(st, [here[jb] * ti[:, jb * 128:(jb + 1) * 128] for jb in range(4)])
        pair_t[4 + k] = settle(own[kb], there)
        return 0
    lax.fori_loop(0, 4, one_pair, 0)


def place():
    region, cell = lax.axis_index("region"), lax.axis_index("cell")
    count = lax.axis_size("region")
    return region, cell, lax.rem(region + count - 1, count), lax.rem(region + 1, count)


def greet():
    region, cell, below, above = place()
    barrier = pltpu.get_barrier_semaphore()

    def one(k, _):
        peer = lax.rem(cell + k, PEERS)
        pl.semaphore_signal(barrier, inc=1, device_id=(region, peer), device_id_type=MESH)
        return 0
    lax.fori_loop(1, PEERS, one, 0)
    pl.semaphore_signal(barrier, inc=1, device_id=(below, cell), device_id_type=MESH)
    pl.semaphore_signal(barrier, inc=1, device_id=(above, cell), device_id_type=MESH)
    return barrier


def remote(src, dst, send_sem, recv_sem, slot, mine, device):
    return pltpu.make_async_remote_copy(
        src_ref=src.at[slot],
        dst_ref=dst.at[mine],
        send_sem=send_sem.at[slot],
        recv_sem=recv_sem.at[mine],
        device_id=device,
        device_id_type=MESH,
    )


def exchange_kernel(counts, send_ref, edge_ref, pair_ref, positions, velocities, mass, smoothing, table, g_out, *refs):
    outs, scratch = refs[:NLOCAL], refs[NLOCAL:-5]
    own, payload, send_sem, recv_sem, local_sem = refs[-5:]
    region, cell, below, above = place()
    barrier = greet()
    lane_id = lax.broadcasted_iota(I32, (1, 512), 1)
    for k in range(4):
        live = lane_id < counts[k]
        own[k] = jnp.concatenate(
            [jnp.where(live, mass[k:k + 1], 0.0)]
            + [positions[i, k:k + 1] - 0.5 for i in range(3)]
            + [velocities[i, k:k + 1] for i in range(3)]
            + [smoothing[k:k + 1]],
            axis=0,
        )
        pltpu.make_async_copy(own.at[k], table.at[OWN + k], local_sem.at[k]).start()
    low = (region > 0).astype(F32)
    high = (region < lax.axis_size("region") - 1).astype(F32)
    payload[LOWER] = own[edge_ref[0]] * low
    payload[UPPER] = own[edge_ref[1]] * high
    payload[cell] = jnp.zeros((8, 512), F32)
    pltpu.make_async_copy(payload.at[cell], table.at[cell], local_sem.at[4]).start()
    local_features(own, *scratch)
    pl.semaphore_wait(barrier, PEERS + 1)
    remote(payload, table, send_sem, recv_sem, LOWER, UPPER, (below, cell)).start()
    remote(payload, table, send_sem, recv_sem, UPPER, LOWER, (above, cell)).start()

    def push(k, _):
        peer = lax.rem(cell + k, PEERS)
        pick = send_ref[peer]
        payload[peer] = jnp.where(pick >= 0, own[jnp.maximum(pick, 0)], 0.0)
        remote(payload, table, send_sem, recv_sem, peer, cell, (region, peer)).start()
        return 0
    lax.fori_loop(1, PEERS, push, 0)

    copies = [
        pltpu.make_async_copy(src, dst, local_sem.at[5 + i])
        for i, (src, dst) in enumerate(zip(local_results(scratch), outs))
    ]
    for copy in copies[4:]:
        copy.start()

    def emit(part, first, size):
        copy = pltpu.make_async_copy(
            scratch[9].at[pl.ds(first, size)], g_out.at[pl.ds(first, size)], local_sem.at[5 + NLOCAL + part]
        )
        copy.start()
        copies.append(copy)

    local_tiles(pair_ref, emit, *scratch)
    for copy in copies[:4]:
        copy.start()
    for k in range(4):
        pltpu.make_async_copy(own.at[k], table.at[OWN + k], local_sem.at[k]).wait()
    pltpu.make_async_copy(payload.at[cell], table.at[cell], local_sem.at[4]).wait()

    def finish(k, _):
        peer = lax.rem(cell + k, PEERS)
        copy = remote(payload, table, send_sem, recv_sem, peer, peer, (region, peer))
        copy.wait_recv()
        copy.wait_send()
        return 0
    lax.fori_loop(1, PEERS, finish, 0)
    for slot, device in ((LOWER, (below, cell)), (UPPER, (above, cell))):
        copy = remote(payload, table, send_sem, recv_sem, slot, slot, device)
        copy.wait_recv()
        copy.wait_send()
    for copy in copies:
        copy.wait()


def exchange(counts, send, edge, pairs, positions, velocities, mass, smoothing):
    smem = pl.BlockSpec(memory_space=pltpu.SMEM)
    vmem = pl.BlockSpec(memory_space=pltpu.VMEM)
    hbm = pl.BlockSpec(memory_space=pl.ANY)
    return pl.pallas_call(
        exchange_kernel,
        out_shape=(
            jax.ShapeDtypeStruct((NSLOT, 8, 512), F32),
            jax.ShapeDtypeStruct((LOCAL, 128, 256), BF16),
        ) + LOCAL_OUT,
        in_specs=[smem] * 4 + [vmem] * 4,
        out_specs=(hbm,) * (2 + NLOCAL),
        scratch_shapes=LOCAL_SCRATCH + [
            pltpu.VMEM((4, 8, 512), F32),
            pltpu.VMEM((34, 8, 512), F32),
            pltpu.SemaphoreType.DMA((34,)),
            pltpu.SemaphoreType.DMA((34,)),
            pltpu.SemaphoreType.DMA((9 + NLOCAL,)),
        ],
        compiler_params=pltpu.CompilerParams(
            collective_id=0, has_side_effects=True, vmem_limit_bytes=60 * MIB
        ),
        name="exchange",
    )(counts, send, edge, pairs, positions, velocities, mass, smoothing)


def return_kernel(counts, send_ref, edge_ref, pair_ref, back, table, g_in, q_rows, q_wide, accel,
                  inbox, total, own, gst, self_t, pair_t, send_sem, recv_sem, local_sem):
    region, cell, below, above = place()
    get_own = pltpu.make_async_copy(table.at[pl.ds(OWN, 4)], own, local_sem.at[0])
    get_g = pltpu.make_async_copy(g_in, gst, local_sem.at[1])
    get_own.start()
    get_g.start()
    barrier = greet()
    pl.semaphore_wait(barrier, PEERS + 1)

    def push(k, _):
        peer = lax.rem(cell + k, PEERS)
        remote(back, inbox, send_sem, recv_sem, peer, cell, (region, peer)).start()
        return 0
    lax.fori_loop(1, PEERS, push, 0)
    remote(back, inbox, send_sem, recv_sem, LOWER, UPPER, (below, cell)).start()
    remote(back, inbox, send_sem, recv_sem, UPPER, LOWER, (above, cell)).start()

    get_own.wait()
    get_g.wait()
    local_mirror(pair_ref, own, gst, q_rows, q_wide, self_t, pair_t)
    for a in range(4):
        t = self_t[a]
        for k in range(4):
            t = t + jnp.where(pair_ref[0, k] == a, pair_t[k], 0.0)
            t = t + jnp.where(pair_ref[1, k] == a, pair_t[4 + k], 0.0)
        total[a] = t[0:4]

    def gather(slot, device, target):
        copy = remote(back, inbox, send_sem, recv_sem, slot, slot, device)
        copy.wait_recv()
        copy.wait_send()
        rows = inbox[slot]
        for a in range(4):
            total[a] += jnp.where(target == a, rows, 0.0)

    def finish(k, _):
        peer = lax.rem(cell + k, PEERS)
        gather(peer, (region, peer), send_ref[peer])
        return 0
    lax.fori_loop(1, PEERS, finish, 0)
    gather(LOWER, (below, cell), edge_ref[0])
    gather(UPPER, (above, cell), edge_ref[1])
    lane_id = lax.broadcasted_iota(I32, (1, 512), 1)
    for a in range(4):
        live = lane_id < counts[a]
        for k in range(3):
            accel[k, a:a + 1] = jnp.where(live, total[a, 1 + k:2 + k], 0.0)


def give_back(counts, send, edge, pairs, back, table, g, q_rows, q_wide):
    smem = pl.BlockSpec(memory_space=pltpu.SMEM)
    vmem = pl.BlockSpec(memory_space=pltpu.VMEM)
    hbm = pl.BlockSpec(memory_space=pl.ANY)
    return pl.pallas_call(
        return_kernel,
        out_shape=jax.ShapeDtypeStruct((3, 4, 512), F32),
        in_specs=[smem] * 4 + [hbm] * 3 + [vmem] * 2,
        out_specs=vmem,
        scratch_shapes=[
            pltpu.VMEM((34, 4, 512), F32),
            pltpu.VMEM((4, 4, 512), F32),
            pltpu.VMEM((4, 8, 512), F32),
            pltpu.VMEM((LOCAL, 128, 256), BF16),
            pltpu.VMEM((4, 8, 512), F32),
            pltpu.VMEM((8, 8, 512), F32),
            pltpu.SemaphoreType.DMA((34,)),
            pltpu.SemaphoreType.DMA((34,)),
            pltpu.SemaphoreType.DMA((2,)),
        ],
        compiler_params=pltpu.CompilerParams(
            collective_id=1, has_side_effects=True, vmem_limit_bytes=60 * MIB
        ),
        name="give_back",
    )(counts, send, edge, pairs, back, table, g, q_rows, q_wide)


def on_device(
    positions, velocities, mass, smoothing, energy, counts, send_cells, local_pairs, edge_cells
):
    send = send_cells.reshape(32)
    edge = edge_cells.reshape(2)
    pairs = local_pairs[0, 0].T
    table, g, *local = exchange(counts, send, edge, pairs, positions, velocities, mass, smoothing)
    density, part, heat, back, q_rows, q_wide = compute(send, pairs, edge, table, energy, local)
    extra = give_back(counts, send, edge, pairs, back, table, g, q_rows, q_wide)
    return density, part + extra, heat


def solution(mesh):
    placed = (
        P(None, ("region", "cell"), None),
        P(None, ("region", "cell"), None),
        P(("region", "cell"), None),
        P(("region", "cell"), None),
        P(("region", "cell"), None),
        P(("region", "cell")),
        P("region", "cell", None, None),
        P("region", "cell", None, None),
        P("region", "cell", None),
    )
    return jax.shard_map(
        on_device,
        mesh=mesh,
        in_specs=placed,
        out_specs=(
            P(("region", "cell"), None),
            P(None, ("region", "cell"), None),
            P(("region", "cell"), None),
        ),
        check_vma=False,
    )
```

```python
import functools
import math
import jax
import jax.numpy as jnp
from jax import lax
from jax.experimental import pallas as pl
from jax.experimental.pallas import tpu as pltpu
from jax.sharding import PartitionSpec as P

GAMMA = 5.0 / 3.0
F32, BF16, I32 = jnp.float32, jnp.bfloat16, jnp.int32
U = 3
UL = 4
PEERS = 32
LOWER, UPPER, OWN, NSLOT = 32, 33, 34, 38
MAXT = 34
LOCAL = 104
GBLK = MAXT * 16 + 20 + 6 * U
ROOT = math.sqrt(24.0 / math.pi)
MIB = 1024 * 1024
MESH = pl.DeviceIdType.MESH


def halves(v):
    hi = v.astype(BF16).astype(F32)
    return hi, v - hi


def thirds(v):
    first, rest = halves(v)
    second, third = halves(rest)
    return first, second, third


def nt(a, b):
    return lax.dot_general(a, b, (((1,), (1,)), ((), ())), preferred_element_type=F32)


def nn(a, b):
    return lax.dot_general(a, b, (((1,), (0,)), ((), ())), preferred_element_type=F32)


def row_ids():
    return lax.broadcasted_iota(I32, (8, 512), 0)


def square(st):
    x = st[1:2]
    y = st[2:3]
    z = st[3:4]
    return x * x + y * y + z * z


def moments(st):
    row = row_ids()
    vx = st[1:2] * st[4:5] + st[2:3] * st[5:6] + st[3:4] * st[6:7]
    return jnp.where(row == 0, 1.0, jnp.where(row == 7, vx, st)) * st[0:1]


def pair_rows(v):
    first, second = halves(v)
    return jnp.concatenate([first, second], axis=0).astype(BF16)


def store_source(st, base, feat_s, rows_s, lane_s):
    row = row_ids()
    hinv = 1.0 / st[7:8]
    sj = ROOT * hinv * hinv
    f = jnp.where(row == 0, square(st), jnp.where(row <= 3, st, jnp.where(row == 4, 1.0, 0.0)))
    f1, f2, f3 = thirds(f)
    t1, t2, t3 = thirds(sj * hinv)
    t1 = jnp.where(row == 5, t1, 0.0)
    t2 = jnp.where(row == 5, t2, 0.0)
    t3 = jnp.where(row == 5, t3, 0.0)
    near = jnp.concatenate([f1, f1, f2, f2, f1, f3], axis=0).astype(BF16)
    ratio = jnp.concatenate([t1, t1, t2, t2, t1, t3], axis=0).astype(BF16)
    rows = pair_rows(moments(st))
    lane = jnp.where(row == 0, sj, st[0:1])
    for jb in range(4):
        cut = slice(jb * 128, (jb + 1) * 128)
        feat_s[base + jb, :, 0:128] = near[:, cut]
        feat_s[base + jb, :, 128:256] = ratio[:, cut]
        rows_s[base + jb, :, 0:128] = rows[:, cut]
        rows_s[base + jb, :, 128:256] = rows[:, cut]
        lane_s[base + jb] = lane[:, cut]


def store_target(st, base, feat_o, s_o, m_o, rows_o):
    row = row_ids()
    h = st[7:8]
    hinv = 1.0 / h
    si = ROOT * hinv * hinv
    ti = si * hinv
    f = jnp.where(row == 0, 1.0, jnp.where(row <= 3, -2.0 * st, jnp.where(row == 4, square(st), 0.0)))
    f = jnp.where(row == 5, h * h * h * (1.0 / ROOT), f * (ti * ti))
    f1, f2, f3 = thirds(f)
    s1, s2, s3 = thirds(si)
    m1, m2, m3 = thirds(st[0:1])
    extra = jnp.where(row == 0, s1, jnp.where(row == 1, s2, jnp.where(row == 2, s3, 0.0)))
    extra = jnp.where(row == 3, m1, jnp.where(row == 4, m2, jnp.where(row == 5, m3, extra)))
    whole = jnp.concatenate([f1, f2, f1, f2, f3, f1, extra, jnp.zeros((8, 512), F32)], axis=0).astype(BF16)
    rows = pair_rows(moments(st) * ti)
    size = (128, 128)
    eye = (lax.broadcasted_iota(I32, size, 0) == lax.broadcasted_iota(I32, size, 1)).astype(F32).astype(BF16)
    at = lax.broadcasted_iota(I32, (64, 256), 0)
    side = lax.broadcasted_iota(I32, (64, 256), 1) >= 128
    lowest = jnp.where(side, 51, 48)
    pick = ((at >= lowest) & (at < lowest + 3)).astype(F32).astype(BF16)
    for ib in range(4):
        cut = slice(ib * 128, (ib + 1) * 128)
        part = nt(eye, whole[:, cut]).astype(BF16)
        feat_o[base + ib] = part[:, :48]
        wide = nn(part, pick)
        s_o[base + ib] = wide[:, :128]
        m_o[base + ib] = wide[:, 128:]
        rows_o[base + ib] = rows[:, cut]


def split_store(gst, at, g):
    hi = g.astype(BF16)
    gst[at, :, 0:128] = hi
    gst[at, :, 128:256] = (g - hi.astype(F32)).astype(BF16)


def fold(v):
    return v[:, :128] + v[:, 128:]


def local_features(own, feat_s, rows_s, lane_s, feat_o, s_o, m_o, rows_o, *_):
    for a in range(4):
        store_source(own[a], a * 4, feat_s, rows_s, lane_s)
        store_target(own[a], a * 4, feat_o, s_o, m_o, rows_o)


def local_tiles(pair_ref, emit, feat_s, rows_s, lane_s, feat_o, s_o, m_o, rows_o, near_a, near_b,
                gst, acc_w, row_w, acc_g, row_g):
    acc_w[...] = jnp.zeros_like(acc_w)
    row_w[...] = jnp.zeros_like(row_w)
    acc_g[...] = jnp.zeros_like(acc_g)
    row_g[...] = jnp.zeros_like(row_g)
    for u in range(UL):
        gst[LOCAL + 2 * UL + u] = jnp.zeros((128, 256), BF16)

    def where(n):
        n = jnp.minimum(n, LOCAL - 1)
        t = lax.rem(n, 10)
        j1 = (t >= 1).astype(I32) + (t >= 3).astype(I32) + (t >= 6).astype(I32)
        i1 = t - (j1 * (j1 + 1)) // 2
        m = jnp.maximum(n - 40, 0)
        k = m // 16
        self_ = n < 40
        ib = jnp.where(self_, i1, lax.rem(m, 4))
        jb = jnp.where(self_, j1, lax.rem(m // 4, 4))
        a = jnp.where(self_, n // 10, pair_ref[0, k])
        b = jnp.where(self_, n // 10, pair_ref[1, k])
        group = jnp.where(self_, n // 10, 4 + k)
        both = jnp.where(self_ & (i1 == j1), 0.0, 1.0)
        return a * 4 + ib, b * 4 + jb, group * 4 + ib, group * 4 + jb, both

    def group(n):
        return tuple(where(n + u) for u in range(UL))

    def distances(buf, those):
        for u in range(UL):
            buf[u] = nn(feat_o[those[u][0]], feat_s[those[u][1]])

    def elements(buf, those, n):
        for u in range(UL):
            oi, si, gi, gj, both = those[u]
            sj = lane_s[si][0:1]
            mass = lane_s[si][1:2]
            d2 = jnp.maximum(buf[u, :, 0:128], 1e-6)
            inv = lax.rsqrt(d2)
            pi = d2 * inv
            pj = pi * buf[u, :, 128:256]
            ai = jnp.maximum(s_o[oi] - pi, 0.0)
            ci = jnp.maximum(ai - pi, 0.0)
            aj = jnp.maximum(sj - pj, 0.0)
            cj = jnp.maximum(aj - pj, 0.0)
            qa = ai * ai
            qc = ci * ci
            ra = aj * aj
            rc = cj * cj
            acc_w[gi] += ((ai + ai) * qa - qc * ci) * mass
            back = ((aj + aj) * ra - rc * cj) * m_o[oi]
            row_w[gj] += both * jnp.sum(back.reshape(16, 8, 128), axis=0)
            split_store(gst, n + u, (qa - qc + ra - rc) * inv)

    def products(those, slot):
        out = []
        for u in range(UL):
            g = gst[slot + u]
            out.append((nt(rows_s[those[u][1]], g), fold(nn(rows_o[those[u][0]], g))))
        return out

    def collect(sums, those):
        for u in range(UL):
            _, _, gi, gj, both = those[u]
            acc_g[gi] += sums[u][0]
            row_g[gj] += sums[u][1] * both

    step = 2 * UL

    def body(n, carry):
        prev, now, later = carry
        base = n * step
        before = jnp.where(n == 0, LOCAL + 2 * UL, base - UL)
        sums = products(prev, before)
        elements(near_a, now, base)
        distances(near_b, later)
        collect(sums, prev)
        after = group(base + step)
        sums = products(now, base)
        elements(near_b, later, base + UL)
        distances(near_a, after)
        collect(sums, now)
        for part, (_, last, _, _) in enumerate(PARTS):
            pl.when(n == last // step - 1)(functools.partial(emit, part))
        return later, after, group(base + step + UL)

    state = group(I32(0))
    distances(near_a, state)
    state = (state, state, group(I32(UL)))
    state = lax.fori_loop(0, LOCAL // step, body, state)
    collect(products(state[0], LOCAL - UL), state[0])


LOCAL_SCRATCH = [
    pltpu.VMEM((16, 48, 256), BF16),
    pltpu.VMEM((16, 16, 256), BF16),
    pltpu.VMEM((16, 8, 128), F32),
    pltpu.VMEM((16, 128, 48), BF16),
    pltpu.VMEM((16, 128, 128), F32),
    pltpu.VMEM((16, 128, 128), F32),
    pltpu.VMEM((16, 16, 128), BF16),
    pltpu.VMEM((UL, 128, 256), F32),
    pltpu.VMEM((UL, 128, 256), F32),
    pltpu.VMEM((LOCAL + 3 * UL, 128, 256), BF16),
    pltpu.VMEM((32, 128, 128), F32),
    pltpu.VMEM((32, 8, 128), F32),
    pltpu.VMEM((32, 16, 128), F32),
    pltpu.VMEM((32, 16, 128), F32),
]
LOCAL_OUT = (
    jax.ShapeDtypeStruct((32, 128, 128), F32),
    jax.ShapeDtypeStruct((32, 8, 128), F32),
    jax.ShapeDtypeStruct((32, 16, 128), F32),
    jax.ShapeDtypeStruct((32, 16, 128), F32),
    jax.ShapeDtypeStruct((16, 128, 48), BF16),
    jax.ShapeDtypeStruct((16, 128, 128), F32),
)
NLOCAL = len(LOCAL_OUT)


def local_results(scratch):
    feat_o, s_o = scratch[3], scratch[4]
    return tuple(scratch[10:14]) + (feat_o, s_o)


PARTS = ((0, 40, 0, 16),) + tuple((40 + 16 * k, 56 + 16 * k, 16 + 4 * k, 4) for k in range(4))


def compute_kernel(send_ref, pair_ref, edge_ref, table, energy_in, w_in, roww_h, gg_h, rowg_h, feat_h, s_h,
                   rho_out, acc_out, er_out, t_out, q_rows, q_wide,
                   ta, ts, feat_s, rows_s, lane_s, near_a, near_b, gst, acc_g, acc_w,
                   cnt_v, n_ref, w_pair, energy, roww_in, gg_in, rowg_in, feat_o, s_o, cnt_sem, w_sem, in_sem):
    moves = [
        pltpu.make_async_copy(src, dst, in_sem.at[i])
        for i, (src, dst) in enumerate(
            ((feat_h, feat_o), (s_h, s_o), (gg_h, gg_in), (energy_in, energy), (roww_h, roww_in), (rowg_h, rowg_in))
        )
    ]
    found = jnp.sum((table[:, 0, :] > 0.0).astype(F32), axis=1, keepdims=True)
    cnt_v[...] = jnp.broadcast_to(found, (NSLOT, 128)).astype(I32)
    fetch = pltpu.make_async_copy(cnt_v, n_ref, cnt_sem)
    fetch.start()
    get_w = pltpu.make_async_copy(w_in.at[pl.ds(0, 16)], acc_w, w_sem.at[0])
    get_p = pltpu.make_async_copy(w_in.at[pl.ds(16, 16)], w_pair, w_sem.at[1])
    get_w.start()
    for move in moves[:3]:
        move.start()
    get_p.start()
    for move in moves[3:]:
        move.start()
    row = row_ids()
    acc_g[...] = jnp.zeros_like(acc_g)
    for u in range(U):
        gst[u] = jnp.zeros((128, 256), BF16)
    t_out[...] = jnp.zeros_like(t_out)
    fetch.wait()

    def blocks(s):
        return (n_ref[s, 0] + 127) >> 7

    def add(count, a, s):
        ta[count] = a
        ts[count] = s
        return count + (n_ref[s, 0] > 0).astype(I32)
    count = lax.fori_loop(0, 32, lambda s, cnt: add(cnt, jnp.maximum(send_ref[s], 0), s), I32(0))
    count = add(count, edge_ref[0], I32(LOWER))
    count = add(count, edge_ref[1], I32(UPPER))
    ta[count] = ta[0]
    ts[count] = ts[0]
    total = lax.fori_loop(0, count, lambda k, v: v + blocks(OWN + ta[k]) * blocks(ts[k]), I32(0))

    def source_loop(k, _):
        for u in range(2):
            s = ts[2 * k + u]
            store_source(table[s], s * 4, feat_s, rows_s, lane_s)
        return 0
    lax.fori_loop(0, (count + 1) // 2, source_loop, 0)
    get_w.wait()
    for move in moves[:2]:
        move.wait()

    def at(tile):
        a, s = ta[tile], ts[tile]
        return a, s, blocks(OWN + a), blocks(s)

    def advance(state):
        tile, ib, jb, a, s, ni, nj = state
        ib = ib + 1
        wrap_i = ib >= ni
        ib = jnp.where(wrap_i, 0, ib)
        jb = jnp.where(wrap_i, jb + 1, jb)
        wrap_j = jb >= nj
        jb = jnp.where(wrap_j, 0, jb)
        tile = jnp.where(wrap_j, jnp.minimum(tile + 1, count), tile)
        return (tile, ib, jb) + at(tile)

    def group(state):
        out = []
        for _ in range(U):
            out.append((state[3] * 4 + state[1], state[4] * 4 + state[2]))
            state = advance(state)
        return state, tuple(out)

    def distances(buf, where):
        for u in range(U):
            buf[u] = nn(feat_o[where[u][0]], feat_s[where[u][1]])

    def elements(buf, where, base):
        for u in range(U):
            oi, si = where[u]
            sj = lane_s[si][0:1]
            mass = lane_s[si][1:2] * (base + u < total).astype(F32)
            d2 = jnp.maximum(buf[u, :, 0:128], 1e-6)
            inv = lax.rsqrt(d2)
            pi = d2 * inv
            pj = pi * buf[u, :, 128:256]
            ai = jnp.maximum(s_o[oi] - pi, 0.0)
            ci = jnp.maximum(ai - pi, 0.0)
            qa = ai * ai
            qc = ci * ci
            acc_w[oi] += ((ai + ai) * qa - qc * ci) * mass
            aj = jnp.maximum(sj - pj, 0.0)
            mj = jnp.minimum(pj, aj)
            split_store(gst, base + U + u, (qa - qc + mj * (aj + aj - mj)) * inv)

    def products(where, base):
        return [nt(rows_s[where[u][1]], gst[base + U + u]) for u in range(U)]

    def collect(sums, where, base):
        for u in range(U):
            acc_g[where[u][0]] += jnp.where(base + u < total, sums[u], 0.0)

    zero = I32(0)
    walk, first = group((zero, zero, zero) + at(zero))
    walk, second = group(walk)
    distances(near_a, first)

    def body(n, carry):
        walk, prev, now, later = carry
        base = n * (2 * U)
        sums = products(prev, base - U)
        elements(near_a, now, base)
        distances(near_b, later)
        collect(sums, prev, base - U)
        walk, after = group(walk)
        sums = products(now, base)
        elements(near_b, later, base + U)
        distances(near_a, after)
        collect(sums, now, base)
        walk, last = group(walk)
        return walk, later, after, last

    steps = (total + 2 * U - 1) // (2 * U)
    lax.fori_loop(0, steps + 1, body, (walk, first, first, second))

    def clear(k, _):
        gst[(2 * steps + 3) * U + k] = jnp.zeros((128, 256), BF16)
        return 0
    lax.fori_loop(0, 17, clear, 0)

    get_p.wait()
    for move in moves[2:]:
        move.wait()
    for k in range(16):
        acc_g[k] += gg_in[k]
    lane_id = lax.broadcasted_iota(I32, (1, 512), 1)
    row_sum = [None] * 4
    flat = [None] * 4
    for a in range(4):
        row_sum[a] = jnp.concatenate([roww_in[a * 4 + b] for b in range(4)], axis=1)
        flat[a] = jnp.concatenate([rowg_in[a * 4 + b] for b in range(4)], axis=1)
    for k in range(4):
        ka, kb = pair_ref[0, k], pair_ref[1, k]
        rw = jnp.concatenate([roww_in[16 + k * 4 + b] for b in range(4)], axis=1)
        rg = jnp.concatenate([rowg_in[16 + k * 4 + b] for b in range(4)], axis=1)
        for a in range(4):
            row_sum[a] = row_sum[a] + jnp.where(kb == a, rw, 0.0)
            flat[a] = flat[a] + jnp.where(kb == a, rg, 0.0)
        for b in range(4):
            acc_g[ka * 4 + b] += gg_in[16 + k * 4 + b]
            acc_w[ka * 4 + b] += w_pair[k * 4 + b]

    for a in range(4):
        st = table[OWN + a]
        h = st[7:8]
        h3 = h * h * h
        ti = ROOT / h3
        sums = jnp.concatenate([acc_g[a * 4 + ib] for ib in range(4)], axis=1)
        sums = (sums[:8] + sums[8:]) * ti + flat[a][:8] + flat[a][8:]
        wsum = jnp.concatenate([jnp.sum(acc_w[a * 4 + ib].T, axis=0, keepdims=True) for ib in range(4)], axis=1)
        wsum = wsum + jnp.sum(row_sum[a], axis=0, keepdims=True)
        rho = wsum * (h3 * (8.0 / math.pi / ROOT ** 3))
        live = lane_id < n_ref[OWN + a, 0]
        press = jnp.where(live, (GAMMA - 1.0) * energy[a:a + 1] / jnp.where(live, rho, 1.0), 0.0)
        rho_out[a:a + 1] = jnp.where(live, rho, 0.0)
        dx = [st[1 + k:2 + k] * sums[0:1] - sums[1 + k:2 + k] for k in range(3)]
        heat = sums[7:8]
        for k in range(3):
            heat = heat + st[4 + k:5 + k] * dx[k] - st[1 + k:2 + k] * sums[4 + k:5 + k]
            acc_out[k, a:a + 1] = jnp.where(live, press * dx[k], 0.0)
        er_out[a:a + 1] = jnp.where(live, -press * heat, 0.0)
        q = jnp.where(row == 0, 1.0, jnp.where(row <= 3, st, 0.0)) * (st[0:1] * press)
        q_rows[a] = pair_rows(q * ti)
        plain = pair_rows(q)
        for jb in range(4):
            cut = slice(jb * 128, (jb + 1) * 128)
            q_wide[a * 4 + jb, :, 0:128] = plain[:, cut]
            q_wide[a * 4 + jb, :, 128:256] = plain[:, cut]

    def mirror(step, base):
        for u in range(2):
            tile = 2 * step + u
            a, s, ni, nj = at(tile)
            q = q_rows[a]
            st = table[s]
            slot = jnp.where(tile < count, s, OWN)
            for jb in range(4):
                cut = slice(jb * 128, (jb + 1) * 128)
                o = fold(nn(q, gst[pl.ds(base + jb * ni, 4)].reshape(512, 256)))
                o = o[:8] + o[8:]
                t_out[slot, :, cut] = (st[:, cut] * o[0:1] - o)[0:4]
            base = base + ni * nj
        return base
    lax.fori_loop(0, (count + 1) // 2, mirror, I32(U))


def compute(send, pairs, edge, table, energy, local):
    smem = pl.BlockSpec(memory_space=pltpu.SMEM)
    vmem = pl.BlockSpec(memory_space=pltpu.VMEM)
    hbm = pl.BlockSpec(memory_space=pl.ANY)
    return pl.pallas_call(
        compute_kernel,
        out_shape=(
            jax.ShapeDtypeStruct((4, 512), F32),
            jax.ShapeDtypeStruct((3, 4, 512), F32),
            jax.ShapeDtypeStruct((4, 512), F32),
            jax.ShapeDtypeStruct((OWN + 1, 4, 512), F32),
            jax.ShapeDtypeStruct((4, 16, 512), BF16),
            jax.ShapeDtypeStruct((16, 16, 256), BF16),
        ),
        in_specs=[smem] * 3 + [vmem] + [hbm] * 7,
        out_specs=(vmem,) * 6,
        scratch_shapes=[
            pltpu.SMEM((MAXT + 2,), I32),
            pltpu.SMEM((MAXT + 2,), I32),
            pltpu.VMEM((34 * 4, 48, 256), BF16),
            pltpu.VMEM((34 * 4, 16, 256), BF16),
            pltpu.VMEM((34 * 4, 8, 128), F32),
            pltpu.VMEM((U, 128, 256), F32),
            pltpu.VMEM((U, 128, 256), F32),
            pltpu.VMEM((GBLK, 128, 256), BF16),
            pltpu.VMEM((16, 16, 128), F32),
            pltpu.VMEM((16, 128, 128), F32),
            pltpu.VMEM((NSLOT, 128), I32),
            pltpu.SMEM((NSLOT, 128), I32),
            pltpu.VMEM((16, 128, 128), F32),
            pltpu.VMEM((4, 512), F32),
            pltpu.VMEM((32, 8, 128), F32),
            pltpu.VMEM((32, 16, 128), F32),
            pltpu.VMEM((32, 16, 128), F32),
            pltpu.VMEM((16, 128, 48), BF16),
            pltpu.VMEM((16, 128, 128), F32),
            pltpu.SemaphoreType.DMA,
            pltpu.SemaphoreType.DMA((2,)),
            pltpu.SemaphoreType.DMA((6,)),
        ],
        compiler_params=pltpu.CompilerParams(vmem_limit_bytes=62 * MIB),
        name="tiles",
    )(send, pairs, edge, table, energy, *local)


def local_mirror(pair_ref, own, gst, q_rows, q_wide, self_t, pair_t):
    def scale(st):
        return ROOT / (st[7:8] * st[7:8] * st[7:8])

    def settle(st, parts):
        o = jnp.concatenate(parts, axis=1)
        o = o[:8] + o[8:]
        return st * o[0:1] - o

    def one_cell(a, _):
        st = own[a]
        ti = scale(st)
        parts = []
        for jb in range(4):
            first = a * 10 + (jb * (jb + 1)) // 2
            g = gst[pl.ds(first, jb + 1)].reshape((jb + 1) * 128, 256)
            o = fold(nn(q_rows[a, :, 0:(jb + 1) * 128], g))
            for other in range(jb + 1, 4):
                block = gst[a * 10 + (other * (other + 1)) // 2 + jb]
                o = o + nt(q_wide[a * 4 + other], block) * ti[:, jb * 128:(jb + 1) * 128]
            parts.append(o)
        self_t[a] = settle(st, parts)
        return 0
    lax.fori_loop(0, 4, one_cell, 0)

    def one_pair(k, _):
        ka, kb = pair_ref[0, k], pair_ref[1, k]
        first = 40 + k * 16
        there, here = [], []
        q = q_rows[ka]
        wide = [q_wide[kb * 4 + other] for other in range(4)]
        for jb in range(4):
            there.append(fold(nn(q, gst[pl.ds(first + jb * 4, 4)].reshape(512, 256))))
            o = nt(wide[0], gst[first + jb])
            for other in range(1, 4):
                o = o + nt(wide[other], gst[first + other * 4 + jb])
            here.append(o)
        st = own[ka]
        ti = scale(st)
        pair_t[k] = settle(st, [here[jb] * ti[:, jb * 128:(jb + 1) * 128] for jb in range(4)])
        pair_t[4 + k] = settle(own[kb], there)
        return 0
    lax.fori_loop(0, 4, one_pair, 0)


def place():
    region, cell = lax.axis_index("region"), lax.axis_index("cell")
    count = lax.axis_size("region")
    return region, cell, lax.rem(region + count - 1, count), lax.rem(region + 1, count)


def greet():
    region, cell, below, above = place()
    barrier = pltpu.get_barrier_semaphore()

    def one(k, _):
        peer = lax.rem(cell + k, PEERS)
        pl.semaphore_signal(barrier, inc=1, device_id=(region, peer), device_id_type=MESH)
        return 0
    lax.fori_loop(1, PEERS, one, 0)
    pl.semaphore_signal(barrier, inc=1, device_id=(below, cell), device_id_type=MESH)
    pl.semaphore_signal(barrier, inc=1, device_id=(above, cell), device_id_type=MESH)
    return barrier


def remote(src, dst, send_sem, recv_sem, slot, mine, device):
    return pltpu.make_async_remote_copy(
        src_ref=src.at[slot],
        dst_ref=dst.at[mine],
        send_sem=send_sem.at[slot],
        recv_sem=recv_sem.at[mine],
        device_id=device,
        device_id_type=MESH,
    )


def exchange_kernel(*refs):
    arrived, table, g_out = refs[:8], refs[8], refs[9]
    outs, scratch = refs[10:10 + NLOCAL], refs[10 + NLOCAL:-14]
    own, payload = refs[-14:-12]
    held, send_sem, recv_sem, local_sem, in_sem = refs[-12:-4], refs[-4], refs[-3], refs[-2], refs[-1]
    moves = [pltpu.make_async_copy(src, dst, in_sem.at[i]) for i, (src, dst) in enumerate(zip(arrived, held))]
    for move in moves:
        move.start()
    region, cell, below, above = place()
    barrier = greet()
    for move in moves:
        move.wait()
    counts, send_ref, edge_ref, pair_ref, positions, velocities, mass, smoothing = held
    lane_id = lax.broadcasted_iota(I32, (1, 512), 1)
    for k in range(4):
        live = lane_id < counts[k]
        own[k] = jnp.concatenate(
            [jnp.where(live, mass[k:k + 1], 0.0)]
            + [positions[i, k:k + 1] - 0.5 for i in range(3)]
            + [velocities[i, k:k + 1] for i in range(3)]
            + [smoothing[k:k + 1]],
            axis=0,
        )
        pltpu.make_async_copy(own.at[k], table.at[OWN + k], local_sem.at[k]).start()
    low = (region > 0).astype(F32)
    high = (region < lax.axis_size("region") - 1).astype(F32)
    payload[LOWER] = own[edge_ref[0]] * low
    payload[UPPER] = own[edge_ref[1]] * high
    payload[cell] = jnp.zeros((8, 512), F32)
    pltpu.make_async_copy(payload.at[cell], table.at[cell], local_sem.at[4]).start()
    local_features(own, *scratch)
    pl.semaphore_wait(barrier, PEERS + 1)
    remote(payload, table, send_sem, recv_sem, LOWER, UPPER, (below, cell)).start()
    remote(payload, table, send_sem, recv_sem, UPPER, LOWER, (above, cell)).start()

    def push(k, _):
        peer = lax.rem(cell + k, PEERS)
        pick = send_ref[peer]
        payload[peer] = jnp.where(pick >= 0, own[jnp.maximum(pick, 0)], 0.0)
        remote(payload, table, send_sem, recv_sem, peer, cell, (region, peer)).start()
        return 0
    lax.fori_loop(1, PEERS, push, 0)

    acc_w, row_w, acc_g, row_g, feat_o, s_o = local_results(scratch)
    first = [
        pltpu.make_async_copy(feat_o, outs[4], local_sem.at[5]),
        pltpu.make_async_copy(s_o, outs[5], local_sem.at[6]),
    ]
    rest = [
        pltpu.make_async_copy(src, dst, local_sem.at[7 + i])
        for i, (src, dst) in enumerate(((row_w, outs[1]), (acc_g, outs[2]), (row_g, outs[3])))
    ]
    for copy in first:
        copy.start()

    def part_copies(part):
        low, high, group, size = PARTS[part]
        blocks, groups = pl.ds(low, high - low), pl.ds(group, size)
        return (
            pltpu.make_async_copy(scratch[9].at[blocks], g_out.at[blocks], local_sem.at[10 + 2 * part]),
            pltpu.make_async_copy(acc_w.at[groups], outs[0].at[groups], local_sem.at[11 + 2 * part]),
        )

    def emit(part):
        for copy in part_copies(part):
            copy.start()

    local_tiles(pair_ref, emit, *scratch)
    for copy in rest:
        copy.start()
    for k in range(4):
        pltpu.make_async_copy(own.at[k], table.at[OWN + k], local_sem.at[k]).wait()
    pltpu.make_async_copy(payload.at[cell], table.at[cell], local_sem.at[4]).wait()

    def finish(k, _):
        peer = lax.rem(cell + k, PEERS)
        copy = remote(payload, table, send_sem, recv_sem, peer, peer, (region, peer))
        copy.wait_recv()
        copy.wait_send()
        return 0
    lax.fori_loop(1, PEERS, finish, 0)
    for slot, device in ((LOWER, (below, cell)), (UPPER, (above, cell))):
        copy = remote(payload, table, send_sem, recv_sem, slot, slot, device)
        copy.wait_recv()
        copy.wait_send()
    for copy in first + rest:
        copy.wait()
    for part in range(len(PARTS)):
        for copy in part_copies(part):
            copy.wait()


def exchange(counts, send, edge, pairs, positions, velocities, mass, smoothing):
    hbm = pl.BlockSpec(memory_space=pl.ANY)
    return pl.pallas_call(
        exchange_kernel,
        out_shape=(
            jax.ShapeDtypeStruct((NSLOT, 8, 512), F32),
            jax.ShapeDtypeStruct((LOCAL, 128, 256), BF16),
        ) + LOCAL_OUT,
        in_specs=[hbm] * 8,
        out_specs=(hbm,) * (2 + NLOCAL),
        scratch_shapes=LOCAL_SCRATCH + [
            pltpu.VMEM((4, 8, 512), F32),
            pltpu.VMEM((34, 8, 512), F32),
            pltpu.SMEM((4,), I32),
            pltpu.SMEM((32,), I32),
            pltpu.SMEM((2,), I32),
            pltpu.SMEM((2, 4), I32),
            pltpu.VMEM((3, 4, 512), F32),
            pltpu.VMEM((3, 4, 512), F32),
            pltpu.VMEM((4, 512), F32),
            pltpu.VMEM((4, 512), F32),
            pltpu.SemaphoreType.DMA((34,)),
            pltpu.SemaphoreType.DMA((34,)),
            pltpu.SemaphoreType.DMA((20,)),
            pltpu.SemaphoreType.DMA((8,)),
        ],
        compiler_params=pltpu.CompilerParams(
            collective_id=0, has_side_effects=True, vmem_limit_bytes=60 * MIB
        ),
        name="exchange",
    )(counts, send, edge, pairs, positions, velocities, mass, smoothing)


def return_kernel(counts_h, send_h, edge_h, pair_h, back, table, g_in, q_in, wide_in, accel,
                  inbox, own, gst, self_t, pair_t, counts, send_ref, edge_ref, pair_ref, q_rows, q_wide,
                  send_sem, recv_sem, local_sem):
    moves = [
        pltpu.make_async_copy(src, dst, local_sem.at[i])
        for i, (src, dst) in enumerate((
            (table.at[pl.ds(OWN, 4)], own), (g_in, gst), (q_in, q_rows), (wide_in, q_wide),
            (counts_h, counts), (send_h, send_ref), (edge_h, edge_ref), (pair_h, pair_ref),
        ))
    ]
    region, cell, below, above = place()
    barrier = greet()
    for move in moves:
        move.start()
    inbox[cell] = jnp.zeros((4, 512), F32)
    pl.semaphore_wait(barrier, PEERS + 1)

    def push(k, _):
        peer = lax.rem(cell + k, PEERS)
        remote(back, inbox, send_sem, recv_sem, peer, cell, (region, peer)).start()
        return 0
    lax.fori_loop(1, PEERS, push, 0)
    remote(back, inbox, send_sem, recv_sem, LOWER, UPPER, (below, cell)).start()
    remote(back, inbox, send_sem, recv_sem, UPPER, LOWER, (above, cell)).start()

    for move in moves:
        move.wait()
    local_mirror(pair_ref, own, gst, q_rows, q_wide, self_t, pair_t)

    def arrived(k, _):
        peer = lax.rem(cell + k, PEERS)
        remote(back, inbox, send_sem, recv_sem, peer, peer, (region, peer)).wait_recv()
        return 0
    lax.fori_loop(1, PEERS, arrived, 0)
    edges = [
        remote(back, inbox, send_sem, recv_sem, slot, slot, device)
        for slot, device in ((LOWER, (below, cell)), (UPPER, (above, cell)))
    ]
    for copy in edges:
        copy.wait_recv()
    total = []
    for a in range(4):
        t = self_t[a]
        for k in range(4):
            t = t + jnp.where(pair_ref[0, k] == a, pair_t[k], 0.0)
            t = t + jnp.where(pair_ref[1, k] == a, pair_t[4 + k], 0.0)
        total.append(t[0:4])
    for slot in range(34):
        target = send_ref[slot] if slot < PEERS else edge_ref[slot - PEERS]
        rows = inbox[slot]
        for a in range(4):
            total[a] = total[a] + jnp.where(target == a, rows, 0.0)
    lane_id = lax.broadcasted_iota(I32, (1, 512), 1)
    for a in range(4):
        live = lane_id < counts[a]
        for k in range(3):
            accel[k, a:a + 1] = jnp.where(live, total[a][1 + k:2 + k], 0.0)

    def left(k, _):
        peer = lax.rem(cell + k, PEERS)
        remote(back, inbox, send_sem, recv_sem, peer, peer, (region, peer)).wait_send()
        return 0
    lax.fori_loop(1, PEERS, left, 0)
    for copy in edges:
        copy.wait_send()


def give_back(counts, send, edge, pairs, back, table, g, q_rows, q_wide):
    hbm = pl.BlockSpec(memory_space=pl.ANY)
    return pl.pallas_call(
        return_kernel,
        out_shape=jax.ShapeDtypeStruct((3, 4, 512), F32),
        in_specs=[hbm] * 9,
        out_specs=pl.BlockSpec(memory_space=pltpu.VMEM),
        scratch_shapes=[
            pltpu.VMEM((34, 4, 512), F32),
            pltpu.VMEM((4, 8, 512), F32),
            pltpu.VMEM((LOCAL, 128, 256), BF16),
            pltpu.VMEM((4, 8, 512), F32),
            pltpu.VMEM((8, 8, 512), F32),
            pltpu.SMEM((4,), I32),
            pltpu.SMEM((32,), I32),
            pltpu.SMEM((2,), I32),
            pltpu.SMEM((2, 4), I32),
            pltpu.VMEM((4, 16, 512), BF16),
            pltpu.VMEM((16, 16, 256), BF16),
            pltpu.SemaphoreType.DMA((34,)),
            pltpu.SemaphoreType.DMA((34,)),
            pltpu.SemaphoreType.DMA((8,)),
        ],
        compiler_params=pltpu.CompilerParams(
            collective_id=1, has_side_effects=True, vmem_limit_bytes=60 * MIB
        ),
        name="give_back",
    )(counts, send, edge, pairs, back, table, g, q_rows, q_wide)


def on_device(
    positions, velocities, mass, smoothing, energy, counts, send_cells, local_pairs, edge_cells
):
    send = send_cells.reshape(32)
    edge = edge_cells.reshape(2)
    pairs = local_pairs[0, 0].T
    table, g, *local = exchange(counts, send, edge, pairs, positions, velocities, mass, smoothing)
    density, part, heat, back, q_rows, q_wide = compute(send, pairs, edge, table, energy, local)
    extra = give_back(counts, send, edge, pairs, back, table, g, q_rows, q_wide)
    return density, part + extra, heat


def solution(mesh):
    placed = (
        P(None, ("region", "cell"), None),
        P(None, ("region", "cell"), None),
        P(("region", "cell"), None),
        P(("region", "cell"), None),
        P(("region", "cell"), None),
        P(("region", "cell")),
        P("region", "cell", None, None),
        P("region", "cell", None, None),
        P("region", "cell", None),
    )
    return jax.shard_map(
        on_device,
        mesh=mesh,
        in_specs=placed,
        out_specs=(
            P(("region", "cell"), None),
            P(None, ("region", "cell"), None),
            P(("region", "cell"), None),
        ),
        check_vma=False,
    )
```

```python
import functools
import math
import jax
import jax.numpy as jnp
from jax import lax
from jax.experimental import pallas as pl
from jax.experimental.pallas import tpu as pltpu
from jax.sharding import PartitionSpec as P

GAMMA = 5.0 / 3.0
F32, BF16, I32 = jnp.float32, jnp.bfloat16, jnp.int32
U = 3
UL = 4
EARLY = 2
PEERS = 32
LOWER, UPPER, OWN, NSLOT = 32, 33, 34, 38
MAXT = 34
LOCAL = 104
GBLK = MAXT * 16 + 20 + 6 * U
ROOT = math.sqrt(24.0 / math.pi)
MIB = 1024 * 1024
MESH = pl.DeviceIdType.MESH


def halves(v):
    hi = v.astype(BF16).astype(F32)
    return hi, v - hi


def thirds(v):
    first, rest = halves(v)
    second, third = halves(rest)
    return first, second, third


def nt(a, b):
    return lax.dot_general(a, b, (((1,), (1,)), ((), ())), preferred_element_type=F32)


def nn(a, b):
    return lax.dot_general(a, b, (((1,), (0,)), ((), ())), preferred_element_type=F32)


def row_ids():
    return lax.broadcasted_iota(I32, (8, 512), 0)


def square(st):
    x = st[1:2]
    y = st[2:3]
    z = st[3:4]
    return x * x + y * y + z * z


def moments(st):
    row = row_ids()
    vx = st[1:2] * st[4:5] + st[2:3] * st[5:6] + st[3:4] * st[6:7]
    return jnp.where(row == 0, 1.0, jnp.where(row == 7, vx, st)) * st[0:1]


def pair_rows(v):
    first, second = halves(v)
    return jnp.concatenate([first, second], axis=0).astype(BF16)


def store_source(st, base, feat_s, rows_s, lane_s):
    row = row_ids()
    hinv = 1.0 / st[7:8]
    sj = ROOT * hinv * hinv
    f = jnp.where(row == 0, square(st), jnp.where(row <= 3, st, jnp.where(row == 4, 1.0, 0.0)))
    f1, f2, f3 = thirds(f)
    t1, t2, t3 = thirds(sj * hinv)
    t1 = jnp.where(row == 5, t1, 0.0)
    t2 = jnp.where(row == 5, t2, 0.0)
    t3 = jnp.where(row == 5, t3, 0.0)
    near = jnp.concatenate([f1, f1, f2, f2, f1, f3], axis=0).astype(BF16)
    ratio = jnp.concatenate([t1, t1, t2, t2, t1, t3], axis=0).astype(BF16)
    rows = pair_rows(moments(st))
    lane = jnp.where(row == 0, sj, st[0:1])
    for jb in range(4):
        cut = slice(jb * 128, (jb + 1) * 128)
        feat_s[base + jb, :, 0:128] = near[:, cut]
        feat_s[base + jb, :, 128:256] = ratio[:, cut]
        rows_s[base + jb, :, 0:128] = rows[:, cut]
        rows_s[base + jb, :, 128:256] = rows[:, cut]
        lane_s[base + jb] = lane[:, cut]


def store_target(st, base, feat_o, s_o, m_o, rows_o):
    row = row_ids()
    h = st[7:8]
    hinv = 1.0 / h
    si = ROOT * hinv * hinv
    ti = si * hinv
    f = jnp.where(row == 0, 1.0, jnp.where(row <= 3, -2.0 * st, jnp.where(row == 4, square(st), 0.0)))
    f = jnp.where(row == 5, h * h * h * (1.0 / ROOT), f * (ti * ti))
    f1, f2, f3 = thirds(f)
    s1, s2, s3 = thirds(si)
    m1, m2, m3 = thirds(st[0:1])
    extra = jnp.where(row == 0, s1, jnp.where(row == 1, s2, jnp.where(row == 2, s3, 0.0)))
    extra = jnp.where(row == 3, m1, jnp.where(row == 4, m2, jnp.where(row == 5, m3, extra)))
    whole = jnp.concatenate([f1, f2, f1, f2, f3, f1, extra, jnp.zeros((8, 512), F32)], axis=0).astype(BF16)
    rows = pair_rows(moments(st) * ti)
    size = (128, 128)
    eye = (lax.broadcasted_iota(I32, size, 0) == lax.broadcasted_iota(I32, size, 1)).astype(F32).astype(BF16)
    at = lax.broadcasted_iota(I32, (64, 256), 0)
    side = lax.broadcasted_iota(I32, (64, 256), 1) >= 128
    lowest = jnp.where(side, 51, 48)
    pick = ((at >= lowest) & (at < lowest + 3)).astype(F32).astype(BF16)
    for ib in range(4):
        cut = slice(ib * 128, (ib + 1) * 128)
        part = nt(eye, whole[:, cut]).astype(BF16)
        feat_o[base + ib] = part[:, :48]
        wide = nn(part, pick)
        s_o[base + ib] = wide[:, :128]
        m_o[base + ib] = wide[:, 128:]
        rows_o[base + ib] = rows[:, cut]


def split_store(gst, at, g):
    hi = g.astype(BF16)
    gst[at, :, 0:128] = hi
    gst[at, :, 128:256] = (g - hi.astype(F32)).astype(BF16)


def fold(v):
    return v[:, :128] + v[:, 128:]


def local_features(own, feat_s, rows_s, lane_s, feat_o, s_o, m_o, rows_o, *_):
    for a in range(4):
        store_source(own[a], a * 4, feat_s, rows_s, lane_s)
        store_target(own[a], a * 4, feat_o, s_o, m_o, rows_o)


def local_tiles(pair_ref, emit, between, feat_s, rows_s, lane_s, feat_o, s_o, m_o, rows_o, near_a, near_b,
                gst, acc_w, row_w, acc_g, row_g):
    acc_w[...] = jnp.zeros_like(acc_w)
    row_w[...] = jnp.zeros_like(row_w)
    acc_g[...] = jnp.zeros_like(acc_g)
    row_g[...] = jnp.zeros_like(row_g)
    for u in range(UL):
        gst[LOCAL + 2 * UL + u] = jnp.zeros((128, 256), BF16)

    def where(n):
        n = jnp.minimum(n, LOCAL - 1)
        t = lax.rem(n, 10)
        j1 = (t >= 1).astype(I32) + (t >= 3).astype(I32) + (t >= 6).astype(I32)
        i1 = t - (j1 * (j1 + 1)) // 2
        m = jnp.maximum(n - 40, 0)
        k = m // 16
        self_ = n < 40
        ib = jnp.where(self_, i1, lax.rem(m, 4))
        jb = jnp.where(self_, j1, lax.rem(m // 4, 4))
        a = jnp.where(self_, n // 10, pair_ref[0, k])
        b = jnp.where(self_, n // 10, pair_ref[1, k])
        group = jnp.where(self_, n // 10, 4 + k)
        both = jnp.where(self_ & (i1 == j1), 0.0, 1.0)
        return a * 4 + ib, b * 4 + jb, group * 4 + ib, group * 4 + jb, both

    def group(n):
        return tuple(where(n + u) for u in range(UL))

    def distances(buf, those):
        for u in range(UL):
            buf[u] = nn(feat_o[those[u][0]], feat_s[those[u][1]])

    def elements(buf, those, n):
        for u in range(UL):
            oi, si, gi, gj, both = those[u]
            sj = lane_s[si][0:1]
            mass = lane_s[si][1:2]
            d2 = jnp.maximum(buf[u, :, 0:128], 1e-6)
            inv = lax.rsqrt(d2)
            pi = d2 * inv
            pj = pi * buf[u, :, 128:256]
            ai = jnp.maximum(s_o[oi] - pi, 0.0)
            ci = jnp.maximum(ai - pi, 0.0)
            aj = jnp.maximum(sj - pj, 0.0)
            cj = jnp.maximum(aj - pj, 0.0)
            qa = ai * ai
            qc = ci * ci
            ra = aj * aj
            rc = cj * cj
            acc_w[gi] += ((ai + ai) * qa - qc * ci) * mass
            back = ((aj + aj) * ra - rc * cj) * m_o[oi]
            row_w[gj] += both * jnp.sum(back.reshape(16, 8, 128), axis=0)
            split_store(gst, n + u, (qa - qc + ra - rc) * inv)

    def products(those, slot):
        out = []
        for u in range(UL):
            g = gst[slot + u]
            out.append((nt(rows_s[those[u][1]], g), fold(nn(rows_o[those[u][0]], g))))
        return out

    def collect(sums, those):
        for u in range(UL):
            _, _, gi, gj, both = those[u]
            acc_g[gi] += sums[u][0]
            row_g[gj] += sums[u][1] * both

    step = 2 * UL

    def body(emits, n, carry):
        prev, now, later = carry
        base = n * step
        before = jnp.where(n == 0, LOCAL + 2 * UL, base - UL)
        sums = products(prev, before)
        elements(near_a, now, base)
        distances(near_b, later)
        collect(sums, prev)
        after = group(base + step)
        sums = products(now, base)
        elements(near_b, later, base + UL)
        distances(near_a, after)
        collect(sums, now)
        if emits:
            for part, (_, last, _, _) in enumerate(PARTS):
                pl.when(n == last // step - 1)(functools.partial(emit, part))
        return later, after, group(base + step + UL)

    state = group(I32(0))
    distances(near_a, state)
    state = (state, state, group(I32(UL)))
    state = lax.fori_loop(0, EARLY, functools.partial(body, False), state)
    between()
    state = lax.fori_loop(EARLY, LOCAL // step, functools.partial(body, True), state)
    collect(products(state[0], LOCAL - UL), state[0])


LOCAL_SCRATCH = [
    pltpu.VMEM((16, 48, 256), BF16),
    pltpu.VMEM((16, 16, 256), BF16),
    pltpu.VMEM((16, 8, 128), F32),
    pltpu.VMEM((16, 128, 48), BF16),
    pltpu.VMEM((16, 128, 128), F32),
    pltpu.VMEM((16, 128, 128), F32),
    pltpu.VMEM((16, 16, 128), BF16),
    pltpu.VMEM((UL, 128, 256), F32),
    pltpu.VMEM((UL, 128, 256), F32),
    pltpu.VMEM((LOCAL + 3 * UL, 128, 256), BF16),
    pltpu.VMEM((32, 128, 128), F32),
    pltpu.VMEM((32, 8, 128), F32),
    pltpu.VMEM((32, 16, 128), F32),
    pltpu.VMEM((32, 16, 128), F32),
]
LOCAL_OUT = (
    jax.ShapeDtypeStruct((32, 128, 128), F32),
    jax.ShapeDtypeStruct((32, 8, 128), F32),
    jax.ShapeDtypeStruct((32, 16, 128), F32),
    jax.ShapeDtypeStruct((32, 16, 128), F32),
    jax.ShapeDtypeStruct((16, 128, 48), BF16),
    jax.ShapeDtypeStruct((16, 128, 128), F32),
)
NLOCAL = len(LOCAL_OUT)


def local_results(scratch):
    feat_o, s_o = scratch[3], scratch[4]
    return tuple(scratch[10:14]) + (feat_o, s_o)


PARTS = ((0, 40, 0, 16),) + tuple((40 + 16 * k, 56 + 16 * k, 16 + 4 * k, 4) for k in range(4))


def compute_kernel(send_ref, pair_ref, edge_ref, table, energy_in, w_in, roww_h, gg_h, rowg_h, feat_h, s_h,
                   rho_out, acc_out, er_out, t_out, q_rows, q_wide,
                   ta, ts, feat_s, rows_s, lane_s, near_a, near_b, gst, acc_g, acc_w,
                   cnt_v, n_ref, w_pair, energy, roww_in, gg_in, rowg_in, feat_o, s_o, cnt_sem, w_sem, in_sem):
    moves = [
        pltpu.make_async_copy(src, dst, in_sem.at[i])
        for i, (src, dst) in enumerate(
            ((feat_h, feat_o), (s_h, s_o), (gg_h, gg_in), (energy_in, energy), (roww_h, roww_in), (rowg_h, rowg_in))
        )
    ]
    found = jnp.sum((table[:, 0, :] > 0.0).astype(F32), axis=1, keepdims=True)
    cnt_v[...] = jnp.broadcast_to(found, (NSLOT, 128)).astype(I32)
    fetch = pltpu.make_async_copy(cnt_v, n_ref, cnt_sem)
    fetch.start()
    get_w = pltpu.make_async_copy(w_in.at[pl.ds(0, 16)], acc_w, w_sem.at[0])
    get_p = pltpu.make_async_copy(w_in.at[pl.ds(16, 16)], w_pair, w_sem.at[1])
    get_w.start()
    for move in moves[:3]:
        move.start()
    get_p.start()
    for move in moves[3:]:
        move.start()
    row = row_ids()
    acc_g[...] = jnp.zeros_like(acc_g)
    for u in range(U):
        gst[u] = jnp.zeros((128, 256), BF16)
    t_out[...] = jnp.zeros_like(t_out)
    fetch.wait()

    def blocks(s):
        return (n_ref[s, 0] + 127) >> 7

    def add(count, a, s):
        ta[count] = a
        ts[count] = s
        return count + (n_ref[s, 0] > 0).astype(I32)
    count = lax.fori_loop(0, 32, lambda s, cnt: add(cnt, jnp.maximum(send_ref[s], 0), s), I32(0))
    count = add(count, edge_ref[0], I32(LOWER))
    count = add(count, edge_ref[1], I32(UPPER))
    ta[count] = ta[0]
    ts[count] = ts[0]
    total = lax.fori_loop(0, count, lambda k, v: v + blocks(OWN + ta[k]) * blocks(ts[k]), I32(0))

    def source_loop(k, _):
        for u in range(2):
            s = ts[2 * k + u]
            store_source(table[s], s * 4, feat_s, rows_s, lane_s)
        return 0
    lax.fori_loop(0, (count + 1) // 2, source_loop, 0)
    get_w.wait()
    for move in moves[:2]:
        move.wait()

    def at(tile):
        a, s = ta[tile], ts[tile]
        return a, s, blocks(OWN + a), blocks(s)

    def advance(state):
        tile, ib, jb, a, s, ni, nj = state
        ib = ib + 1
        wrap_i = ib >= ni
        ib = jnp.where(wrap_i, 0, ib)
        jb = jnp.where(wrap_i, jb + 1, jb)
        wrap_j = jb >= nj
        jb = jnp.where(wrap_j, 0, jb)
        tile = jnp.where(wrap_j, jnp.minimum(tile + 1, count), tile)
        return (tile, ib, jb) + at(tile)

    def group(state):
        out = []
        for _ in range(U):
            out.append((state[3] * 4 + state[1], state[4] * 4 + state[2]))
            state = advance(state)
        return state, tuple(out)

    def distances(buf, where):
        for u in range(U):
            buf[u] = nn(feat_o[where[u][0]], feat_s[where[u][1]])

    def elements(buf, where, base):
        for u in range(U):
            oi, si = where[u]
            sj = lane_s[si][0:1]
            mass = lane_s[si][1:2] * (base + u < total).astype(F32)
            d2 = jnp.maximum(buf[u, :, 0:128], 1e-6)
            inv = lax.rsqrt(d2)
            pi = d2 * inv
            pj = pi * buf[u, :, 128:256]
            ai = jnp.maximum(s_o[oi] - pi, 0.0)
            ci = jnp.maximum(ai - pi, 0.0)
            qa = ai * ai
            qc = ci * ci
            acc_w[oi] += ((ai + ai) * qa - qc * ci) * mass
            aj = jnp.maximum(sj - pj, 0.0)
            mj = jnp.minimum(pj, aj)
            split_store(gst, base + U + u, (qa - qc + mj * (aj + aj - mj)) * inv)

    def products(where, base):
        return [nt(rows_s[where[u][1]], gst[base + U + u]) for u in range(U)]

    def collect(sums, where, base):
        for u in range(U):
            acc_g[where[u][0]] += jnp.where(base + u < total, sums[u], 0.0)

    zero = I32(0)
    walk, first = group((zero, zero, zero) + at(zero))
    walk, second = group(walk)
    distances(near_a, first)

    def body(n, carry):
        walk, prev, now, later = carry
        base = n * (2 * U)
        sums = products(prev, base - U)
        elements(near_a, now, base)
        distances(near_b, later)
        collect(sums, prev, base - U)
        walk, after = group(walk)
        sums = products(now, base)
        elements(near_b, later, base + U)
        distances(near_a, after)
        collect(sums, now, base)
        walk, last = group(walk)
        return walk, later, after, last

    steps = (total + 2 * U - 1) // (2 * U)
    lax.fori_loop(0, steps + 1, body, (walk, first, first, second))

    def clear(k, _):
        gst[(2 * steps + 3) * U + k] = jnp.zeros((128, 256), BF16)
        return 0
    lax.fori_loop(0, 17, clear, 0)

    get_p.wait()
    for move in moves[2:]:
        move.wait()
    for k in range(16):
        acc_g[k] += gg_in[k]
    lane_id = lax.broadcasted_iota(I32, (1, 512), 1)
    row_sum = [None] * 4
    flat = [None] * 4
    for a in range(4):
        row_sum[a] = jnp.concatenate([roww_in[a * 4 + b] for b in range(4)], axis=1)
        flat[a] = jnp.concatenate([rowg_in[a * 4 + b] for b in range(4)], axis=1)
    for k in range(4):
        ka, kb = pair_ref[0, k], pair_ref[1, k]
        rw = jnp.concatenate([roww_in[16 + k * 4 + b] for b in range(4)], axis=1)
        rg = jnp.concatenate([rowg_in[16 + k * 4 + b] for b in range(4)], axis=1)
        for a in range(4):
            row_sum[a] = row_sum[a] + jnp.where(kb == a, rw, 0.0)
            flat[a] = flat[a] + jnp.where(kb == a, rg, 0.0)
        for b in range(4):
            acc_g[ka * 4 + b] += gg_in[16 + k * 4 + b]
            acc_w[ka * 4 + b] += w_pair[k * 4 + b]

    for a in range(4):
        st = table[OWN + a]
        h = st[7:8]
        h3 = h * h * h
        ti = ROOT / h3
        sums = jnp.concatenate([acc_g[a * 4 + ib] for ib in range(4)], axis=1)
        sums = (sums[:8] + sums[8:]) * ti + flat[a][:8] + flat[a][8:]
        wsum = jnp.concatenate([jnp.sum(acc_w[a * 4 + ib].T, axis=0, keepdims=True) for ib in range(4)], axis=1)
        wsum = wsum + jnp.sum(row_sum[a], axis=0, keepdims=True)
        rho = wsum * (h3 * (8.0 / math.pi / ROOT ** 3))
        live = lane_id < n_ref[OWN + a, 0]
        press = jnp.where(live, (GAMMA - 1.0) * energy[a:a + 1] / jnp.where(live, rho, 1.0), 0.0)
        rho_out[a:a + 1] = jnp.where(live, rho, 0.0)
        dx = [st[1 + k:2 + k] * sums[0:1] - sums[1 + k:2 + k] for k in range(3)]
        heat = sums[7:8]
        for k in range(3):
            heat = heat + st[4 + k:5 + k] * dx[k] - st[1 + k:2 + k] * sums[4 + k:5 + k]
            acc_out[k, a:a + 1] = jnp.where(live, press * dx[k], 0.0)
        er_out[a:a + 1] = jnp.where(live, -press * heat, 0.0)
        q = jnp.where(row == 0, 1.0, jnp.where(row <= 3, st, 0.0)) * (st[0:1] * press)
        q_rows[a] = pair_rows(q * ti)
        plain = pair_rows(q)
        for jb in range(4):
            cut = slice(jb * 128, (jb + 1) * 128)
            q_wide[a * 4 + jb, :, 0:128] = plain[:, cut]
            q_wide[a * 4 + jb, :, 128:256] = plain[:, cut]

    def mirror(_, state):
        for u in range(8):
            tile, jb, a, s, ni, nj, base = state
            slot = jnp.where(tile < count, s, OWN)
            cut = pl.ds(pl.multiple_of(jb * 128, 128), 128)
            o = fold(nn(q_rows[a], gst[pl.ds(base, 4)].reshape(512, 256)))
            o = o[:8] + o[8:]
            t_out[slot, :, cut] = (table[s, :, cut] * o[0:1] - o)[0:4]
            jb = jb + 1
            wrap = jb >= nj
            jb = jnp.where(wrap, 0, jb)
            tile = jnp.where(wrap, jnp.minimum(tile + 1, count), tile)
            base = jnp.where(tile < count, base + ni, base)
            state = (tile, jb) + at(tile) + (base,)
        return state
    panels = lax.fori_loop(0, count, lambda k, v: v + blocks(ts[k]), I32(0))
    lax.fori_loop(0, (panels + 7) // 8, mirror, (zero, zero) + at(zero) + (I32(U),))


def compute(send, pairs, edge, table, energy, local):
    smem = pl.BlockSpec(memory_space=pltpu.SMEM)
    vmem = pl.BlockSpec(memory_space=pltpu.VMEM)
    hbm = pl.BlockSpec(memory_space=pl.ANY)
    return pl.pallas_call(
        compute_kernel,
        out_shape=(
            jax.ShapeDtypeStruct((4, 512), F32),
            jax.ShapeDtypeStruct((3, 4, 512), F32),
            jax.ShapeDtypeStruct((4, 512), F32),
            jax.ShapeDtypeStruct((OWN + 1, 4, 512), F32),
            jax.ShapeDtypeStruct((4, 16, 512), BF16),
            jax.ShapeDtypeStruct((16, 16, 256), BF16),
        ),
        in_specs=[smem] * 3 + [vmem] + [hbm] * 7,
        out_specs=(vmem,) * 6,
        scratch_shapes=[
            pltpu.SMEM((MAXT + 2,), I32),
            pltpu.SMEM((MAXT + 2,), I32),
            pltpu.VMEM((34 * 4, 48, 256), BF16),
            pltpu.VMEM((34 * 4, 16, 256), BF16),
            pltpu.VMEM((34 * 4, 8, 128), F32),
            pltpu.VMEM((U, 128, 256), F32),
            pltpu.VMEM((U, 128, 256), F32),
            pltpu.VMEM((GBLK, 128, 256), BF16),
            pltpu.VMEM((16, 16, 128), F32),
            pltpu.VMEM((16, 128, 128), F32),
            pltpu.VMEM((NSLOT, 128), I32),
            pltpu.SMEM((NSLOT, 128), I32),
            pltpu.VMEM((16, 128, 128), F32),
            pltpu.VMEM((4, 512), F32),
            pltpu.VMEM((32, 8, 128), F32),
            pltpu.VMEM((32, 16, 128), F32),
            pltpu.VMEM((32, 16, 128), F32),
            pltpu.VMEM((16, 128, 48), BF16),
            pltpu.VMEM((16, 128, 128), F32),
            pltpu.SemaphoreType.DMA,
            pltpu.SemaphoreType.DMA((2,)),
            pltpu.SemaphoreType.DMA((6,)),
        ],
        compiler_params=pltpu.CompilerParams(vmem_limit_bytes=62 * MIB),
        name="tiles",
    )(send, pairs, edge, table, energy, *local)


def local_mirror(pair_ref, own, gst, q_rows, q_wide, self_t, pair_t):
    def scale(st):
        return ROOT / (st[7:8] * st[7:8] * st[7:8])

    def settle(st, parts):
        o = jnp.concatenate(parts, axis=1)
        o = o[:8] + o[8:]
        return st * o[0:1] - o

    def one_cell(a, _):
        st = own[a]
        ti = scale(st)
        parts = []
        for jb in range(4):
            first = a * 10 + (jb * (jb + 1)) // 2
            g = gst[pl.ds(first, jb + 1)].reshape((jb + 1) * 128, 256)
            o = fold(nn(q_rows[a, :, 0:(jb + 1) * 128], g))
            for other in range(jb + 1, 4):
                block = gst[a * 10 + (other * (other + 1)) // 2 + jb]
                o = o + nt(q_wide[a * 4 + other], block) * ti[:, jb * 128:(jb + 1) * 128]
            parts.append(o)
        self_t[a] = settle(st, parts)
        return 0
    lax.fori_loop(0, 4, one_cell, 0)

    def one_pair(k, _):
        ka, kb = pair_ref[0, k], pair_ref[1, k]
        first = 40 + k * 16
        there, here = [], []
        q = q_rows[ka]
        wide = [q_wide[kb * 4 + other] for other in range(4)]
        for jb in range(4):
            there.append(fold(nn(q, gst[pl.ds(first + jb * 4, 4)].reshape(512, 256))))
            o = nt(wide[0], gst[first + jb])
            for other in range(1, 4):
                o = o + nt(wide[other], gst[first + other * 4 + jb])
            here.append(o)
        st = own[ka]
        ti = scale(st)
        pair_t[k] = settle(st, [here[jb] * ti[:, jb * 128:(jb + 1) * 128] for jb in range(4)])
        pair_t[4 + k] = settle(own[kb], there)
        return 0
    lax.fori_loop(0, 4, one_pair, 0)


def place():
    region, cell = lax.axis_index("region"), lax.axis_index("cell")
    count = lax.axis_size("region")
    return region, cell, lax.rem(region + count - 1, count), lax.rem(region + 1, count)


def peer_of(cell, k):

    def far(i):
        return jnp.where(i == 0, 2, jnp.where(i == 1, 1, jnp.where(i == 2, 3, 0)))
    x = lax.rem(cell // 8 + far(k // 8), 4)
    y = lax.rem(cell // 2 + far(lax.rem(k // 2, 4)), 4)
    core = lax.rem(cell + 1 - lax.rem(k, 2), 2)
    return x * 8 + y * 2 + core


def greet():
    region, cell, below, above = place()
    barrier = pltpu.get_barrier_semaphore()

    def one(k, _):
        peer = peer_of(cell, k)
        pl.semaphore_signal(barrier, inc=1, device_id=(region, peer), device_id_type=MESH)
        return 0
    lax.fori_loop(0, PEERS - 1, one, 0)
    pl.semaphore_signal(barrier, inc=1, device_id=(below, cell), device_id_type=MESH)
    pl.semaphore_signal(barrier, inc=1, device_id=(above, cell), device_id_type=MESH)
    return barrier


def remote(src, dst, send_sem, recv_sem, slot, mine, device):
    return pltpu.make_async_remote_copy(
        src_ref=src.at[slot],
        dst_ref=dst.at[mine],
        send_sem=send_sem.at[slot],
        recv_sem=recv_sem.at[mine],
        device_id=device,
        device_id_type=MESH,
    )


def exchange_kernel(*refs):
    arrived, table, g_out = refs[:8], refs[8], refs[9]
    outs, scratch = refs[10:10 + NLOCAL], refs[10 + NLOCAL:-14]
    own, payload = refs[-14:-12]
    held, send_sem, recv_sem, local_sem, in_sem = refs[-12:-4], refs[-4], refs[-3], refs[-2], refs[-1]
    moves = [pltpu.make_async_copy(src, dst, in_sem.at[i]) for i, (src, dst) in enumerate(zip(arrived, held))]
    for move in moves:
        move.start()
    region, cell, below, above = place()
    barrier = greet()
    for move in moves:
        move.wait()
    counts, send_ref, edge_ref, pair_ref, positions, velocities, mass, smoothing = held
    lane_id = lax.broadcasted_iota(I32, (1, 512), 1)
    for k in range(4):
        live = lane_id < counts[k]
        own[k] = jnp.concatenate(
            [jnp.where(live, mass[k:k + 1], 0.0)]
            + [positions[i, k:k + 1] - 0.5 for i in range(3)]
            + [velocities[i, k:k + 1] for i in range(3)]
            + [smoothing[k:k + 1]],
            axis=0,
        )
        pltpu.make_async_copy(own.at[k], table.at[OWN + k], local_sem.at[k]).start()
    low = (region > 0).astype(F32)
    high = (region < lax.axis_size("region") - 1).astype(F32)
    payload[LOWER] = own[edge_ref[0]] * low
    payload[UPPER] = own[edge_ref[1]] * high
    payload[cell] = jnp.zeros((8, 512), F32)
    pltpu.make_async_copy(payload.at[cell], table.at[cell], local_sem.at[4]).start()
    local_features(own, *scratch)
    acc_w, row_w, acc_g, row_g, feat_o, s_o = local_results(scratch)
    first = [
        pltpu.make_async_copy(feat_o, outs[4], local_sem.at[5]),
        pltpu.make_async_copy(s_o, outs[5], local_sem.at[6]),
    ]
    rest = [
        pltpu.make_async_copy(src, dst, local_sem.at[7 + i])
        for i, (src, dst) in enumerate(((row_w, outs[1]), (acc_g, outs[2]), (row_g, outs[3])))
    ]
    for copy in first:
        copy.start()

    def part_copies(part):
        low, high, group, size = PARTS[part]
        blocks, groups = pl.ds(low, high - low), pl.ds(group, size)
        return (
            pltpu.make_async_copy(scratch[9].at[blocks], g_out.at[blocks], local_sem.at[10 + 2 * part]),
            pltpu.make_async_copy(acc_w.at[groups], outs[0].at[groups], local_sem.at[11 + 2 * part]),
        )

    def emit(part):
        for copy in part_copies(part):
            copy.start()

    def between():
        pl.semaphore_wait(barrier, PEERS + 1)
        remote(payload, table, send_sem, recv_sem, LOWER, UPPER, (below, cell)).start()
        remote(payload, table, send_sem, recv_sem, UPPER, LOWER, (above, cell)).start()

        def push(k, _):
            peer = peer_of(cell, k)
            pick = send_ref[peer]
            payload[peer] = jnp.where(pick >= 0, own[jnp.maximum(pick, 0)], 0.0)
            remote(payload, table, send_sem, recv_sem, peer, cell, (region, peer)).start()
            return 0
        lax.fori_loop(0, PEERS - 1, push, 0)

    local_tiles(pair_ref, emit, between, *scratch)
    for copy in rest:
        copy.start()
    for k in range(4):
        pltpu.make_async_copy(own.at[k], table.at[OWN + k], local_sem.at[k]).wait()
    pltpu.make_async_copy(payload.at[cell], table.at[cell], local_sem.at[4]).wait()

    def finish(k, _):
        peer = lax.rem(cell + k, PEERS)
        copy = remote(payload, table, send_sem, recv_sem, peer, peer, (region, peer))
        copy.wait_recv()
        copy.wait_send()
        return 0
    lax.fori_loop(1, PEERS, finish, 0)
    for slot, device in ((LOWER, (below, cell)), (UPPER, (above, cell))):
        copy = remote(payload, table, send_sem, recv_sem, slot, slot, device)
        copy.wait_recv()
        copy.wait_send()
    for copy in first + rest:
        copy.wait()
    for part in range(len(PARTS)):
        for copy in part_copies(part):
            copy.wait()


def exchange(counts, send, edge, pairs, positions, velocities, mass, smoothing):
    hbm = pl.BlockSpec(memory_space=pl.ANY)
    return pl.pallas_call(
        exchange_kernel,
        out_shape=(
            jax.ShapeDtypeStruct((NSLOT, 8, 512), F32),
            jax.ShapeDtypeStruct((LOCAL, 128, 256), BF16),
        ) + LOCAL_OUT,
        in_specs=[hbm] * 8,
        out_specs=(hbm,) * (2 + NLOCAL),
        scratch_shapes=LOCAL_SCRATCH + [
            pltpu.VMEM((4, 8, 512), F32),
            pltpu.VMEM((34, 8, 512), F32),
            pltpu.SMEM((4,), I32),
            pltpu.SMEM((32,), I32),
            pltpu.SMEM((2,), I32),
            pltpu.SMEM((2, 4), I32),
            pltpu.VMEM((3, 4, 512), F32),
            pltpu.VMEM((3, 4, 512), F32),
            pltpu.VMEM((4, 512), F32),
            pltpu.VMEM((4, 512), F32),
            pltpu.SemaphoreType.DMA((34,)),
            pltpu.SemaphoreType.DMA((34,)),
            pltpu.SemaphoreType.DMA((20,)),
            pltpu.SemaphoreType.DMA((8,)),
        ],
        compiler_params=pltpu.CompilerParams(
            collective_id=0, has_side_effects=True, vmem_limit_bytes=60 * MIB
        ),
        name="exchange",
    )(counts, send, edge, pairs, positions, velocities, mass, smoothing)


def return_kernel(counts_h, send_h, edge_h, pair_h, back, table, g_in, q_in, wide_in, accel,
                  inbox, own, gst, self_t, pair_t, counts, send_ref, edge_ref, pair_ref, q_rows, q_wide,
                  send_sem, recv_sem, local_sem):
    moves = [
        pltpu.make_async_copy(src, dst, local_sem.at[i])
        for i, (src, dst) in enumerate((
            (table.at[pl.ds(OWN, 4)], own), (g_in, gst), (q_in, q_rows), (wide_in, q_wide),
            (counts_h, counts), (send_h, send_ref), (edge_h, edge_ref), (pair_h, pair_ref),
        ))
    ]
    region, cell, below, above = place()
    barrier = greet()
    for move in moves:
        move.start()
    inbox[cell] = jnp.zeros((4, 512), F32)
    pl.semaphore_wait(barrier, PEERS + 1)

    def push(k, _):
        peer = peer_of(cell, k)
        remote(back, inbox, send_sem, recv_sem, peer, cell, (region, peer)).start()
        return 0
    lax.fori_loop(0, PEERS - 1, push, 0)
    remote(back, inbox, send_sem, recv_sem, LOWER, UPPER, (below, cell)).start()
    remote(back, inbox, send_sem, recv_sem, UPPER, LOWER, (above, cell)).start()

    for move in moves:
        move.wait()
    local_mirror(pair_ref, own, gst, q_rows, q_wide, self_t, pair_t)

    def arrived(k, _):
        peer = lax.rem(cell + k, PEERS)
        remote(back, inbox, send_sem, recv_sem, peer, peer, (region, peer)).wait_recv()
        return 0
    lax.fori_loop(1, PEERS, arrived, 0)
    edges = [
        remote(back, inbox, send_sem, recv_sem, slot, slot, device)
        for slot, device in ((LOWER, (below, cell)), (UPPER, (above, cell)))
    ]
    for copy in edges:
        copy.wait_recv()
    total = []
    for a in range(4):
        t = self_t[a]
        for k in range(4):
            t = t + jnp.where(pair_ref[0, k] == a, pair_t[k], 0.0)
            t = t + jnp.where(pair_ref[1, k] == a, pair_t[4 + k], 0.0)
        total.append(t[0:4])
    for slot in range(34):
        target = send_ref[slot] if slot < PEERS else edge_ref[slot - PEERS]
        rows = inbox[slot]
        for a in range(4):
            total[a] = total[a] + jnp.where(target == a, rows, 0.0)
    lane_id = lax.broadcasted_iota(I32, (1, 512), 1)
    for a in range(4):
        live = lane_id < counts[a]
        for k in range(3):
            accel[k, a:a + 1] = jnp.where(live, total[a][1 + k:2 + k], 0.0)

    def left(k, _):
        peer = lax.rem(cell + k, PEERS)
        remote(back, inbox, send_sem, recv_sem, peer, peer, (region, peer)).wait_send()
        return 0
    lax.fori_loop(1, PEERS, left, 0)
    for copy in edges:
        copy.wait_send()


def give_back(counts, send, edge, pairs, back, table, g, q_rows, q_wide):
    hbm = pl.BlockSpec(memory_space=pl.ANY)
    return pl.pallas_call(
        return_kernel,
        out_shape=jax.ShapeDtypeStruct((3, 4, 512), F32),
        in_specs=[hbm] * 9,
        out_specs=pl.BlockSpec(memory_space=pltpu.VMEM),
        scratch_shapes=[
            pltpu.VMEM((34, 4, 512), F32),
            pltpu.VMEM((4, 8, 512), F32),
            pltpu.VMEM((LOCAL, 128, 256), BF16),
            pltpu.VMEM((4, 8, 512), F32),
            pltpu.VMEM((8, 8, 512), F32),
            pltpu.SMEM((4,), I32),
            pltpu.SMEM((32,), I32),
            pltpu.SMEM((2,), I32),
            pltpu.SMEM((2, 4), I32),
            pltpu.VMEM((4, 16, 512), BF16),
            pltpu.VMEM((16, 16, 256), BF16),
            pltpu.SemaphoreType.DMA((34,)),
            pltpu.SemaphoreType.DMA((34,)),
            pltpu.SemaphoreType.DMA((8,)),
        ],
        compiler_params=pltpu.CompilerParams(
            collective_id=1, has_side_effects=True, vmem_limit_bytes=60 * MIB
        ),
        name="give_back",
    )(counts, send, edge, pairs, back, table, g, q_rows, q_wide)


def on_device(
    positions, velocities, mass, smoothing, energy, counts, send_cells, local_pairs, edge_cells
):
    send = send_cells.reshape(32)
    edge = edge_cells.reshape(2)
    pairs = local_pairs[0, 0].T
    table, g, *local = exchange(counts, send, edge, pairs, positions, velocities, mass, smoothing)
    density, part, heat, back, q_rows, q_wide = compute(send, pairs, edge, table, energy, local)
    extra = give_back(counts, send, edge, pairs, back, table, g, q_rows, q_wide)
    return density, part + extra, heat


def solution(mesh):
    placed = (
        P(None, ("region", "cell"), None),
        P(None, ("region", "cell"), None),
        P(("region", "cell"), None),
        P(("region", "cell"), None),
        P(("region", "cell"), None),
        P(("region", "cell")),
        P("region", "cell", None, None),
        P("region", "cell", None, None),
        P("region", "cell", None),
    )
    return jax.shard_map(
        on_device,
        mesh=mesh,
        in_specs=placed,
        out_specs=(
            P(("region", "cell"), None),
            P(None, ("region", "cell"), None),
            P(("region", "cell"), None),
        ),
        check_vma=False,
    )
```

```python
import functools
import math
import jax
import jax.numpy as jnp
from jax import lax
from jax.experimental import pallas as pl
from jax.experimental.pallas import tpu as pltpu
from jax.sharding import PartitionSpec as P

GAMMA = 5.0 / 3.0
F32, BF16, I32 = jnp.float32, jnp.bfloat16, jnp.int32
U = 3
UL = 4
EARLY = 2
PEERS = 32
LOWER, UPPER, OWN, NSLOT = 32, 33, 34, 38
MAXT = 34
LOCAL = 104
GBLK = MAXT * 16 + 20 + 6 * U
ROOT = math.sqrt(24.0 / math.pi)
MIB = 1024 * 1024
MESH = pl.DeviceIdType.MESH


def halves(v):
    hi = v.astype(BF16).astype(F32)
    return hi, v - hi


def thirds(v):
    first, rest = halves(v)
    second, third = halves(rest)
    return first, second, third


def nt(a, b):
    return lax.dot_general(a, b, (((1,), (1,)), ((), ())), preferred_element_type=F32)


def nn(a, b):
    return lax.dot_general(a, b, (((1,), (0,)), ((), ())), preferred_element_type=F32)


def row_ids():
    return lax.broadcasted_iota(I32, (8, 512), 0)


def square(st):
    x = st[1:2]
    y = st[2:3]
    z = st[3:4]
    return x * x + y * y + z * z


def moments(st):
    row = row_ids()
    vx = st[1:2] * st[4:5] + st[2:3] * st[5:6] + st[3:4] * st[6:7]
    return jnp.where(row == 0, 1.0, jnp.where(row == 7, vx, st)) * st[0:1]


def pair_rows(v):
    first, second = halves(v)
    return jnp.concatenate([first, second], axis=0).astype(BF16)


def store_source(st, base, feat_s, rows_s, lane_s):
    row = row_ids()
    hinv = 1.0 / st[7:8]
    sj = ROOT * hinv * hinv
    f = jnp.where(row == 0, square(st), jnp.where(row <= 3, st, jnp.where(row == 4, 1.0, 0.0)))
    f1, f2, f3 = thirds(f)
    t1, t2, t3 = thirds(sj * hinv)
    t1 = jnp.where(row == 5, t1, 0.0)
    t2 = jnp.where(row == 5, t2, 0.0)
    t3 = jnp.where(row == 5, t3, 0.0)
    near = jnp.concatenate([f1, f1, f2, f2, f1, f3], axis=0).astype(BF16)
    ratio = jnp.concatenate([t1, t1, t2, t2, t1, t3], axis=0).astype(BF16)
    rows = pair_rows(moments(st))
    lane = jnp.where(row == 0, sj, st[0:1])
    for jb in range(4):
        cut = slice(jb * 128, (jb + 1) * 128)
        feat_s[base + jb, :, 0:128] = near[:, cut]
        feat_s[base + jb, :, 128:256] = ratio[:, cut]
        rows_s[base + jb, :, 0:128] = rows[:, cut]
        rows_s[base + jb, :, 128:256] = rows[:, cut]
        lane_s[base + jb] = lane[:, cut]


def store_target(st, base, feat_o, s_o, m_o, rows_o):
    row = row_ids()
    h = st[7:8]
    hinv = 1.0 / h
    si = ROOT * hinv * hinv
    ti = si * hinv
    f = jnp.where(row == 0, 1.0, jnp.where(row <= 3, -2.0 * st, jnp.where(row == 4, square(st), 0.0)))
    f = jnp.where(row == 5, h * h * h * (1.0 / ROOT), f * (ti * ti))
    f1, f2, f3 = thirds(f)
    s1, s2, s3 = thirds(si)
    m1, m2, m3 = thirds(st[0:1])
    extra = jnp.where(row == 0, s1, jnp.where(row == 1, s2, jnp.where(row == 2, s3, 0.0)))
    extra = jnp.where(row == 3, m1, jnp.where(row == 4, m2, jnp.where(row == 5, m3, extra)))
    whole = jnp.concatenate([f1, f2, f1, f2, f3, f1, extra, jnp.zeros((8, 512), F32)], axis=0).astype(BF16)
    rows = pair_rows(moments(st) * ti)
    size = (128, 128)
    eye = (lax.broadcasted_iota(I32, size, 0) == lax.broadcasted_iota(I32, size, 1)).astype(F32).astype(BF16)
    at = lax.broadcasted_iota(I32, (64, 256), 0)
    side = lax.broadcasted_iota(I32, (64, 256), 1) >= 128
    lowest = jnp.where(side, 51, 48)
    pick = ((at >= lowest) & (at < lowest + 3)).astype(F32).astype(BF16)
    for ib in range(4):
        cut = slice(ib * 128, (ib + 1) * 128)
        part = nt(eye, whole[:, cut]).astype(BF16)
        feat_o[base + ib] = part[:, :48]
        wide = nn(part, pick)
        s_o[base + ib] = wide[:, :128]
        m_o[base + ib] = wide[:, 128:]
        rows_o[base + ib] = rows[:, cut]


def split_store(gst, at, g):
    hi = g.astype(BF16)
    gst[at, :, 0:128] = hi
    gst[at, :, 128:256] = (g - hi.astype(F32)).astype(BF16)


def fold(v):
    return v[:, :128] + v[:, 128:]


def local_features(own, feat_s, rows_s, lane_s, feat_o, s_o, m_o, rows_o, *_):
    for a in range(4):
        store_source(own[a], a * 4, feat_s, rows_s, lane_s)
        store_target(own[a], a * 4, feat_o, s_o, m_o, rows_o)


def local_tiles(pair_ref, emit, between, feat_s, rows_s, lane_s, feat_o, s_o, m_o, rows_o, near_a, near_b,
                gst, acc_w, row_w, acc_g, row_g):
    acc_w[...] = jnp.zeros_like(acc_w)
    row_w[...] = jnp.zeros_like(row_w)
    acc_g[...] = jnp.zeros_like(acc_g)
    row_g[...] = jnp.zeros_like(row_g)
    for u in range(UL):
        gst[LOCAL + 2 * UL + u] = jnp.zeros((128, 256), BF16)

    def where(n):
        n = jnp.minimum(n, LOCAL - 1)
        t = lax.rem(n, 10)
        j1 = (t >= 1).astype(I32) + (t >= 3).astype(I32) + (t >= 6).astype(I32)
        i1 = t - (j1 * (j1 + 1)) // 2
        m = jnp.maximum(n - 40, 0)
        k = m // 16
        self_ = n < 40
        ib = jnp.where(self_, i1, lax.rem(m, 4))
        jb = jnp.where(self_, j1, lax.rem(m // 4, 4))
        a = jnp.where(self_, n // 10, pair_ref[0, k])
        b = jnp.where(self_, n // 10, pair_ref[1, k])
        group = jnp.where(self_, n // 10, 4 + k)
        both = jnp.where(self_ & (i1 == j1), 0.0, 1.0)
        return a * 4 + ib, b * 4 + jb, group * 4 + ib, group * 4 + jb, both

    def group(n):
        return tuple(where(n + u) for u in range(UL))

    def distances(buf, those):
        for u in range(UL):
            buf[u] = nn(feat_o[those[u][0]], feat_s[those[u][1]])

    def elements(buf, those, n):
        for u in range(UL):
            oi, si, gi, gj, both = those[u]
            sj = lane_s[si][0:1]
            mass = lane_s[si][1:2]
            d2 = jnp.maximum(buf[u, :, 0:128], 1e-6)
            inv = lax.rsqrt(d2)
            pi = d2 * inv
            pj = pi * buf[u, :, 128:256]
            ai = jnp.maximum(s_o[oi] - pi, 0.0)
            ci = jnp.maximum(ai - pi, 0.0)
            aj = jnp.maximum(sj - pj, 0.0)
            cj = jnp.maximum(aj - pj, 0.0)
            qa = ai * ai
            qc = ci * ci
            ra = aj * aj
            rc = cj * cj
            acc_w[gi] += ((ai + ai) * qa - qc * ci) * mass
            back = ((aj + aj) * ra - rc * cj) * m_o[oi]
            row_w[gj] += both * jnp.sum(back.reshape(16, 8, 128), axis=0)
            split_store(gst, n + u, (qa - qc + ra - rc) * inv)

    def products(those, slot):
        out = []
        for u in range(UL):
            g = gst[slot + u]
            out.append((nt(rows_s[those[u][1]], g), fold(nn(rows_o[those[u][0]], g))))
        return out

    def collect(sums, those):
        for u in range(UL):
            _, _, gi, gj, both = those[u]
            acc_g[gi] += sums[u][0]
            row_g[gj] += sums[u][1] * both

    step = 2 * UL

    def body(emits, n, carry):
        prev, now, later = carry
        base = n * step
        before = jnp.where(n == 0, LOCAL + 2 * UL, base - UL)
        sums = products(prev, before)
        elements(near_a, now, base)
        distances(near_b, later)
        collect(sums, prev)
        after = group(base + step)
        sums = products(now, base)
        elements(near_b, later, base + UL)
        distances(near_a, after)
        collect(sums, now)
        if emits:
            for part, (_, last, _, _) in enumerate(PARTS):
                pl.when(n == last // step - 1)(functools.partial(emit, part))
        return later, after, group(base + step + UL)

    state = group(I32(0))
    distances(near_a, state)
    state = (state, state, group(I32(UL)))
    state = lax.fori_loop(0, EARLY, functools.partial(body, False), state)
    between()
    state = lax.fori_loop(EARLY, LOCAL // step, functools.partial(body, True), state)
    collect(products(state[0], LOCAL - UL), state[0])


LOCAL_SCRATCH = [
    pltpu.VMEM((16, 48, 256), BF16),
    pltpu.VMEM((16, 16, 256), BF16),
    pltpu.VMEM((16, 8, 128), F32),
    pltpu.VMEM((16, 128, 48), BF16),
    pltpu.VMEM((16, 128, 128), F32),
    pltpu.VMEM((16, 128, 128), F32),
    pltpu.VMEM((16, 16, 128), BF16),
    pltpu.VMEM((UL, 128, 256), F32),
    pltpu.VMEM((UL, 128, 256), F32),
    pltpu.VMEM((LOCAL + 3 * UL, 128, 256), BF16),
    pltpu.VMEM((32, 128, 128), F32),
    pltpu.VMEM((32, 8, 128), F32),
    pltpu.VMEM((32, 16, 128), F32),
    pltpu.VMEM((32, 16, 128), F32),
]
LOCAL_OUT = (
    jax.ShapeDtypeStruct((32, 128, 128), F32),
    jax.ShapeDtypeStruct((32, 8, 128), F32),
    jax.ShapeDtypeStruct((32, 16, 128), F32),
    jax.ShapeDtypeStruct((32, 16, 128), F32),
    jax.ShapeDtypeStruct((16, 128, 48), BF16),
    jax.ShapeDtypeStruct((16, 128, 128), F32),
)
NLOCAL = len(LOCAL_OUT)


def local_results(scratch):
    feat_o, s_o = scratch[3], scratch[4]
    return tuple(scratch[10:14]) + (feat_o, s_o)


PARTS = ((0, 40, 0, 16),) + tuple((40 + 16 * k, 56 + 16 * k, 16 + 4 * k, 4) for k in range(4))


def compute_kernel(send_ref, pair_ref, edge_ref, table, energy_in, w_in, roww_h, gg_h, rowg_h, feat_h, s_h,
                   rho_out, acc_out, er_out, t_out, q_rows, q_wide,
                   ta, ts, feat_s, rows_s, lane_s, near_a, near_b, gst, acc_g, acc_w,
                   cnt_v, n_ref, w_pair, energy, roww_in, gg_in, rowg_in, feat_o, s_o, cnt_sem, w_sem, in_sem):
    moves = [
        pltpu.make_async_copy(src, dst, in_sem.at[i])
        for i, (src, dst) in enumerate(
            ((feat_h, feat_o), (s_h, s_o), (gg_h, gg_in), (energy_in, energy), (roww_h, roww_in), (rowg_h, rowg_in))
        )
    ]
    found = jnp.sum((table[:, 0, :] > 0.0).astype(F32), axis=1, keepdims=True)
    cnt_v[...] = jnp.broadcast_to(found, (NSLOT, 128)).astype(I32)
    fetch = pltpu.make_async_copy(cnt_v, n_ref, cnt_sem)
    fetch.start()
    get_w = pltpu.make_async_copy(w_in.at[pl.ds(0, 16)], acc_w, w_sem.at[0])
    get_p = pltpu.make_async_copy(w_in.at[pl.ds(16, 16)], w_pair, w_sem.at[1])
    get_w.start()
    for move in moves[:3]:
        move.start()
    get_p.start()
    for move in moves[3:]:
        move.start()
    row = row_ids()
    acc_g[...] = jnp.zeros_like(acc_g)
    for u in range(U):
        gst[u] = jnp.zeros((128, 256), BF16)
    t_out[...] = jnp.zeros_like(t_out)
    fetch.wait()

    def blocks(s):
        return (n_ref[s, 0] + 127) >> 7

    def add(count, a, s):
        ta[count] = a
        ts[count] = s
        return count + (n_ref[s, 0] > 0).astype(I32)
    count = lax.fori_loop(0, 32, lambda s, cnt: add(cnt, jnp.maximum(send_ref[s], 0), s), I32(0))
    count = add(count, edge_ref[0], I32(LOWER))
    count = add(count, edge_ref[1], I32(UPPER))
    ta[count] = ta[0]
    ts[count] = ts[0]
    total = lax.fori_loop(0, count, lambda k, v: v + blocks(OWN + ta[k]) * blocks(ts[k]), I32(0))

    def source_loop(k, _):
        for u in range(2):
            s = ts[2 * k + u]
            store_source(table[s], s * 4, feat_s, rows_s, lane_s)
        return 0
    lax.fori_loop(0, (count + 1) // 2, source_loop, 0)
    get_w.wait()
    for move in moves[:2]:
        move.wait()

    def at(tile):
        a, s = ta[tile], ts[tile]
        return a, s, blocks(OWN + a), blocks(s)

    def advance(state):
        tile, ib, jb, a, s, ni, nj = state
        ib = ib + 1
        wrap_i = ib >= ni
        ib = jnp.where(wrap_i, 0, ib)
        jb = jnp.where(wrap_i, jb + 1, jb)
        wrap_j = jb >= nj
        jb = jnp.where(wrap_j, 0, jb)
        tile = jnp.where(wrap_j, jnp.minimum(tile + 1, count), tile)
        return (tile, ib, jb) + at(tile)

    def group(state):
        out = []
        for _ in range(U):
            out.append((state[3] * 4 + state[1], state[4] * 4 + state[2]))
            state = advance(state)
        return state, tuple(out)

    def distances(buf, where):
        for u in range(U):
            buf[u] = nn(feat_o[where[u][0]], feat_s[where[u][1]])

    def elements(buf, where, base):
        for u in range(U):
            oi, si = where[u]
            sj = lane_s[si][0:1]
            mass = lane_s[si][1:2] * (base + u < total).astype(F32)
            d2 = jnp.maximum(buf[u, :, 0:128], 1e-6)
            inv = lax.rsqrt(d2)
            pi = d2 * inv
            pj = pi * buf[u, :, 128:256]
            ai = jnp.maximum(s_o[oi] - pi, 0.0)
            ci = jnp.maximum(ai - pi, 0.0)
            qa = ai * ai
            qc = ci * ci
            acc_w[oi] += ((ai + ai) * qa - qc * ci) * mass
            aj = jnp.maximum(sj - pj, 0.0)
            mj = jnp.minimum(pj, aj)
            split_store(gst, base + U + u, (qa - qc + mj * (aj + aj - mj)) * inv)

    def products(where, base):
        return [nt(rows_s[where[u][1]], gst[base + U + u]) for u in range(U)]

    def collect(sums, where, base):
        for u in range(U):
            acc_g[where[u][0]] += jnp.where(base + u < total, sums[u], 0.0)

    zero = I32(0)
    walk, first = group((zero, zero, zero) + at(zero))
    walk, second = group(walk)
    distances(near_a, first)

    def body(n, carry):
        walk, prev, now, later = carry
        base = n * (2 * U)
        sums = products(prev, base - U)
        elements(near_a, now, base)
        distances(near_b, later)
        collect(sums, prev, base - U)
        walk, after = group(walk)
        sums = products(now, base)
        elements(near_b, later, base + U)
        distances(near_a, after)
        collect(sums, now, base)
        walk, last = group(walk)
        return walk, later, after, last

    steps = (total + 2 * U - 1) // (2 * U)
    lax.fori_loop(0, steps + 1, body, (walk, first, first, second))

    def clear(k, _):
        gst[(2 * steps + 3) * U + k] = jnp.zeros((128, 256), BF16)
        return 0
    lax.fori_loop(0, 17, clear, 0)

    get_p.wait()
    for move in moves[2:]:
        move.wait()
    for k in range(16):
        acc_g[k] += gg_in[k]
    lane_id = lax.broadcasted_iota(I32, (1, 512), 1)
    row_sum = [None] * 4
    flat = [None] * 4
    for a in range(4):
        row_sum[a] = jnp.concatenate([roww_in[a * 4 + b] for b in range(4)], axis=1)
        flat[a] = jnp.concatenate([rowg_in[a * 4 + b] for b in range(4)], axis=1)
    for k in range(4):
        ka, kb = pair_ref[0, k], pair_ref[1, k]
        rw = jnp.concatenate([roww_in[16 + k * 4 + b] for b in range(4)], axis=1)
        rg = jnp.concatenate([rowg_in[16 + k * 4 + b] for b in range(4)], axis=1)
        for a in range(4):
            row_sum[a] = row_sum[a] + jnp.where(kb == a, rw, 0.0)
            flat[a] = flat[a] + jnp.where(kb == a, rg, 0.0)
        for b in range(4):
            acc_g[ka * 4 + b] += gg_in[16 + k * 4 + b]
            acc_w[ka * 4 + b] += w_pair[k * 4 + b]

    for a in range(4):
        st = table[OWN + a]
        h = st[7:8]
        h3 = h * h * h
        ti = ROOT / h3
        sums = jnp.concatenate([acc_g[a * 4 + ib] for ib in range(4)], axis=1)
        sums = (sums[:8] + sums[8:]) * ti + flat[a][:8] + flat[a][8:]
        wsum = jnp.concatenate([jnp.sum(acc_w[a * 4 + ib].T, axis=0, keepdims=True) for ib in range(4)], axis=1)
        wsum = wsum + jnp.sum(row_sum[a], axis=0, keepdims=True)
        rho = wsum * (h3 * (8.0 / math.pi / ROOT ** 3))
        live = lane_id < n_ref[OWN + a, 0]
        press = jnp.where(live, (GAMMA - 1.0) * energy[a:a + 1] / jnp.where(live, rho, 1.0), 0.0)
        rho_out[a:a + 1] = jnp.where(live, rho, 0.0)
        dx = [st[1 + k:2 + k] * sums[0:1] - sums[1 + k:2 + k] for k in range(3)]
        heat = sums[7:8]
        for k in range(3):
            heat = heat + st[4 + k:5 + k] * dx[k] - st[1 + k:2 + k] * sums[4 + k:5 + k]
            acc_out[k, a:a + 1] = jnp.where(live, press * dx[k], 0.0)
        er_out[a:a + 1] = jnp.where(live, -press * heat, 0.0)
        q = jnp.where(row == 0, 1.0, jnp.where(row <= 3, st, 0.0)) * (st[0:1] * press)
        q_rows[a] = pair_rows(q * ti)
        plain = pair_rows(q)
        for jb in range(4):
            cut = slice(jb * 128, (jb + 1) * 128)
            q_wide[a * 4 + jb, :, 0:128] = plain[:, cut]
            q_wide[a * 4 + jb, :, 128:256] = plain[:, cut]

    def mirror(_, state):
        for u in range(8):
            tile, jb, a, s, ni, nj, base = state
            slot = jnp.where(tile < count, s, OWN)
            cut = pl.ds(pl.multiple_of(jb * 128, 128), 128)
            o = fold(nn(q_rows[a], gst[pl.ds(base, 4)].reshape(512, 256)))
            o = o[:8] + o[8:]
            t_out[slot, :, cut] = (table[s, :, cut] * o[0:1] - o)[0:4]
            jb = jb + 1
            wrap = jb >= nj
            jb = jnp.where(wrap, 0, jb)
            tile = jnp.where(wrap, jnp.minimum(tile + 1, count), tile)
            base = jnp.where(tile < count, base + ni, base)
            state = (tile, jb) + at(tile) + (base,)
        return state
    panels = lax.fori_loop(0, count, lambda k, v: v + blocks(ts[k]), I32(0))
    lax.fori_loop(0, (panels + 7) // 8, mirror, (zero, zero) + at(zero) + (I32(U),))


def compute(send, pairs, edge, table, energy, local):
    smem = pl.BlockSpec(memory_space=pltpu.SMEM)
    vmem = pl.BlockSpec(memory_space=pltpu.VMEM)
    hbm = pl.BlockSpec(memory_space=pl.ANY)
    return pl.pallas_call(
        compute_kernel,
        out_shape=(
            jax.ShapeDtypeStruct((4, 512), F32),
            jax.ShapeDtypeStruct((3, 4, 512), F32),
            jax.ShapeDtypeStruct((4, 512), F32),
            jax.ShapeDtypeStruct((OWN + 1, 4, 512), F32),
            jax.ShapeDtypeStruct((4, 16, 512), BF16),
            jax.ShapeDtypeStruct((16, 16, 256), BF16),
        ),
        in_specs=[smem] * 3 + [vmem] + [hbm] * 7,
        out_specs=(vmem,) * 6,
        scratch_shapes=[
            pltpu.SMEM((MAXT + 2,), I32),
            pltpu.SMEM((MAXT + 2,), I32),
            pltpu.VMEM((34 * 4, 48, 256), BF16),
            pltpu.VMEM((34 * 4, 16, 256), BF16),
            pltpu.VMEM((34 * 4, 8, 128), F32),
            pltpu.VMEM((U, 128, 256), F32),
            pltpu.VMEM((U, 128, 256), F32),
            pltpu.VMEM((GBLK, 128, 256), BF16),
            pltpu.VMEM((16, 16, 128), F32),
            pltpu.VMEM((16, 128, 128), F32),
            pltpu.VMEM((NSLOT, 128), I32),
            pltpu.SMEM((NSLOT, 128), I32),
            pltpu.VMEM((16, 128, 128), F32),
            pltpu.VMEM((4, 512), F32),
            pltpu.VMEM((32, 8, 128), F32),
            pltpu.VMEM((32, 16, 128), F32),
            pltpu.VMEM((32, 16, 128), F32),
            pltpu.VMEM((16, 128, 48), BF16),
            pltpu.VMEM((16, 128, 128), F32),
            pltpu.SemaphoreType.DMA,
            pltpu.SemaphoreType.DMA((2,)),
            pltpu.SemaphoreType.DMA((6,)),
        ],
        compiler_params=pltpu.CompilerParams(vmem_limit_bytes=62 * MIB),
        name="tiles",
    )(send, pairs, edge, table, energy, *local)


def local_mirror(pair_ref, own, gst, q_rows, q_wide, self_t, pair_t):
    def scale(st):
        return ROOT / (st[7:8] * st[7:8] * st[7:8])

    def settle(st, parts):
        o = jnp.concatenate(parts, axis=1)
        o = o[:8] + o[8:]
        return st * o[0:1] - o

    def one_cell(a, _):
        st = own[a]
        ti = scale(st)
        parts = []
        for jb in range(4):
            first = a * 10 + (jb * (jb + 1)) // 2
            g = gst[pl.ds(first, jb + 1)].reshape((jb + 1) * 128, 256)
            o = fold(nn(q_rows[a, :, 0:(jb + 1) * 128], g))
            for other in range(jb + 1, 4):
                block = gst[a * 10 + (other * (other + 1)) // 2 + jb]
                o = o + nt(q_wide[a * 4 + other], block) * ti[:, jb * 128:(jb + 1) * 128]
            parts.append(o)
        self_t[a] = settle(st, parts)
        return 0
    lax.fori_loop(0, 4, one_cell, 0)

    def one_pair(k, _):
        ka, kb = pair_ref[0, k], pair_ref[1, k]
        first = 40 + k * 16
        there, here = [], []
        q = q_rows[ka]
        wide = [q_wide[kb * 4 + other] for other in range(4)]
        for jb in range(4):
            there.append(fold(nn(q, gst[pl.ds(first + jb * 4, 4)].reshape(512, 256))))
            o = nt(wide[0], gst[first + jb])
            for other in range(1, 4):
                o = o + nt(wide[other], gst[first + other * 4 + jb])
            here.append(o)
        st = own[ka]
        ti = scale(st)
        pair_t[k] = settle(st, [here[jb] * ti[:, jb * 128:(jb + 1) * 128] for jb in range(4)])
        pair_t[4 + k] = settle(own[kb], there)
        return 0
    lax.fori_loop(0, 4, one_pair, 0)


def place():
    region, cell = lax.axis_index("region"), lax.axis_index("cell")
    count = lax.axis_size("region")
    return region, cell, lax.rem(region + count - 1, count), lax.rem(region + 1, count)


def peers_of(cell):
    order = (2, 1, 3, 0)
    x, y, core = cell // 8, lax.rem(cell // 2, 4), lax.rem(cell, 2)
    xs = [lax.rem(x + step, 4) * 8 for step in order]
    ys = [lax.rem(y + step, 4) * 2 for step in order]
    return [i + j + k for i in xs for j in ys for k in (1 - core, core)][:-1]


def greet():
    region, cell, below, above = place()
    barrier = pltpu.get_barrier_semaphore()

    for peer in peers_of(cell):
        pl.semaphore_signal(barrier, inc=1, device_id=(region, peer), device_id_type=MESH)
    pl.semaphore_signal(barrier, inc=1, device_id=(below, cell), device_id_type=MESH)
    pl.semaphore_signal(barrier, inc=1, device_id=(above, cell), device_id_type=MESH)
    return barrier


def remote(src, dst, send_sem, recv_sem, slot, mine, device):
    return pltpu.make_async_remote_copy(
        src_ref=src.at[slot],
        dst_ref=dst.at[mine],
        send_sem=send_sem.at[slot],
        recv_sem=recv_sem.at[mine],
        device_id=device,
        device_id_type=MESH,
    )


def exchange_kernel(*refs):
    arrived, table, g_out = refs[:8], refs[8], refs[9]
    outs, scratch = refs[10:10 + NLOCAL], refs[10 + NLOCAL:-14]
    own, payload = refs[-14:-12]
    held, send_sem, recv_sem, local_sem, in_sem = refs[-12:-4], refs[-4], refs[-3], refs[-2], refs[-1]
    moves = [pltpu.make_async_copy(src, dst, in_sem.at[i]) for i, (src, dst) in enumerate(zip(arrived, held))]
    for move in moves:
        move.start()
    region, cell, below, above = place()
    barrier = greet()
    for move in moves:
        move.wait()
    counts, send_ref, edge_ref, pair_ref, positions, velocities, mass, smoothing = held
    lane_id = lax.broadcasted_iota(I32, (1, 512), 1)
    for k in range(4):
        live = lane_id < counts[k]
        own[k] = jnp.concatenate(
            [jnp.where(live, mass[k:k + 1], 0.0)]
            + [positions[i, k:k + 1] - 0.5 for i in range(3)]
            + [velocities[i, k:k + 1] for i in range(3)]
            + [smoothing[k:k + 1]],
            axis=0,
        )
        pltpu.make_async_copy(own.at[k], table.at[OWN + k], local_sem.at[k]).start()
    low = (region > 0).astype(F32)
    high = (region < lax.axis_size("region") - 1).astype(F32)
    payload[LOWER] = own[edge_ref[0]] * low
    payload[UPPER] = own[edge_ref[1]] * high
    payload[cell] = jnp.zeros((8, 512), F32)
    pltpu.make_async_copy(payload.at[cell], table.at[cell], local_sem.at[4]).start()
    local_features(own, *scratch)
    acc_w, row_w, acc_g, row_g, feat_o, s_o = local_results(scratch)
    first = [
        pltpu.make_async_copy(feat_o, outs[4], local_sem.at[5]),
        pltpu.make_async_copy(s_o, outs[5], local_sem.at[6]),
    ]
    rest = [
        pltpu.make_async_copy(src, dst, local_sem.at[7 + i])
        for i, (src, dst) in enumerate(((row_w, outs[1]), (acc_g, outs[2]), (row_g, outs[3])))
    ]
    for copy in first:
        copy.start()

    def part_copies(part):
        low, high, group, size = PARTS[part]
        blocks, groups = pl.ds(low, high - low), pl.ds(group, size)
        return (
            pltpu.make_async_copy(scratch[9].at[blocks], g_out.at[blocks], local_sem.at[10 + 2 * part]),
            pltpu.make_async_copy(acc_w.at[groups], outs[0].at[groups], local_sem.at[11 + 2 * part]),
        )

    def emit(part):
        for copy in part_copies(part):
            copy.start()

    def between():
        pl.semaphore_wait(barrier, PEERS + 1)
        remote(payload, table, send_sem, recv_sem, LOWER, UPPER, (below, cell)).start()
        remote(payload, table, send_sem, recv_sem, UPPER, LOWER, (above, cell)).start()

        for peer in peers_of(cell):
            pick = send_ref[peer]
            payload[peer] = jnp.where(pick >= 0, own[jnp.maximum(pick, 0)], 0.0)
            remote(payload, table, send_sem, recv_sem, peer, cell, (region, peer)).start()

    local_tiles(pair_ref, emit, between, *scratch)
    for copy in rest:
        copy.start()
    for k in range(4):
        pltpu.make_async_copy(own.at[k], table.at[OWN + k], local_sem.at[k]).wait()
    pltpu.make_async_copy(payload.at[cell], table.at[cell], local_sem.at[4]).wait()

    def finish(k, _):
        peer = lax.rem(cell + k, PEERS)
        copy = remote(payload, table, send_sem, recv_sem, peer, peer, (region, peer))
        copy.wait_recv()
        copy.wait_send()
        return 0
    lax.fori_loop(1, PEERS, finish, 0)
    for slot, device in ((LOWER, (below, cell)), (UPPER, (above, cell))):
        copy = remote(payload, table, send_sem, recv_sem, slot, slot, device)
        copy.wait_recv()
        copy.wait_send()
    for copy in first + rest:
        copy.wait()
    for part in range(len(PARTS)):
        for copy in part_copies(part):
            copy.wait()


def exchange(counts, send, edge, pairs, positions, velocities, mass, smoothing):
    hbm = pl.BlockSpec(memory_space=pl.ANY)
    return pl.pallas_call(
        exchange_kernel,
        out_shape=(
            jax.ShapeDtypeStruct((NSLOT, 8, 512), F32),
            jax.ShapeDtypeStruct((LOCAL, 128, 256), BF16),
        ) + LOCAL_OUT,
        in_specs=[hbm] * 8,
        out_specs=(hbm,) * (2 + NLOCAL),
        scratch_shapes=LOCAL_SCRATCH + [
            pltpu.VMEM((4, 8, 512), F32),
            pltpu.VMEM((34, 8, 512), F32),
            pltpu.SMEM((4,), I32),
            pltpu.SMEM((32,), I32),
            pltpu.SMEM((2,), I32),
            pltpu.SMEM((2, 4), I32),
            pltpu.VMEM((3, 4, 512), F32),
            pltpu.VMEM((3, 4, 512), F32),
            pltpu.VMEM((4, 512), F32),
            pltpu.VMEM((4, 512), F32),
            pltpu.SemaphoreType.DMA((34,)),
            pltpu.SemaphoreType.DMA((34,)),
            pltpu.SemaphoreType.DMA((20,)),
            pltpu.SemaphoreType.DMA((8,)),
        ],
        compiler_params=pltpu.CompilerParams(
            collective_id=0, has_side_effects=True, vmem_limit_bytes=60 * MIB
        ),
        name="exchange",
    )(counts, send, edge, pairs, positions, velocities, mass, smoothing)


def return_kernel(counts_h, send_h, edge_h, pair_h, back, table, g_in, q_in, wide_in, accel,
                  inbox, own, gst, self_t, pair_t, counts, send_ref, edge_ref, pair_ref, q_rows, q_wide,
                  send_sem, recv_sem, local_sem):
    moves = [
        pltpu.make_async_copy(src, dst, local_sem.at[i])
        for i, (src, dst) in enumerate((
            (table.at[pl.ds(OWN, 4)], own), (g_in, gst), (q_in, q_rows), (wide_in, q_wide),
            (counts_h, counts), (send_h, send_ref), (edge_h, edge_ref), (pair_h, pair_ref),
        ))
    ]
    region, cell, below, above = place()
    barrier = greet()
    for move in moves:
        move.start()
    inbox[cell] = jnp.zeros((4, 512), F32)
    pl.semaphore_wait(barrier, PEERS + 1)

    for peer in peers_of(cell):
        remote(back, inbox, send_sem, recv_sem, peer, cell, (region, peer)).start()
    remote(back, inbox, send_sem, recv_sem, LOWER, UPPER, (below, cell)).start()
    remote(back, inbox, send_sem, recv_sem, UPPER, LOWER, (above, cell)).start()

    for move in moves:
        move.wait()
    local_mirror(pair_ref, own, gst, q_rows, q_wide, self_t, pair_t)

    def arrived(k, _):
        peer = lax.rem(cell + k, PEERS)
        remote(back, inbox, send_sem, recv_sem, peer, peer, (region, peer)).wait_recv()
        return 0
    lax.fori_loop(1, PEERS, arrived, 0)
    edges = [
        remote(back, inbox, send_sem, recv_sem, slot, slot, device)
        for slot, device in ((LOWER, (below, cell)), (UPPER, (above, cell)))
    ]
    for copy in edges:
        copy.wait_recv()
    total = []
    for a in range(4):
        t = self_t[a]
        for k in range(4):
            t = t + jnp.where(pair_ref[0, k] == a, pair_t[k], 0.0)
            t = t + jnp.where(pair_ref[1, k] == a, pair_t[4 + k], 0.0)
        total.append(t[0:4])
    for slot in range(34):
        target = send_ref[slot] if slot < PEERS else edge_ref[slot - PEERS]
        rows = inbox[slot]
        for a in range(4):
            total[a] = total[a] + jnp.where(target == a, rows, 0.0)
    lane_id = lax.broadcasted_iota(I32, (1, 512), 1)
    for a in range(4):
        live = lane_id < counts[a]
        for k in range(3):
            accel[k, a:a + 1] = jnp.where(live, total[a][1 + k:2 + k], 0.0)

    def left(k, _):
        peer = lax.rem(cell + k, PEERS)
        remote(back, inbox, send_sem, recv_sem, peer, peer, (region, peer)).wait_send()
        return 0
    lax.fori_loop(1, PEERS, left, 0)
    for copy in edges:
        copy.wait_send()


def give_back(counts, send, edge, pairs, back, table, g, q_rows, q_wide):
    hbm = pl.BlockSpec(memory_space=pl.ANY)
    return pl.pallas_call(
        return_kernel,
        out_shape=jax.ShapeDtypeStruct((3, 4, 512), F32),
        in_specs=[hbm] * 9,
        out_specs=pl.BlockSpec(memory_space=pltpu.VMEM),
        scratch_shapes=[
            pltpu.VMEM((34, 4, 512), F32),
            pltpu.VMEM((4, 8, 512), F32),
            pltpu.VMEM((LOCAL, 128, 256), BF16),
            pltpu.VMEM((4, 8, 512), F32),
            pltpu.VMEM((8, 8, 512), F32),
            pltpu.SMEM((4,), I32),
            pltpu.SMEM((32,), I32),
            pltpu.SMEM((2,), I32),
            pltpu.SMEM((2, 4), I32),
            pltpu.VMEM((4, 16, 512), BF16),
            pltpu.VMEM((16, 16, 256), BF16),
            pltpu.SemaphoreType.DMA((34,)),
            pltpu.SemaphoreType.DMA((34,)),
            pltpu.SemaphoreType.DMA((8,)),
        ],
        compiler_params=pltpu.CompilerParams(
            collective_id=1, has_side_effects=True, vmem_limit_bytes=60 * MIB
        ),
        name="give_back",
    )(counts, send, edge, pairs, back, table, g, q_rows, q_wide)


def on_device(
    positions, velocities, mass, smoothing, energy, counts, send_cells, local_pairs, edge_cells
):
    send = send_cells.reshape(32)
    edge = edge_cells.reshape(2)
    pairs = local_pairs[0, 0].T
    table, g, *local = exchange(counts, send, edge, pairs, positions, velocities, mass, smoothing)
    density, part, heat, back, q_rows, q_wide = compute(send, pairs, edge, table, energy, local)
    extra = give_back(counts, send, edge, pairs, back, table, g, q_rows, q_wide)
    return density, part + extra, heat


def solution(mesh):
    placed = (
        P(None, ("region", "cell"), None),
        P(None, ("region", "cell"), None),
        P(("region", "cell"), None),
        P(("region", "cell"), None),
        P(("region", "cell"), None),
        P(("region", "cell")),
        P("region", "cell", None, None),
        P("region", "cell", None, None),
        P("region", "cell", None),
    )
    return jax.shard_map(
        on_device,
        mesh=mesh,
        in_specs=placed,
        out_specs=(
            P(("region", "cell"), None),
            P(None, ("region", "cell"), None),
            P(("region", "cell"), None),
        ),
        check_vma=False,
    )
```
